512 devices in a mesh: genome: 512 (over z, x, y, core).
Axes of the slice: x: 4, y: 4, z: 16, core: 2. Of those that a mesh axis runs over, the one named last changes fastest.
Arguments:
- contacts: int32 [131072, 1024], P('genome'), may hold values from 0 to 1040, as said below
- mappable: int32 [131072], P('genome'), may hold values 0 or 1
Outputs:
- pvalue_donut: float32 [131072, 1024], P('genome')
- pvalue_lower: float32 [131072, 1024], P('genome')
- bin_bias: float32 [131072], P('genome')
The draws below stay inside these ranges and needn't reach their ends.
Inputs may be any that keep to these rules, and one draw needn't show every extreme that they name: contacts[i, d] counts the contacts of bin i with bin i + d; it is zero where i + d >= 131072 and 1 or more where d = 0 and i < 131072.
All inputs are finite; a program needn't handle non-finite values. No bound on the sum of `mappable` on one device may be relied on, other than what follows from the above.
Results may differ from the reference program's by a relative error of at most 0.0003.
Values sent between devices are 32-bit elements; how exact they have to be, the bound alone decides.
No kernel may reach another device: no remote copies, remote signals or barrier semaphores. Data moves between devices by JAX's collectives and lax.ppermute only.
A program may use at most 64 MiB of HBM per device.

```python
import jax
import jax.numpy as jnp
from jax import lax

BAND = 1024
ROWS_DEV = 256
ITERS = 2
OUTER = 5
INNER = 2
NBINS = 131072


def draw_contacts(key, part):
    key = jax.random.fold_in(key, 11)
    key_factor, key_counts = jax.random.split(key)
    factor = jax.random.randint(key_factor, (NBINS + BAND,), 1, 3)
    factor = factor.at[NBINS - 1].set(2)
    bin_index = lax.broadcasted_iota(jnp.int32, (NBINS, BAND), 0)
    distance = lax.broadcasted_iota(jnp.int32, (NBINS, BAND), 1)
    upper_level = factor[bin_index] * factor[bin_index + distance] * (2 + 256 // (distance + 2))
    upper_level = upper_level * ((NBINS + 2 * bin_index) // NBINS)
    lowest = jnp.where(distance == 0, 1, 0)
    drawn_counts = jax.random.randint(key_counts, (NBINS, BAND), lowest, upper_level + 1)
    corner = (bin_index == NBINS - 1) & (distance == 0)
    drawn_counts = jnp.where(corner, upper_level, drawn_counts)
    inside = bin_index + distance < NBINS
    return jnp.where(inside, drawn_counts, 0).astype(jnp.int32)


def plant(drawn, key, least, high):
    index_at = [jax.random.randint(jax.random.fold_in(key, axis), (), 0, length) for axis, length in enumerate(drawn.shape)]
    widest = drawn.shape.index(max(drawn.shape))
    next_to = index_at[:widest] + [(index_at[widest] + 1) % drawn.shape[widest]] + index_at[widest + 1:]
    return drawn.at[tuple(index_at)].set(least).at[tuple(next_to)].set(high)


def setup_inputs(seed: int = 0) -> dict:
    key_list = jax.random.split(jax.random.key(seed), 3)
    return {
        "contacts": draw_contacts(jax.random.fold_in(key_list[2], 71), 0),
        "mappable": plant((jax.random.randint(key_list[1], (NBINS,), 0, 8) < 7).astype(jnp.int32), jax.random.fold_in(key_list[1], 1), 0, 1),
    }


def hankel(ahead_vec, row_count, band_width):
    line_len = row_count + band_width + 1
    tiled_row = jnp.tile(ahead_vec, row_count + 1)[:row_count * line_len]
    return tiled_row.reshape(row_count, line_len)[:, :band_width]

def column_sums(balanced):
    row_count, band_width = balanced.shape
    line_len = row_count + band_width
    padded = jnp.pad(balanced, ((0, 0), (0, row_count + 1)))
    return lax.optimization_barrier(jnp.sum(padded.reshape(-1)[:row_count * line_len].reshape(row_count, line_len), axis=0))

def shear_sums(rows_in):
    height = rows_in.shape[0] - 2 * OUTER
    band_width = rows_in.shape[1]
    padded = jnp.pad(rows_in, ((0, 0), (2 * OUTER, 2 * OUTER)))
    span_len = band_width + 2 * OUTER

    def across(offset_low, offset_high):
        running = padded[:, OUTER + offset_low:OUTER + offset_low + span_len]
        for offset in range(offset_low + 1, offset_high + 1):
            running = running + padded[:, OUTER + offset:OUTER + offset + span_len]
        return running

    def tilted(sum_table, row_shift):
        return sum_table[OUTER + row_shift:OUTER + row_shift + height, OUTER - row_shift:OUTER - row_shift + band_width]
    outer_rows = across(-OUTER, OUTER)
    inner_rows = across(-INNER, INNER)
    left_outer = across(-OUTER, -1)
    left_inner = across(-INNER, -1)
    donut_sum = tilted(inner_rows, 0) - tilted(outer_rows, 0)
    for row_shift in range(-OUTER, OUTER + 1):
        donut_sum = donut_sum + tilted(outer_rows, row_shift)
        if abs(row_shift) <= INNER:
            donut_sum = donut_sum - tilted(inner_rows, row_shift)
        else:
            donut_sum = donut_sum - padded[OUTER + row_shift:OUTER + row_shift + height, 2 * OUTER - row_shift:2 * OUTER - row_shift + band_width]
    lower_sum = tilted(left_outer, 1) - tilted(left_inner, 1)
    for row_shift in range(2, OUTER + 1):
        lower_sum = lower_sum + tilted(left_outer, row_shift)
        if row_shift <= INNER:
            lower_sum = lower_sum - tilted(left_inner, row_shift)
    return (donut_sum, lower_sum)

def poisson_tail(counts, local_mean):
    shape_k = jnp.maximum(counts.astype(jnp.float32), 1.0)
    ninth = 1.0 / (9.0 * shape_k)
    z_score = (jnp.cbrt(local_mean / shape_k) - (1.0 - ninth)) / jnp.sqrt(ninth)
    return 0.5 * lax.erfc(-z_score / jnp.sqrt(jnp.float32(2.0)))

def tail_values(observed, regional, expected, contacts, weight, pair_mask, distance):
    valid_cols = distance >= 2 * OUTER
    local_ratio = observed / jnp.where(valid_cols, regional, 1.0)
    local_mean = expected[None, :] * local_ratio / jnp.where(pair_mask > 0, weight, 1.0)
    tail_prob = poisson_tail(contacts, jnp.maximum(local_mean, 0.0))
    keep_mask = valid_cols & (pair_mask > 0) & (contacts > 0)
    return jnp.where(keep_mask, tail_prob, 1.0)

def reference(contacts, mappable):
    blocks = NBINS // ROWS_DEV
    mapped = mappable.astype(jnp.float32)
    shaped = contacts.reshape(blocks, ROWS_DEV, BAND)
    numbers = jnp.arange(blocks, dtype=jnp.int32)
    distance = lax.broadcasted_iota(jnp.int32, (1, BAND), 1)

    def near_band(extended, inverse, number, row_block):
        begin = number * ROWS_DEV
        near_ahead = lax.dynamic_slice_in_dim(extended, begin, ROWS_DEV + BAND)
        own_part = lax.dynamic_slice_in_dim(inverse, begin, ROWS_DEV)
        ahead_band = hankel(near_ahead, ROWS_DEV, BAND)
        return (row_block.astype(jnp.float32) * own_part[:, None] * ahead_band, ahead_band, own_part)

    def bin_sums(inverse):
        extended = jnp.concatenate([inverse, jnp.zeros((BAND,), jnp.float32)])

        def scan_step(spread_total, block_item):
            number, row_block = block_item
            balanced, ahead_band, own_part = near_band(extended, inverse, number, row_block)
            spread = column_sums(jnp.where(distance > 0, balanced, 0.0))
            begin = number * ROWS_DEV
            current = lax.dynamic_slice_in_dim(spread_total, begin, ROWS_DEV + BAND)
            spread_total = lax.dynamic_update_slice_in_dim(spread_total, current + spread, begin, 0)
            return (spread_total, lax.optimization_barrier(jnp.sum(balanced, axis=1)))
        spread_total, own_sums = lax.scan(scan_step, jnp.zeros((NBINS + BAND,), jnp.float32), (numbers, shaped))
        return own_sums.reshape(-1) + spread_total[:NBINS]
    bias_vec = jnp.ones((NBINS,), jnp.float32)
    inverse = mapped
    mapped_count = jnp.sum(mapped)
    for iteration in range(ITERS):
        row_sums = bin_sums(inverse)
        average = jnp.sum(mapped * row_sums) / mapped_count
        bias_vec = jnp.where(mappable > 0, bias_vec * row_sums / average, 1.0)
        inverse = jnp.where(mappable > 0, 1.0 / bias_vec, 0.0)
    extended = jnp.concatenate([inverse, jnp.zeros((BAND,), jnp.float32)])

    def finish(block_item):
        number, row_block = block_item
        balanced, ahead_band, own_part = near_band(extended, inverse, number, row_block)
        own_mapped = lax.dynamic_slice_in_dim(mapped, number * ROWS_DEV, ROWS_DEV)
        pair_mask = own_mapped[:, None] * (ahead_band > 0).astype(jnp.float32)
        return (balanced, lax.optimization_barrier(jnp.sum(balanced, axis=0)), lax.optimization_barrier(jnp.sum(pair_mask, axis=0)))
    bands, diag_parts, pair_parts = lax.map(finish, (numbers, shaped))
    expected = lax.optimization_barrier(jnp.sum(diag_parts, axis=0)) / lax.optimization_barrier(jnp.sum(pair_parts, axis=0))
    padded = jnp.pad(bands.reshape(NBINS, BAND), ((OUTER, OUTER), (0, 0)))
    donut_exp, lower_exp = shear_sums(jnp.broadcast_to(expected[None, :], (2 * OUTER + 1, BAND)))

    def judge_block(block_item):
        number, row_block = block_item
        balanced, ahead_band, own_part = near_band(extended, inverse, number, row_block)
        own_mapped = lax.dynamic_slice_in_dim(mapped, number * ROWS_DEV, ROWS_DEV)
        pair_mask = own_mapped[:, None] * (ahead_band > 0).astype(jnp.float32)
        rows_in = lax.dynamic_slice_in_dim(padded, number * ROWS_DEV, ROWS_DEV + 2 * OUTER)
        donut_obs, lower_obs = shear_sums(rows_in)
        weight = own_part[:, None] * ahead_band
        return (tail_values(donut_obs, donut_exp, expected, row_block, weight, pair_mask, distance), tail_values(lower_obs, lower_exp, expected, row_block, weight, pair_mask, distance))
    donut_p, lower_p = lax.map(judge_block, (numbers, shaped))
    return (donut_p.reshape(NBINS, BAND), lower_p.reshape(NBINS, BAND), bias_vec)
```

```python
import jax
import jax.numpy as jnp
from jax import lax
from jax.sharding import PartitionSpec as P

ITERS = 2
OUTER = 5
INNER = 2


def shifted(value, axis, steps):
    count = lax.axis_size(axis)
    leading, last = (max(0, -steps), min(count, count - steps))
    return lax.ppermute(value, axis, [(source, source + steps) for source in range(leading, last)])


def with_halo(cells, sides, width):
    for axis, dim in sides:
        count = lax.axis_size(axis)
        ends = count - 1
        head = lax.slice_in_dim(cells, 0, width, axis=dim)
        tail = lax.slice_in_dim(cells, cells.shape[dim] - width, cells.shape[dim], axis=dim)
        cells = jnp.concatenate(
            [
                lax.ppermute(tail, axis, [(i, (i + 1) % count) for i in range(ends)]),
                cells,
                lax.ppermute(head, axis, [((i + 1) % count, i) for i in range(ends)]),
            ],
            axis=dim,
        )
    return cells


def hankel(ahead_vec, row_count, band_width):
    line_len = row_count + band_width + 1
    tiled_row = jnp.tile(ahead_vec, row_count + 1)[: row_count * line_len]
    return tiled_row.reshape(row_count, line_len)[:, :band_width]


def column_sums(balanced):
    row_count, band_width = balanced.shape
    line_len = row_count + band_width
    padded = jnp.pad(balanced, ((0, 0), (0, row_count + 1)))
    return jnp.sum(padded.reshape(-1)[: row_count * line_len].reshape(row_count, line_len), axis=0)


def shear_sums(rows_in):
    height = rows_in.shape[0] - 2 * OUTER
    band_width = rows_in.shape[1]
    padded = jnp.pad(rows_in, ((0, 0), (2 * OUTER, 2 * OUTER)))
    span_len = band_width + 2 * OUTER

    def across(offset_low, offset_high):
        running = padded[:, OUTER + offset_low : OUTER + offset_low + span_len]
        for offset in range(offset_low + 1, offset_high + 1):
            running = running + padded[:, OUTER + offset : OUTER + offset + span_len]
        return running

    def tilted(sum_table, row_shift):
        return sum_table[
            OUTER + row_shift : OUTER + row_shift + height,
            OUTER - row_shift : OUTER - row_shift + band_width,
        ]

    outer_rows = across(-OUTER, OUTER)
    inner_rows = across(-INNER, INNER)
    left_outer = across(-OUTER, -1)
    left_inner = across(-INNER, -1)
    donut_sum = tilted(inner_rows, 0) - tilted(outer_rows, 0)
    for row_shift in range(-OUTER, OUTER + 1):
        donut_sum = donut_sum + tilted(outer_rows, row_shift)
        if abs(row_shift) <= INNER:
            donut_sum = donut_sum - tilted(inner_rows, row_shift)
        else:
            donut_sum = (
                donut_sum
                - padded[
                    OUTER + row_shift : OUTER + row_shift + height,
                    2 * OUTER - row_shift : 2 * OUTER - row_shift + band_width,
                ]
            )
    lower_sum = tilted(left_outer, 1) - tilted(left_inner, 1)
    for row_shift in range(2, OUTER + 1):
        lower_sum = lower_sum + tilted(left_outer, row_shift)
        if row_shift <= INNER:
            lower_sum = lower_sum - tilted(left_inner, row_shift)
    return (donut_sum, lower_sum)


def gathered(value, groups):
    count = len(groups[0])
    copies = jnp.broadcast_to(value[None], (count,) + value.shape)
    return lax.all_to_all(copies, "genome", 0, 0, axis_index_groups=groups)


def total_over_genome(value):
    count = lax.axis_size("genome")
    near = min(count, 32)
    planes = [[start + i for i in range(near)] for start in range(0, count, near)]
    lines = [[i + start for start in range(0, count, near)] for i in range(near)]
    value = jnp.sum(gathered(value, planes), axis=0)
    return jnp.sum(gathered(value, lines), axis=0)


def poisson_tail(counts, local_mean):
    shape_k = jnp.maximum(counts.astype(jnp.float32), 1.0)
    ninth = 1.0 / (9.0 * shape_k)
    z_score = (jnp.cbrt(local_mean / shape_k) - (1.0 - ninth)) / jnp.sqrt(ninth)
    return 0.5 * lax.erfc(-z_score / jnp.sqrt(jnp.float32(2.0)))


def tail_values(observed, regional, expected, contacts, weight, pair_mask, distance):
    valid_cols = distance >= 2 * OUTER
    local_ratio = observed / jnp.where(valid_cols, regional, 1.0)
    local_mean = expected[None, :] * local_ratio / jnp.where(pair_mask > 0, weight, 1.0)
    tail_prob = poisson_tail(contacts, jnp.maximum(local_mean, 0.0))
    keep_mask = valid_cols & (pair_mask > 0) & (contacts > 0)
    return jnp.where(keep_mask, tail_prob, 1.0)


def shards(contacts, mappable):
    row_count, band_width = contacts.shape
    hop_total = band_width // row_count
    mapped = mappable.astype(jnp.float32)
    counts_float = contacts.astype(jnp.float32)
    distance = lax.broadcasted_iota(jnp.int32, (1, band_width), 1)

    def inverse_ahead(inverse):
        pieces = [inverse]
        for hop_count in range(1, hop_total + 1):
            pieces.append(shifted(inverse, "genome", -hop_count))
        return jnp.concatenate(pieces)

    bias_vec = jnp.ones((row_count,), jnp.float32)
    inverse = mapped
    covered = []
    for iteration in range(ITERS):
        ahead_band = hankel(inverse_ahead(inverse), row_count, band_width)
        balanced = counts_float * inverse[:, None] * ahead_band
        spread = column_sums(jnp.where(distance > 0, balanced, 0.0))
        row_sums = jnp.sum(balanced, axis=1) + spread[:row_count]
        for hop_count in range(1, hop_total + 1):
            row_sums = row_sums + shifted(
                spread[hop_count * row_count : (hop_count + 1) * row_count], "genome", hop_count
            )
        covered.append(jnp.sum(mapped * row_sums))
        bias_vec = jnp.where(mappable > 0, bias_vec * row_sums, 1.0)
        inverse = jnp.where(mappable > 0, 1.0 / bias_vec, 0.0)
    ahead_band = hankel(inverse_ahead(inverse), row_count, band_width)
    balanced = counts_float * inverse[:, None] * ahead_band
    pair_mask = mapped[:, None] * (ahead_band > 0).astype(jnp.float32)
    totals = total_over_genome(
        jnp.concatenate(
            [jnp.sum(balanced, axis=0), jnp.sum(pair_mask, axis=0), jnp.stack(covered)]
        )
    )
    diag_total, pair_total = totals[:band_width], totals[band_width : 2 * band_width]
    mapped_count = pair_total[0]
    for iteration in range(ITERS):
        average = totals[2 * band_width + iteration] / mapped_count
        bias_vec = jnp.where(mappable > 0, bias_vec / average, 1.0)
    expected = diag_total / pair_total
    rows_in = with_halo(balanced, (("genome", 0),), OUTER)
    donut_obs, lower_obs = shear_sums(rows_in)
    donut_exp, lower_exp = shear_sums(
        jnp.broadcast_to(expected[None, :], (2 * OUTER + 1, band_width))
    )
    weight = inverse[:, None] * ahead_band
    pvalue_donut = tail_values(
        donut_obs, donut_exp, expected, contacts, weight, pair_mask, distance
    )
    pvalue_lower = tail_values(
        lower_obs, lower_exp, expected, contacts, weight, pair_mask, distance
    )
    return (pvalue_donut, pvalue_lower, bias_vec)


def solution(mesh):
    placed = (P("genome", None), P("genome"))
    return jax.shard_map(
        shards,
        mesh=mesh,
        in_specs=placed,
        out_specs=(P("genome", None), P("genome", None), P("genome")),
        check_vma=False,
    )
```

```python
import jax
import jax.numpy as jnp
from jax import lax
from jax.experimental import pallas as pl
from jax.experimental.pallas import tpu as pltpu
from jax.sharding import PartitionSpec as P

OUTER = 5
INNER = 2
ROWS = 256
BAND = 1024
LANE = 128
SLAB = ROWS // LANE
HOPS = BAND // ROWS
SPAN = ROWS + BAND
WIDE = SPAN + LANE
STEP = 32
EDGE = 8
MASKED = -1.0
VMEM = pl.BlockSpec(memory_space=pltpu.VMEM)
SMEM = pl.BlockSpec(memory_space=pltpu.SMEM)
F32 = jnp.float32
X_AT, SPREAD_AT, SUMS_AT, MESSAGE = 0, SLAB, SLAB * (HOPS + 2), 16


def lanes(tiles):
    return jnp.concatenate([tiles[r : r + 1] for r in range(tiles.shape[0])], axis=1)


def put_lanes(ref, first, row):
    for t in range(row.shape[1] // LANE):
        ref[first + t : first + t + 1, :] = row[:, t * LANE : (t + 1) * LANE]


def on_diagonal(start, count, width):
    rows = lax.broadcasted_iota(jnp.int32, (count, width), 0) + start
    return rows == lax.broadcasted_iota(jnp.int32, (count, width), 1)


def column_of(row, start, count):
    part = jnp.where(on_diagonal(start, count, ROWS), row, 0.0)
    return jnp.sum(part, axis=1, keepdims=True)


def fold(value):
    total = value[0:8]
    for r in range(8, value.shape[0], 8):
        total = total + value[r : r + 8]
    return total


def spread_of(skewed_ref, weight_row):
    total = jnp.zeros((8, SPAN), F32)
    for start in range(0, ROWS, STEP):
        weight = column_of(weight_row, start, STEP)
        part = skewed_ref[start : start + STEP, :] * weight
        part = jnp.where(on_diagonal(start, STEP, SPAN), 0.0, part)
        total = total + fold(part)
    return jnp.sum(total, axis=0, keepdims=True)


def own_sums(skewed_ref, ahead_row):
    total = jnp.zeros((8, ROWS), F32)
    for start in range(0, ROWS, STEP):
        part = skewed_ref[start : start + STEP, :] * ahead_row
        sums = jnp.sum(part, axis=1, keepdims=True)
        total = total + fold(jnp.where(on_diagonal(start, STEP, ROWS), sums, 0.0))
    return jnp.sum(total, axis=0, keepdims=True)


def put_message(out_ref, x_row, spread_row, sums_row):
    out_ref[...] = jnp.zeros((MESSAGE, LANE), F32)
    put_lanes(out_ref, X_AT, x_row)
    put_lanes(out_ref, SPREAD_AT, spread_row)
    put_lanes(out_ref, SUMS_AT, sums_row)


def begin_kernel(contacts_ref, mapped_ref, skewed_ref, out_ref):
    mapped = lanes(mapped_ref[...]).astype(F32)
    for start in range(0, ROWS, STEP):
        counts = contacts_ref[start : start + STEP, :].astype(F32)
        padded = jnp.concatenate([counts, jnp.zeros((STEP, SPAN - BAND), F32)], axis=1)
        skewed_ref[start : start + STEP, :] = pltpu.roll(padded, start, 1, stride=1, stride_axis=0)
    put_message(out_ref, mapped, spread_of(skewed_ref, mapped), jnp.zeros((1, ROWS), F32))


def ahead_of(core, slabs):
    tiles = [jnp.where(core == 0, slabs[k], slabs[k + 1]) for k in range(HOPS + 1)]
    return jnp.concatenate([lanes(t) for t in tiles], axis=1)


def sum_rows(core_ref, skewed_ref, pair_ref, near_ref, far_ref, mapped_ref):
    core = core_ref[0]

    def message(k):
        at = k % 2
        chip = k // 2
        if chip == 0:
            return pair_ref.at[at]
        ref = near_ref if abs(chip) == 1 else far_ref
        return ref.at[1 if chip > 0 else 0, at]

    x_tiles = [message(k)[X_AT : X_AT + SLAB, :] for k in range(HOPS + 2)]
    arrived = jnp.zeros((SLAB, LANE), F32)
    for k in range(HOPS + 1):
        at = SPREAD_AT + SLAB * k
        arrived = arrived + jnp.where(
            core == 0, message(-k)[at : at + SLAB, :], message(1 - k)[at : at + SLAB, :]
        )
    sums = own_sums(skewed_ref, ahead_of(core, x_tiles)) + lanes(arrived)
    x_row = lanes(jnp.where(core == 0, x_tiles[0], x_tiles[1]))
    mapped = lanes(mapped_ref[...]) > 0
    return mapped, x_row * sums


def middle_kernel(core_ref, skewed_ref, pair_ref, near_ref, far_ref, mapped_ref, out_ref):
    mapped, sums = sum_rows(core_ref, skewed_ref, pair_ref, near_ref, far_ref, mapped_ref)
    x_row = jnp.where(mapped, 1.0 / jnp.where(mapped, sums, 1.0), 0.0)
    put_message(out_ref, x_row, spread_of(skewed_ref, x_row), sums)


def last_kernel(core_ref, skewed_ref, pair_ref, near_ref, far_ref, mapped_ref, out_ref):
    mapped, sums = sum_rows(core_ref, skewed_ref, pair_ref, near_ref, far_ref, mapped_ref)
    before = jnp.where(core_ref[0] == 0, pair_ref[0], pair_ref[1])
    before = lanes(before[SUMS_AT : SUMS_AT + SLAB])
    bias = jnp.where(mapped, before * sums, 1.0)
    out_ref[...] = jnp.zeros((8, LANE), F32)
    put_lanes(out_ref, 0, jnp.where(mapped, 1.0 / bias, 0.0))
    put_lanes(out_ref, SLAB, bias)
    for at, value in ((4, before), (5, sums)):
        total = jnp.sum(jnp.where(mapped, value, 0.0), axis=1, keepdims=True)
        out_ref[at : at + 1, :] = jnp.broadcast_to(total, (1, LANE))


def along_diagonals(rows_of, width):
    total = None
    for g in range(LANE // 8):
        part = None
        for h in range(SLAB):
            rows = rows_of(h * LANE + 8 * g)
            rows = rows[:, h * LANE : h * LANE + SPAN - LANE]
            part = rows if part is None else part + rows
        if g:
            part = pltpu.roll(part, SPAN - LANE - 8 * g, 1)
        total = part if total is None else total + part
    out = total[0:1, :width]
    for s in range(1, 8):
        out = out + pltpu.roll(total, SPAN - LANE - s, 1)[s : s + 1, :width]
    return out


def band_kernel(core_ref, skewed_ref, pair_ref, ahead_ref, own_ref, final_ref, swap_ref, cross_ref, sums_ref):
    core = core_ref[0]
    slabs = [pair_ref[0], pair_ref[1], ahead_ref[0, 0], ahead_ref[0, 1], ahead_ref[1, 0], ahead_ref[1, 1]]
    ahead = ahead_of(core, [s[X_AT : X_AT + SLAB] for s in slabs])
    x_row = ahead[:, :ROWS]
    for start in range(0, ROWS, STEP):
        final_ref[start : start + STEP, :] = (
            skewed_ref[start : start + STEP, :] * column_of(x_row, start, STEP) * ahead
        )
    first, last = final_ref[0:EDGE, :], final_ref[ROWS - EDGE : ROWS, :]
    swap_ref[...] = jnp.where(core == 0, last, first)
    cross_ref[...] = jnp.where(core == 0, first, last)
    mapped_ahead = (ahead > 0).astype(F32)
    mapped_row = mapped_ahead[:, :ROWS]
    diagonals = along_diagonals(lambda r: final_ref[r : r + 8, :], BAND)
    pairs = along_diagonals(lambda r: column_of(mapped_row, r, 8) * mapped_ahead, BAND)
    own = own_ref[...]
    row = jnp.concatenate([diagonals, pairs, own[4:5, : LANE // 2], own[5:6, : LANE // 2]], axis=1)
    for n in range(sums_ref.shape[0]):
        sums_ref[n] = row


def straight(rows, start):
    if start:
        rows = pltpu.roll(rows, SPAN - start, 1)
    rows = rows[:, : BAND + LANE]
    row = lax.broadcasted_iota(jnp.int32, rows.shape, 0)
    for step in (1, 2, 4):
        rows = jnp.where((row & step) > 0, pltpu.roll(rows, BAND + LANE - step, 1), rows)
    return rows[:, :BAND]


def window_kernel(core_ref, final_ref, swap_ref, cross_ref, pair_ref, ahead_ref, contacts_ref,
                  donut_ref, lower_ref, base_ref, edged_ref, lefts_ref, sides_ref, left_in_ref, sides_in_ref):
    core = core_ref[0]
    slabs = [pair_ref[0], pair_ref[1], ahead_ref[0, 0], ahead_ref[0, 1], ahead_ref[1, 0], ahead_ref[1, 1]]

    swap, cross = swap_ref[...], cross_ref[...]
    before = jnp.where(core == 0, cross, swap)
    after = jnp.where(core == 0, swap, cross)
    gap = jnp.zeros((EDGE, LANE), F32)
    edged_ref[0:EDGE, :] = jnp.concatenate(
        [before[:, ROWS:], gap, before[:, :ROWS]], axis=1
    )
    edged_ref[ROWS + EDGE :, :] = jnp.concatenate(
        [gap] * SLAB + [after[:, : WIDE - ROWS]], axis=1
    )
    edged_ref[EDGE : ROWS + EDGE, :SPAN] = final_ref[...]
    edged_ref[EDGE : ROWS + EDGE, SPAN:] = jnp.zeros((ROWS, WIDE - SPAN), F32)
    for start in range(0, ROWS + 2 * EDGE, 16):
        cells = edged_ref[start : start + 16, :]
        two = cells + pltpu.roll(cells, WIDE - 1, 1)
        three = two + pltpu.roll(cells, WIDE - 2, 1)
        left_out = pltpu.roll(three, 5, 1)
        left_in = pltpu.roll(two, 2, 1)
        lefts_ref[start : start + 16, :] = left_out
        left_in_ref[start : start + 16, :] = left_in
        sides_ref[start : start + 16, :] = left_out + pltpu.roll(three, WIDE - 3, 1)
        sides_in_ref[start : start + 16, :] = left_in + pltpu.roll(two, WIDE - 1, 1)

    ahead = ahead_of(core, [s[X_AT : X_AT + SLAB] for s in slabs])
    mapped = ahead > 0
    bias_ahead = jnp.where(mapped, 1.0 / jnp.where(mapped, ahead, 1.0), 0.0)
    bias_row = bias_ahead[:, :ROWS]
    def band_rows(sums, start):
        weight = column_of(bias_row, start, STEP) * bias_ahead
        value = jnp.where(weight > 0, jnp.maximum(sums, 0.0) * weight, MASKED)
        return jnp.concatenate([straight(value[r : r + 8], start + r) for r in range(0, STEP, 8)], axis=0)

    for start in range(0, ROWS, STEP):

        def rows(ref, shift):
            at = start + EDGE + shift
            return ref[at : at + STEP, :SPAN]

        shifts = range(1, OUTER + 1)
        lower = sum(rows(lefts_ref, a) for a in shifts)
        lower = lower + sum(rows(left_in_ref, a) for a in shifts if a > INNER)
        donut = sum(rows(sides_ref, a) + rows(sides_ref, -a) for a in shifts)
        donut = donut + sum(rows(sides_in_ref, a) + rows(sides_in_ref, -a) for a in shifts if a > INNER)
        counts = contacts_ref[start : start + STEP, :]
        k = jnp.maximum(counts, 1).astype(F32)
        inverse_k = 1.0 / k
        scale = jnp.sqrt(k) * (3.0 / 2.0**0.5)
        distance = lax.broadcasted_iota(jnp.int32, (STEP, BAND), 1)
        keep = (counts > 0) & (distance >= 2 * OUTER)
        base = (1.0 - inverse_k * (1.0 / 9.0)) * scale
        for sums, out_ref in ((donut, donut_ref), (lower, lower_ref)):
            value = band_rows(sums, start)
            ok = keep & (value >= 0.0)
            root = jnp.where(value > 0.0, jnp.exp(jnp.log(jnp.where(value > 0.0, value, 1.0) * inverse_k) * (1.0 / 3.0)), 0.0)
            out_ref[start : start + STEP, :] = jnp.where(ok, root * scale, MASKED)
        base_ref[start : start + STEP, :] = base


def half_erfc(x):
    size = jnp.abs(x)
    t = 1.0 / (1.0 + 0.5 * size)
    poly = 0.17087277
    for c in (-0.82215223, 1.48851587, -1.13520398, 0.27886807, -0.18628806, 0.09678418, 0.37409196, 1.00002368, -1.26551223):
        poly = poly * t + c
    tail = 0.5 * t * jnp.exp(poly - size * size)
    return jnp.where(x >= 0.0, tail, 1.0 - tail)


def filter_sums(expected):
    margin = 2 * OUTER
    padded = jnp.concatenate([expected, jnp.zeros((1, LANE), F32)], axis=1)
    donut_weight, lower_weight = {}, {}
    for a in range(-OUTER, OUTER + 1):
        for c in range(-OUTER, OUTER + 1):
            if a and c and not (abs(a) <= INNER and abs(c) <= INNER):
                donut_weight[c - a] = donut_weight.get(c - a, 0) + 1
            if a >= 1 and c <= -1 and not (a <= INNER and c >= -INNER):
                lower_weight[c - a] = lower_weight.get(c - a, 0) + 1
    donut = lower = None
    for k in range(-margin, margin + 1):
        moved = pltpu.roll(padded, (-k) % (BAND + LANE), 1) if k else padded
        moved = moved[:, :BAND]
        if k in donut_weight:
            part = moved * float(donut_weight[k])
            donut = part if donut is None else donut + part
        if k in lower_weight:
            part = moved * float(lower_weight[k])
            lower = part if lower is None else lower + part
    return donut, lower


def cube_root(value):
    positive = value > 0.0
    root = jnp.exp(jnp.log(jnp.where(positive, value, 1.0)) * (1.0 / 3.0))
    return jnp.where(positive, root, value)


def tail_kernel(sums_ref, own_ref, donut_ref, lower_ref, base_ref, pvalue_donut_ref, pvalue_lower_ref, bias_ref, ratio_ref):
    @pl.when(pl.program_id(0) == 0)
    def _():
        total = sums_ref[0]
        for n in range(1, sums_ref.shape[0]):
            total = total + sums_ref[n]
        diagonals, pairs = total[:, :BAND], total[:, BAND : 2 * BAND]
        expected = diagonals / pairs
        donut_exp, lower_exp = filter_sums(expected)
        ratio_ref[0:1, :] = cube_root(expected / donut_exp)
        ratio_ref[1:2, :] = cube_root(expected / lower_exp)
        mapped_count = pairs[:, 0:1]
        half = LANE // 2
        first = total[:, 2 * BAND : 2 * BAND + 1] / mapped_count
        second = total[:, 2 * BAND + half : 2 * BAND + half + 1] / mapped_count
        own = own_ref[...]
        bias = own[SLAB : 2 * SLAB]
        mapped = own[0:SLAB] > 0
        bias_ref[...] = jnp.where(mapped, bias / first / second, 1.0)

    count = base_ref.shape[0]
    for start in range(0, count, STEP):
        base = base_ref[start : start + STEP, :]
        for at, root_ref, out_ref in ((0, donut_ref, pvalue_donut_ref), (1, lower_ref, pvalue_lower_ref)):
            root = root_ref[start : start + STEP, :]
            value = half_erfc(base - root * ratio_ref[at : at + 1, :])
            out_ref[start : start + STEP, :] = jnp.where(root < 0.0, 1.0, value)


def params(mib=48):
    return pltpu.CompilerParams(vmem_limit_bytes=mib * 2**20)


def cost(flops, moved):
    return pl.CostEstimate(flops=flops, bytes_accessed=moved, transcendentals=0)


def call(kernel, ins, outs, specs=None):
    return pl.pallas_call(
        kernel,
        out_shape=[jax.ShapeDtypeStruct(s, F32) for s in outs],
        in_specs=specs or [VMEM] * len(ins),
        out_specs=[VMEM] * len(outs),
        compiler_params=params(),
    )(*ins)


def begin(contacts, mapped):
    return call(begin_kernel, (contacts, mapped), [(ROWS, SPAN), (MESSAGE, LANE)])


def middle(core, skewed, pair, near, far, mapped):
    return call(middle_kernel, (core, skewed, pair, near, far, mapped), [(MESSAGE, LANE)], [SMEM] + [VMEM] * 5)[0]


def last(core, skewed, pair, near, far, mapped):
    return call(last_kernel, (core, skewed, pair, near, far, mapped), [(8, LANE)], [SMEM] + [VMEM] * 5)[0]


def final_band(core, skewed, pair, ahead, own, copies):
    return call(
        band_kernel,
        (core, skewed, pair, ahead, own),
        [(ROWS, SPAN), (EDGE, SPAN), (EDGE, SPAN), (copies, 1, 2 * BAND + LANE)],
        [SMEM] + [VMEM] * 4,
    )


def whole(shape):
    return pl.BlockSpec(shape, lambda i: (0,) * len(shape))


def windows(core, final, swap, cross, pair, ahead, contacts):
    return pl.pallas_call(
        window_kernel,
        out_shape=[jax.ShapeDtypeStruct((ROWS, BAND), F32)] * 3,
        in_specs=[SMEM] + [VMEM] * 6,
        out_specs=[VMEM] * 3,
        scratch_shapes=[pltpu.VMEM((ROWS + 2 * EDGE, WIDE), F32)] * 5,
        compiler_params=params(),
        cost_estimate=cost(2 * 10**7, 6 * 2**20),
    )(core, final, swap, cross, pair, ahead, contacts)


def tails(sums, own, donut, lower, base, count=64):
    block = pl.BlockSpec((count, BAND), lambda i: (i, 0))
    return pl.pallas_call(
        tail_kernel,
        grid=(ROWS // count,),
        out_shape=[jax.ShapeDtypeStruct((ROWS, BAND), F32)] * 2 + [jax.ShapeDtypeStruct((SLAB, LANE), F32)],
        in_specs=[whole(sums.shape), whole(own.shape)] + [block] * 3,
        out_specs=[block] * 2 + [whole((SLAB, LANE))],
        scratch_shapes=[pltpu.VMEM((8, BAND), F32)],
        compiler_params=params(),
    )(sums, own, donut, lower, base)


def solution(mesh):
    count = mesh.shape["genome"]
    plane = min(32, count)
    chips = [[i, i + 1] for i in range(0, count, 2)]
    planes = [[start + i for i in range(plane)] for start in range(0, count, plane)]
    lines = [[i + start for start in range(0, count, plane)] for i in range(plane)]

    def both_cores(value):
        return lax.all_gather(value, "genome", axis_index_groups=chips)

    def moved(value, target):
        pairs = [(i, target(i)) for i in range(count)]
        return lax.ppermute(value, "genome", [(i, t) for i, t in pairs if 0 <= t < count])

    def around(message):
        pair = both_cores(message)
        near = moved(pair, lambda i: i + 2 if i % 2 == 0 else i - 2)
        far = moved(pair, lambda i: i + 4 if i % 2 == 0 else i - 4)
        return pair, both_cores(near), both_cores(far)

    def shards(contacts, mappable):
        core = lax.rem(lax.axis_index("genome"), 2).astype(jnp.int32).reshape(1)
        mapped = mappable.reshape(SLAB, LANE)
        skewed, message = begin(contacts, mapped)
        message = middle(core, skewed, *around(message), mapped)
        own = last(core, skewed, *around(message), mapped)
        pair = both_cores(own)
        ahead = both_cores(moved(pair, lambda i: i - 2 if i % 2 == 0 else i - 4))
        final, swap, cross, sums = final_band(core, skewed, pair, ahead, own, plane)
        swap = moved(swap, lambda i: i ^ 1)
        cross = moved(cross, lambda i: i - 1 if i % 2 == 0 else i + 1)
        sums = lax.all_to_all(sums, "genome", 0, 0, axis_index_groups=planes)
        sums = jnp.broadcast_to(jnp.sum(sums, axis=0, keepdims=True), (count // plane,) + sums.shape[1:])
        sums = lax.all_to_all(sums, "genome", 0, 0, axis_index_groups=lines)
        donut, lower, base = windows(core, final, swap, cross, pair, ahead, contacts)
        pvalue_donut, pvalue_lower, bias = tails(sums, own, donut, lower, base)
        return pvalue_donut, pvalue_lower, bias.reshape(ROWS)

    placed = (P("genome", None), P("genome"))
    return jax.shard_map(
        shards,
        mesh=mesh,
        in_specs=placed,
        out_specs=(P("genome", None), P("genome", None), P("genome")),
        check_vma=False,
    )
```

```python
import jax
import jax.numpy as jnp
from jax import lax
from jax.experimental import pallas as pl
from jax.experimental.pallas import tpu as pltpu
from jax.sharding import PartitionSpec as P

OUTER = 5
INNER = 2
ROWS = 256
BAND = 1024
LANE = 128
SLAB = ROWS // LANE
HOPS = BAND // ROWS
SPAN = ROWS + BAND
WIDE = SPAN + LANE
STEP = 32
EDGE = 8
MASKED = -1.0
VMEM = pl.BlockSpec(memory_space=pltpu.VMEM)
SMEM = pl.BlockSpec(memory_space=pltpu.SMEM)
F32 = jnp.float32
X_AT, SPREAD_AT, SUMS_AT, MAPPED_AT, MESSAGE = 0, SLAB, SLAB * (HOPS + 2), SLAB * (HOPS + 3), 16


def lanes(tiles):
    return jnp.concatenate([tiles[r : r + 1] for r in range(tiles.shape[0])], axis=1)


def put_lanes(ref, first, row):
    for t in range(row.shape[1] // LANE):
        ref[first + t : first + t + 1, :] = row[:, t * LANE : (t + 1) * LANE]


def on_diagonal(start, count, width):
    rows = lax.broadcasted_iota(jnp.int32, (count, width), 0) + start
    return rows == lax.broadcasted_iota(jnp.int32, (count, width), 1)


def column_of(row, start, count):
    part = jnp.where(on_diagonal(start, count, ROWS), row, 0.0)
    return jnp.sum(part, axis=1, keepdims=True)


def fold(value):
    total = value[0:8]
    for r in range(8, value.shape[0], 8):
        total = total + value[r : r + 8]
    return total


def spread_part(rows, weight_row, start):
    part = rows * column_of(weight_row, start, STEP)
    return fold(jnp.where(on_diagonal(start, STEP, SPAN), 0.0, part))


def spread_of(skewed_ref, weight_row):
    total = jnp.zeros((8, SPAN), F32)
    for start in range(0, ROWS, STEP):
        total = total + spread_part(skewed_ref[start : start + STEP, :], weight_row, start)
    return jnp.sum(total, axis=0, keepdims=True)


def own_sums(skewed_ref, ahead_row):
    total = jnp.zeros((8, ROWS), F32)
    for start in range(0, ROWS, STEP):
        part = skewed_ref[start : start + STEP, :] * ahead_row
        sums = jnp.sum(part, axis=1, keepdims=True)
        total = total + fold(jnp.where(on_diagonal(start, STEP, ROWS), sums, 0.0))
    return jnp.sum(total, axis=0, keepdims=True)


def put_message(out_ref, x_row, spread_row, sums_row, mapped_row):
    put_lanes(out_ref, X_AT, x_row)
    put_lanes(out_ref, SPREAD_AT, spread_row)
    put_lanes(out_ref, SUMS_AT, sums_row)
    put_lanes(out_ref, MAPPED_AT, mapped_row)


def begin_kernel(contacts_ref, mapped_ref, skewed_ref, out_ref):
    for start in range(0, ROWS, STEP):
        counts = contacts_ref[start : start + STEP, :].astype(F32)
        padded = jnp.concatenate([counts, jnp.zeros((STEP, SPAN - BAND), F32)], axis=1)
        skewed_ref[start : start + STEP, :] = pltpu.roll(padded, start, 1, stride=1, stride_axis=0)
    mapped = lanes(mapped_ref[...]).astype(F32)
    put_message(out_ref, mapped, spread_of(skewed_ref, mapped), jnp.zeros((1, ROWS), F32), mapped)


def ahead_of(core, slabs):
    tiles = [jnp.where(core == 0, slabs[k], slabs[k + 1]) for k in range(HOPS + 1)]
    return jnp.concatenate([lanes(t) for t in tiles], axis=1)


def sum_rows(core_ref, skewed_ref, pair_ref, near_ref, far_ref):
    core = core_ref[0]

    def message(k):
        at = k % 2
        chip = k // 2
        if chip == 0:
            return pair_ref.at[at]
        ref = near_ref if abs(chip) == 1 else far_ref
        return ref.at[1 if chip > 0 else 0, at]

    x_tiles = [message(k)[X_AT : X_AT + SLAB, :] for k in range(HOPS + 2)]
    arrived = jnp.zeros((SLAB, LANE), F32)
    for k in range(HOPS + 1):
        at = SPREAD_AT + SLAB * k
        arrived = arrived + jnp.where(
            core == 0, message(-k)[at : at + SLAB, :], message(1 - k)[at : at + SLAB, :]
        )
    sums = own_sums(skewed_ref, ahead_of(core, x_tiles)) + lanes(arrived)
    x_row = lanes(jnp.where(core == 0, x_tiles[0], x_tiles[1]))
    mapped = jnp.where(core == 0, pair_ref[0, MAPPED_AT : MAPPED_AT + SLAB, :], pair_ref[1, MAPPED_AT : MAPPED_AT + SLAB, :])
    return lanes(mapped), x_row * sums


def middle_kernel(core_ref, skewed_ref, pair_ref, near_ref, far_ref, out_ref):
    mapped, sums = sum_rows(core_ref, skewed_ref, pair_ref, near_ref, far_ref)
    x_row = jnp.where(mapped > 0, 1.0 / jnp.where(mapped > 0, sums, 1.0), 0.0)
    put_message(out_ref, x_row, spread_of(skewed_ref, x_row), sums, mapped)


def last_kernel(core_ref, skewed_ref, pair_ref, near_ref, far_ref, out_ref):
    mapped, sums = sum_rows(core_ref, skewed_ref, pair_ref, near_ref, far_ref)
    before = jnp.where(core_ref[0] == 0, pair_ref[0], pair_ref[1])
    before = lanes(before[SUMS_AT : SUMS_AT + SLAB])
    bias = jnp.where(mapped > 0, before * sums, 1.0)
    out_ref[...] = jnp.zeros((8, LANE), F32)
    put_lanes(out_ref, 0, jnp.where(mapped > 0, 1.0 / bias, 0.0))
    put_lanes(out_ref, SLAB, bias)
    for at, value in ((4, before), (5, sums)):
        total = jnp.sum(jnp.where(mapped > 0, value, 0.0), axis=1, keepdims=True)
        out_ref[at : at + 1, :] = jnp.broadcast_to(total, (1, LANE))


def flipped(rows):
    order = 7 - lax.broadcasted_iota(jnp.int32, (8, LANE), 0)
    tiles = [jnp.take_along_axis(rows[:, t : t + LANE], order, axis=0, mode="promise_in_bounds") for t in range(0, rows.shape[1], LANE)]
    return jnp.concatenate(tiles, axis=1)


def along_diagonals(rows_of, width):
    total = None
    for g in range(LANE // 8):
        part = None
        for h in range(SLAB):
            rows = rows_of(h * LANE + 8 * g)
            rows = rows[:, h * LANE : h * LANE + SPAN - LANE]
            part = rows if part is None else part + rows
        if g:
            part = pltpu.roll(part, SPAN - LANE - 8 * g, 1)
        total = part if total is None else total + part
    total = pltpu.roll(flipped(total), SPAN - LANE - 7, 1, stride=1, stride_axis=0)
    return jnp.sum(total[:, :width], axis=0, keepdims=True)


def pairs_kernel(core_ref, pair_ref, near_ref, far_ref, out_ref):
    refs = [pair_ref.at[0], pair_ref.at[1], near_ref.at[1, 0], near_ref.at[1, 1], far_ref.at[1, 0], far_ref.at[1, 1]]
    ahead = ahead_of(core_ref[0], [r[MAPPED_AT : MAPPED_AT + SLAB, :] for r in refs])
    row = ahead[:, :ROWS]
    out_ref[...] = along_diagonals(lambda r: column_of(row, r, 8) * ahead, BAND)


def band_kernel(core_ref, skewed_ref, pair_ref, ahead_ref, own_ref, pairs_ref, final_ref, swap_ref, cross_ref, sums_ref):
    core = core_ref[0]
    slabs = [pair_ref[0], pair_ref[1], ahead_ref[0, 0], ahead_ref[0, 1], ahead_ref[1, 0], ahead_ref[1, 1]]
    ahead = ahead_of(core, [s[X_AT : X_AT + SLAB] for s in slabs])
    x_row = ahead[:, :ROWS]
    for start in range(0, ROWS, STEP):
        final_ref[start : start + STEP, :] = (
            skewed_ref[start : start + STEP, :] * column_of(x_row, start, STEP) * ahead
        )
    first, last = final_ref[0:EDGE, :], final_ref[ROWS - EDGE : ROWS, :]
    swap_ref[...] = jnp.where(core == 0, last, first)
    cross_ref[...] = jnp.where(core == 0, first, last)
    diagonals = along_diagonals(lambda r: final_ref[r : r + 8, :], BAND)
    pairs = pairs_ref[...]
    own = own_ref[...]
    row = jnp.concatenate([diagonals, pairs, own[4:5, : LANE // 2], own[5:6, : LANE // 2]], axis=1)
    for n in range(sums_ref.shape[0]):
        sums_ref[n] = row


def straight(rows, start):
    rows = pltpu.roll(flipped(rows), SPAN - start - 7, 1, stride=1, stride_axis=0)
    return flipped(rows[:, :BAND])


def put_tiles(ref, start, value):
    for t in range(WIDE // LANE):
        ref[t, start : start + value.shape[0], :] = value[:, t * LANE : (t + 1) * LANE]


def window_kernel(core_ref, final_ref, swap_ref, cross_ref, pair_ref, ahead_ref, contacts_ref,
                  donut_ref, lower_ref, base_ref, left_out_ref, left_ref, sides_out_ref, sides_ref):
    core = core_ref[0]
    slabs = [pair_ref[0], pair_ref[1], ahead_ref[0, 0], ahead_ref[0, 1], ahead_ref[1, 0], ahead_ref[1, 1]]

    swap, cross = swap_ref[...], cross_ref[...]
    before = jnp.where(core == 0, cross, swap)
    after = jnp.where(core == 0, swap, cross)
    gap = jnp.zeros((EDGE, LANE), F32)
    for start in range(0, ROWS + 2 * EDGE, EDGE):
        if start == 0:
            cells = jnp.concatenate([before[:, ROWS:], gap, before[:, :ROWS]], axis=1)
        elif start == ROWS + EDGE:
            cells = jnp.concatenate([gap] * SLAB + [after[:, : WIDE - ROWS]], axis=1)
        else:
            cells = jnp.concatenate([final_ref[start - EDGE : start, :], gap], axis=1)
        two = cells + pltpu.roll(cells, WIDE - 1, 1)
        three = two + pltpu.roll(cells, WIDE - 2, 1)
        left_out = pltpu.roll(three, 5, 1)
        left = left_out + pltpu.roll(two, 2, 1)
        sides_out = left_out + pltpu.roll(three, WIDE - 3, 1)
        put_tiles(left_out_ref, start, left_out)
        put_tiles(left_ref, start, left)
        put_tiles(sides_out_ref, start, sides_out)
        put_tiles(sides_ref, start, sides_out + (left - left_out) + pltpu.roll(two, WIDE - 1, 1))

    ahead = ahead_of(core, [s[X_AT : X_AT + SLAB] for s in slabs])
    mapped = ahead > 0
    bias_ahead = jnp.where(mapped, 1.0 / jnp.where(mapped, ahead, 1.0), 0.0)
    bias_row = bias_ahead[:, :ROWS]
    near, beyond = range(1, INNER + 1), range(INNER + 1, OUTER + 1)

    for start in range(0, ROWS, 8):

        def rows(ref, shift):
            at = start + EDGE + shift
            return jnp.concatenate([ref[t, at : at + 8, :] for t in range(SPAN // LANE)], axis=1)

        weight = column_of(bias_row, start, 8) * bias_ahead
        lower = sum([rows(left_out_ref, a) for a in near] + [rows(left_ref, a) for a in beyond])
        donut = sum([rows(sides_out_ref, s * a) for a in near for s in (1, -1)]
                    + [rows(sides_ref, s * a) for a in beyond for s in (1, -1)])
        counts = contacts_ref[start : start + 8, :]
        k = jnp.maximum(counts, 1).astype(F32)
        inverse_k = 1.0 / k
        scale = jnp.sqrt(k) * (3.0 / 2.0**0.5)
        distance = lax.broadcasted_iota(jnp.int32, (8, BAND), 1)
        keep = (counts > 0) & (distance >= 2 * OUTER)
        base_ref[start : start + 8, :] = (1.0 - inverse_k * (1.0 / 9.0)) * scale
        for sums, out_ref in ((donut, donut_ref), (lower, lower_ref)):
            value = jnp.where(weight > 0, jnp.maximum(sums, 0.0) * weight, MASKED)
            value = straight(value, start)
            positive = value > 0.0
            root = jnp.exp(jnp.log(jnp.where(positive, value, 1.0) * inverse_k) * (1.0 / 3.0))
            root = jnp.where(positive, root * scale, 0.0)
            out_ref[start : start + 8, :] = jnp.where(keep & (value >= 0.0), root, MASKED)


def half_erfc(x):
    size = jnp.abs(x)
    t = 1.0 / (1.0 + 0.5 * size)
    poly = 0.17087277
    for c in (-0.82215223, 1.48851587, -1.13520398, 0.27886807, -0.18628806, 0.09678418, 0.37409196, 1.00002368, -1.26551223):
        poly = poly * t + c
    tail = 0.5 * t * jnp.exp(poly - size * size)
    return jnp.where(x >= 0.0, tail, 1.0 - tail)


def filter_sums(expected):
    margin = 2 * OUTER
    padded = jnp.concatenate([expected, jnp.zeros((1, LANE), F32)], axis=1)
    donut_weight, lower_weight = {}, {}
    for a in range(-OUTER, OUTER + 1):
        for c in range(-OUTER, OUTER + 1):
            if a and c and not (abs(a) <= INNER and abs(c) <= INNER):
                donut_weight[c - a] = donut_weight.get(c - a, 0) + 1
            if a >= 1 and c <= -1 and not (a <= INNER and c >= -INNER):
                lower_weight[c - a] = lower_weight.get(c - a, 0) + 1
    donut = lower = None
    for k in range(-margin, margin + 1):
        moved = pltpu.roll(padded, (-k) % (BAND + LANE), 1) if k else padded
        moved = moved[:, :BAND]
        if k in donut_weight:
            part = moved * float(donut_weight[k])
            donut = part if donut is None else donut + part
        if k in lower_weight:
            part = moved * float(lower_weight[k])
            lower = part if lower is None else lower + part
    return donut, lower


def cube_root(value):
    positive = value > 0.0
    root = jnp.exp(jnp.log(jnp.where(positive, value, 1.0)) * (1.0 / 3.0))
    return jnp.where(positive, root, value)


def tail_kernel(sums_ref, own_ref, donut_ref, lower_ref, base_ref, pvalue_donut_ref, pvalue_lower_ref, bias_ref, ratio_ref):
    @pl.when(pl.program_id(0) == 0)
    def _():
        total = sums_ref[0]
        for n in range(1, sums_ref.shape[0]):
            total = total + sums_ref[n]
        diagonals, pairs = total[:, :BAND], total[:, BAND : 2 * BAND]
        expected = diagonals / pairs
        donut_exp, lower_exp = filter_sums(expected)
        ratio_ref[0:1, :] = cube_root(expected / donut_exp)
        ratio_ref[1:2, :] = cube_root(expected / lower_exp)
        mapped_count = pairs[:, 0:1]
        half = LANE // 2
        first = total[:, 2 * BAND : 2 * BAND + 1] / mapped_count
        second = total[:, 2 * BAND + half : 2 * BAND + half + 1] / mapped_count
        own = own_ref[...]
        bias = own[SLAB : 2 * SLAB]
        mapped = own[0:SLAB] > 0
        bias_ref[...] = jnp.where(mapped, bias / first / second, 1.0)

    count = base_ref.shape[0]
    for start in range(0, count, STEP):
        base = base_ref[start : start + STEP, :]
        for at, root_ref, out_ref in ((0, donut_ref, pvalue_donut_ref), (1, lower_ref, pvalue_lower_ref)):
            root = root_ref[start : start + STEP, :]
            value = half_erfc(base - root * ratio_ref[at : at + 1, :])
            out_ref[start : start + STEP, :] = jnp.where(root < 0.0, 1.0, value)


def params(mib=8):
    return pltpu.CompilerParams(vmem_limit_bytes=mib * 2**20)


def cost(flops, moved):
    return pl.CostEstimate(flops=flops, bytes_accessed=moved, transcendentals=0)


def call(kernel, ins, outs, specs=None, **more):
    return pl.pallas_call(
        kernel,
        out_shape=[jax.ShapeDtypeStruct(s, F32) for s in outs],
        in_specs=specs or [VMEM] * len(ins),
        out_specs=[VMEM] * len(outs),
        compiler_params=params(),
        **more,
    )(*ins)


def begin(contacts, mapped):
    return call(begin_kernel, (contacts, mapped), [(ROWS, SPAN), (MESSAGE, LANE)])


def middle(core, skewed, pair, near, far):
    return call(middle_kernel, (core, skewed, pair, near, far), [(MESSAGE, LANE)], [SMEM] + [VMEM] * 4)[0]


def last(core, skewed, pair, near, far):
    return call(last_kernel, (core, skewed, pair, near, far), [(8, LANE)], [SMEM] + [VMEM] * 4)[0]


def pair_counts(core, pair, near, far):
    return call(
        pairs_kernel, (core, pair, near, far), [(1, BAND)], [SMEM] + [VMEM] * 3, cost_estimate=cost(10**6, 2**16)
    )[0]


def final_band(core, skewed, pair, ahead, own, pairs, copies):
    return call(
        band_kernel,
        (core, skewed, pair, ahead, own, pairs),
        [(ROWS, SPAN), (EDGE, SPAN), (EDGE, SPAN), (copies, 1, 2 * BAND + LANE)],
        [SMEM] + [VMEM] * 5,
    )


def whole(shape):
    return pl.BlockSpec(shape, lambda i: (0,) * len(shape))


def windows(core, final, swap, cross, pair, ahead, contacts):
    return pl.pallas_call(
        window_kernel,
        out_shape=[jax.ShapeDtypeStruct((ROWS, BAND), F32)] * 3,
        in_specs=[SMEM] + [VMEM] * 6,
        out_specs=[VMEM] * 3,
        scratch_shapes=[pltpu.VMEM((WIDE // LANE, ROWS + 2 * EDGE, LANE), F32)] * 4,
        compiler_params=params(16),
        cost_estimate=cost(2 * 10**7, 6 * 2**20),
    )(core, final, swap, cross, pair, ahead, contacts)


def tails(sums, own, donut, lower, base, count=64):
    block = pl.BlockSpec((count, BAND), lambda i: (i, 0))
    return pl.pallas_call(
        tail_kernel,
        grid=(ROWS // count,),
        out_shape=[jax.ShapeDtypeStruct((ROWS, BAND), F32)] * 2 + [jax.ShapeDtypeStruct((SLAB, LANE), F32)],
        in_specs=[whole(sums.shape), whole(own.shape)] + [block] * 3,
        out_specs=[block] * 2 + [whole((SLAB, LANE))],
        scratch_shapes=[pltpu.VMEM((8, BAND), F32)],
        compiler_params=params(),
    )(sums, own, donut, lower, base)


def solution(mesh):
    count = mesh.shape["genome"]
    plane = min(32, count)
    chips = [[i, i + 1] for i in range(0, count, 2)]
    planes = [[start + i for i in range(plane)] for start in range(0, count, plane)]
    lines = [[i + start for start in range(0, count, plane)] for i in range(plane)]

    def both_cores(value):
        return lax.all_gather(value, "genome", axis_index_groups=chips)

    def moved(value, target):
        pairs = [(i, target(i)) for i in range(count)]
        return lax.ppermute(value, "genome", [(i, t) for i, t in pairs if 0 <= t < count])

    def around(message):
        pair = both_cores(message)
        near = moved(pair, lambda i: i + 2 if i % 2 == 0 else i - 2)
        far = moved(pair, lambda i: i + 4 if i % 2 == 0 else i - 4)
        return pair, both_cores(near), both_cores(far)

    def shards(contacts, mappable):
        core = lax.rem(lax.axis_index("genome"), 2).astype(jnp.int32).reshape(1)
        mapped = mappable.reshape(SLAB, LANE)
        skewed, message = begin(contacts, mapped)
        exchanged = around(message)
        pairs = pair_counts(core, *exchanged)
        message = middle(core, skewed, *exchanged)
        own = last(core, skewed, *around(message))
        pair = both_cores(own)
        ahead = both_cores(moved(pair, lambda i: i - 2 if i % 2 == 0 else i - 4))
        final, swap, cross, sums = final_band(core, skewed, pair, ahead, own, pairs, plane)
        swap = moved(swap, lambda i: i ^ 1)
        cross = moved(cross, lambda i: i - 1 if i % 2 == 0 else i + 1)
        sums = lax.all_to_all(sums, "genome", 0, 0, axis_index_groups=planes)
        sums, swap, cross = lax.optimization_barrier((sums, swap, cross))
        sums = jnp.broadcast_to(jnp.sum(sums, axis=0, keepdims=True), (count // plane,) + sums.shape[1:])
        sums = lax.all_to_all(sums, "genome", 0, 0, axis_index_groups=lines)
        donut, lower, base = windows(core, final, swap, cross, pair, ahead, contacts)
        pvalue_donut, pvalue_lower, bias = tails(sums, own, donut, lower, base)
        return pvalue_donut, pvalue_lower, bias.reshape(ROWS)

    placed = (P("genome", None), P("genome"))
    return jax.shard_map(
        shards,
        mesh=mesh,
        in_specs=placed,
        out_specs=(P("genome", None), P("genome", None), P("genome")),
        check_vma=False,
    )
```

```python
import jax
import jax.numpy as jnp
from jax import lax
from jax.experimental import pallas as pl
from jax.experimental.pallas import tpu as pltpu
from jax.sharding import PartitionSpec as P

OUTER = 5
INNER = 2
ROWS = 256
BAND = 1024
LANE = 128
SLAB = ROWS // LANE
HOPS = BAND // ROWS
SPAN = ROWS + BAND
WIDE = SPAN + LANE
STEP = 32
EDGE = 8
MASKED = -1.0
VMEM = pl.BlockSpec(memory_space=pltpu.VMEM)
SMEM = pl.BlockSpec(memory_space=pltpu.SMEM)
F32 = jnp.float32
X_AT, SPREAD_AT, SUMS_AT, MAPPED_AT, MESSAGE = 0, SLAB, SLAB * (HOPS + 2), SLAB * (HOPS + 3), 16


def lanes(tiles):
    return jnp.concatenate([tiles[r : r + 1] for r in range(tiles.shape[0])], axis=1)


def put_lanes(ref, first, row):
    for t in range(row.shape[1] // LANE):
        ref[first + t : first + t + 1, :] = row[:, t * LANE : (t + 1) * LANE]


def on_diagonal(start, count, width):
    rows = lax.broadcasted_iota(jnp.int32, (count, width), 0) + start
    return rows == lax.broadcasted_iota(jnp.int32, (count, width), 1)


def column_of(row, start, count):
    part = jnp.where(on_diagonal(start, count, ROWS), row, 0.0)
    return jnp.sum(part, axis=1, keepdims=True)


def fold(value):
    total = value[0:8]
    for r in range(8, value.shape[0], 8):
        total = total + value[r : r + 8]
    return total


def spread_part(rows, weight_row, start):
    part = rows * column_of(weight_row, start, STEP)
    return fold(jnp.where(on_diagonal(start, STEP, SPAN), 0.0, part))


def spread_of(skewed_ref, weight_row):
    total = jnp.zeros((8, SPAN), F32)
    for start in range(0, ROWS, STEP):
        total = total + spread_part(skewed_ref[start : start + STEP, :], weight_row, start)
    return jnp.sum(total, axis=0, keepdims=True)


def own_sums(skewed_ref, ahead_row):
    total = jnp.zeros((8, ROWS), F32)
    for start in range(0, ROWS, STEP):
        part = skewed_ref[start : start + STEP, :] * ahead_row
        sums = jnp.sum(part, axis=1, keepdims=True)
        total = total + fold(jnp.where(on_diagonal(start, STEP, ROWS), sums, 0.0))
    return jnp.sum(total, axis=0, keepdims=True)


def put_message(out_ref, x_row, spread_row, sums_row, mapped_row):
    put_lanes(out_ref, X_AT, x_row)
    put_lanes(out_ref, SPREAD_AT, spread_row)
    put_lanes(out_ref, SUMS_AT, sums_row)
    put_lanes(out_ref, MAPPED_AT, mapped_row)


def begin_kernel(contacts_ref, mapped_ref, skewed_ref, out_ref):
    for start in range(0, ROWS, STEP):
        counts = contacts_ref[start : start + STEP, :].astype(F32)
        padded = jnp.concatenate([counts, jnp.zeros((STEP, SPAN - BAND), F32)], axis=1)
        skewed_ref[start : start + STEP, :] = pltpu.roll(padded, start, 1, stride=1, stride_axis=0)
    mapped = lanes(mapped_ref[...]).astype(F32)
    put_message(out_ref, mapped, spread_of(skewed_ref, mapped), jnp.zeros((1, ROWS), F32), mapped)


def ahead_of(core, slabs):
    tiles = [jnp.where(core == 0, slabs[k], slabs[k + 1]) for k in range(HOPS + 1)]
    return jnp.concatenate([lanes(t) for t in tiles], axis=1)


def sum_rows(core_ref, skewed_ref, pair_ref, near_ref, far_ref):
    core = core_ref[0]

    def message(k):
        at = k % 2
        chip = k // 2
        if chip == 0:
            return pair_ref.at[at]
        ref = near_ref if abs(chip) == 1 else far_ref
        return ref.at[1 if chip > 0 else 0, at]

    x_tiles = [message(k)[X_AT : X_AT + SLAB, :] for k in range(HOPS + 2)]
    arrived = jnp.zeros((SLAB, LANE), F32)
    for k in range(HOPS + 1):
        at = SPREAD_AT + SLAB * k
        arrived = arrived + jnp.where(
            core == 0, message(-k)[at : at + SLAB, :], message(1 - k)[at : at + SLAB, :]
        )
    sums = own_sums(skewed_ref, ahead_of(core, x_tiles)) + lanes(arrived)
    x_row = lanes(jnp.where(core == 0, x_tiles[0], x_tiles[1]))
    mapped = jnp.where(core == 0, pair_ref[0, MAPPED_AT : MAPPED_AT + SLAB, :], pair_ref[1, MAPPED_AT : MAPPED_AT + SLAB, :])
    return lanes(mapped), x_row * sums


def middle_kernel(core_ref, skewed_ref, pair_ref, near_ref, far_ref, out_ref):
    mapped, sums = sum_rows(core_ref, skewed_ref, pair_ref, near_ref, far_ref)
    x_row = jnp.where(mapped > 0, 1.0 / jnp.where(mapped > 0, sums, 1.0), 0.0)
    put_message(out_ref, x_row, spread_of(skewed_ref, x_row), sums, mapped)


def last_kernel(core_ref, skewed_ref, pair_ref, near_ref, far_ref, out_ref):
    mapped, sums = sum_rows(core_ref, skewed_ref, pair_ref, near_ref, far_ref)
    before = jnp.where(core_ref[0] == 0, pair_ref[0], pair_ref[1])
    before = lanes(before[SUMS_AT : SUMS_AT + SLAB])
    bias = jnp.where(mapped > 0, before * sums, 1.0)
    out_ref[...] = jnp.zeros((8, LANE), F32)
    put_lanes(out_ref, 0, jnp.where(mapped > 0, 1.0 / bias, 0.0))
    put_lanes(out_ref, SLAB, bias)
    for at, value in ((4, before), (5, sums)):
        total = jnp.sum(jnp.where(mapped > 0, value, 0.0), axis=1, keepdims=True)
        out_ref[at : at + 1, :] = jnp.broadcast_to(total, (1, LANE))


def flipped(rows):
    order = 7 - lax.broadcasted_iota(jnp.int32, (8, LANE), 0)
    tiles = [jnp.take_along_axis(rows[:, t : t + LANE], order, axis=0, mode="promise_in_bounds") for t in range(0, rows.shape[1], LANE)]
    return jnp.concatenate(tiles, axis=1)


def along_diagonals(rows_of, width):
    total = None
    for g in range(LANE // 8):
        part = None
        for h in range(SLAB):
            rows = rows_of(h * LANE + 8 * g)
            rows = rows[:, h * LANE : h * LANE + SPAN - LANE]
            part = rows if part is None else part + rows
        if g:
            part = pltpu.roll(part, SPAN - LANE - 8 * g, 1)
        total = part if total is None else total + part
    total = pltpu.roll(flipped(total), SPAN - LANE - 7, 1, stride=1, stride_axis=0)
    return jnp.sum(total[:, :width], axis=0, keepdims=True)


def pairs_kernel(core_ref, pair_ref, near_ref, far_ref, out_ref):
    refs = [pair_ref.at[0], pair_ref.at[1], near_ref.at[1, 0], near_ref.at[1, 1], far_ref.at[1, 0], far_ref.at[1, 1]]
    ahead = ahead_of(core_ref[0], [r[MAPPED_AT : MAPPED_AT + SLAB, :] for r in refs])
    row = ahead[:, :ROWS]
    out_ref[...] = along_diagonals(lambda r: column_of(row, r, 8) * ahead, BAND)


def band_kernel(core_ref, skewed_ref, pair_ref, ahead_ref, own_ref, pairs_ref,
                swap_ref, cross_ref, sums_ref, vectors_ref, final_ref):
    core = core_ref[0]
    slabs = [pair_ref[0], pair_ref[1], ahead_ref[0, 0], ahead_ref[0, 1], ahead_ref[1, 0], ahead_ref[1, 1]]
    ahead = ahead_of(core, [s[X_AT : X_AT + SLAB] for s in slabs])
    x_row = ahead[:, :ROWS]
    for start in range(0, ROWS, STEP):
        final_ref[start : start + STEP, :] = (
            skewed_ref[start : start + STEP, :] * column_of(x_row, start, STEP) * ahead
        )
    first, last = final_ref[0:EDGE, :], final_ref[ROWS - EDGE : ROWS, :]
    swap_ref[...] = jnp.where(core == 0, last, first)
    cross_ref[...] = jnp.where(core == 0, first, last)
    diagonals = along_diagonals(lambda r: final_ref[r : r + 8, :], BAND)
    own = own_ref[...]
    row = jnp.concatenate([diagonals, pairs_ref[...], own[4:5, : LANE // 2], own[5:6, : LANE // 2]], axis=1)
    for n in range(sums_ref.shape[0]):
        sums_ref[n] = row
    vectors_ref[0:1, :] = ahead
    vectors_ref[1:2, :] = jnp.where(ahead > 0, 1.0 / jnp.where(ahead > 0, ahead, 1.0), 0.0)
    vectors_ref[2:3, :] = jnp.concatenate([lanes(own[SLAB : 2 * SLAB]), jnp.zeros((1, SPAN - ROWS), F32)], axis=1)


def straight(rows, start):
    rows = pltpu.roll(flipped(rows), SPAN - start - 7, 1, stride=1, stride_axis=0)
    return flipped(rows[:, :BAND])


def put_tiles(ref, start, value):
    for t in range(value.shape[1] // LANE):
        ref[t, start : start + value.shape[0], :] = value[:, t * LANE : (t + 1) * LANE]


def put_tables(refs, start, cells):
    left_out_ref, left_ref, sides_out_ref, sides_ref = refs
    two = cells + pltpu.roll(cells, WIDE - 1, 1)
    three = two + pltpu.roll(cells, WIDE - 2, 1)
    left_out = pltpu.roll(three, 5, 1)
    left_in = pltpu.roll(two, 2, 1)
    sides_out = left_out + pltpu.roll(three, WIDE - 3, 1)
    put_tiles(left_out_ref, start, left_out)
    put_tiles(left_ref, start, left_out + left_in)
    put_tiles(sides_out_ref, start, sides_out)
    put_tiles(sides_ref, start, sides_out + left_in + pltpu.roll(two, WIDE - 1, 1))


NEAR, BEYOND = range(1, INNER + 1), range(INNER + 1, OUTER + 1)


def box_sums(out_ref, in_ref, at, signs):
    def rows(ref, shift):
        return jnp.concatenate([ref[t, at + shift : at + shift + 8, :] for t in range(SPAN // LANE)], axis=1)

    return sum([rows(out_ref, s * a) for a in NEAR for s in signs] + [rows(in_ref, s * a) for a in BEYOND for s in signs])


def scale_of(counts):
    k = jnp.maximum(counts, 1).astype(F32)
    return 1.0 / k, jnp.sqrt(k) * (3.0 / 2.0**0.5)


def root_of(sums, weight, start, counts, inverse_k, scale):
    value = jnp.where(weight > 0, jnp.maximum(sums, 0.0) * weight, MASKED)
    value = straight(value, start)
    positive = value > 0.0
    root = jnp.exp(jnp.log(jnp.where(positive, value, 1.0) * inverse_k) * (1.0 / 3.0))
    root = jnp.where(positive, root * scale, 0.0)
    distance = lax.broadcasted_iota(jnp.int32, (8, BAND), 1)
    return jnp.where((counts > 0) & (distance >= 2 * OUTER) & (value >= 0.0), root, MASKED)


def window_kernel(contacts_ref, vectors_ref, donut_ref, lower_ref, base_hbm, partial_ref, counts_ref,
                  left_out_ref, left_ref, sides_out_ref, sides_ref, base_ref, sems):
    ahead, bias_ahead = vectors_ref[0:1, :], vectors_ref[1:2, :]
    x_row, bias_row = ahead[:, :ROWS], bias_ahead[:, :ROWS]
    tables = (left_out_ref, left_ref, sides_out_ref, sides_ref)
    empty = jnp.zeros((EDGE, WIDE), F32)
    for ref in tables:
        put_tiles(ref, 0, empty)
        put_tiles(ref, ROWS + EDGE, empty)
    for start in range(0, ROWS, 8):
        cells = contacts_ref[start : start + 8, :].astype(F32)
        cells = jnp.concatenate([cells, jnp.zeros((8, SPAN - BAND), F32)], axis=1)
        cells = pltpu.roll(cells, start, 1, stride=1, stride_axis=0) * column_of(x_row, start, 8) * ahead
        put_tables(tables, start + EDGE, jnp.concatenate([cells, jnp.zeros((8, WIDE - SPAN), F32)], axis=1))
    copies = []
    for start in range(0, ROWS, 8):
        weight = column_of(bias_row, start, 8) * bias_ahead
        lower = box_sums(left_out_ref, left_ref, start + EDGE, (1,))
        donut = box_sums(sides_out_ref, sides_ref, start + EDGE, (1, -1))
        counts = contacts_ref[start : start + 8, :]
        inverse_k, scale = scale_of(counts)
        base_ref[start : start + 8, :] = (1.0 - inverse_k * (1.0 / 9.0)) * scale
        donut_ref[start : start + 8, :] = root_of(donut, weight, start, counts, inverse_k, scale)
        lower_ref[start : start + 8, :] = root_of(lower, weight, start, counts, inverse_k, scale)
        if start == 0:
            partial_ref[0:8, :] = donut
            counts_ref[0:8, :] = counts
        if start == ROWS - 8:
            partial_ref[8:16, :] = donut
            partial_ref[16:24, :] = lower
            counts_ref[8:16, :] = counts
        if (start + 8) % (ROWS // 4) == 0:
            n = len(copies)
            part = pl.ds(n * (ROWS // 4), ROWS // 4)
            copies.append(pltpu.make_async_copy(base_ref.at[part, :], base_hbm.at[part, :], sems.at[n]))
            copies[n].start()
    for copy in copies:
        copy.wait()


def edge_kernel(core_ref, swap_ref, cross_ref, partial_ref, counts_ref, vectors_ref, out_ref,
                left_out_ref, left_ref, sides_out_ref, sides_ref):
    core = core_ref[0]
    swap, cross = swap_ref[...], cross_ref[...]
    before = jnp.where(core == 0, cross, swap)
    after = jnp.where(core == 0, swap, cross)
    gap = jnp.zeros((EDGE, LANE), F32)
    empty = jnp.zeros((EDGE, WIDE), F32)
    tables = (left_out_ref, left_ref, sides_out_ref, sides_ref)
    for ref in tables:
        put_tiles(ref, EDGE, empty)
    put_tables(tables, 0, jnp.concatenate([before[:, ROWS:], gap, before[:, :ROWS]], axis=1))
    put_tables(tables, 2 * EDGE, jnp.concatenate([gap] * SLAB + [after[:, : WIDE - ROWS]], axis=1))
    bias_ahead = vectors_ref[1:2, :]
    bias_row = bias_ahead[:, :ROWS]
    last = ROWS - 8
    donut_first = partial_ref[0:8, :] + box_sums(sides_out_ref, sides_ref, EDGE, (-1,))
    donut_last = partial_ref[8:16, :] + box_sums(sides_out_ref, sides_ref, EDGE, (1,))
    lower_last = partial_ref[16:24, :] + box_sums(left_out_ref, left_ref, EDGE, (1,))
    for at, sums, start, half in ((0, donut_first, 0, 0), (8, donut_last, last, 8), (16, lower_last, last, 8)):
        counts = counts_ref[half : half + 8, :]
        weight = column_of(bias_row, start, 8) * bias_ahead
        out_ref[at : at + 8, :] = root_of(sums, weight, start, counts, *scale_of(counts))
    out_ref[24:25, :] = jnp.concatenate([vectors_ref[2:3, :ROWS], vectors_ref[0:1, : BAND - ROWS]], axis=1)


def half_erfc(x):
    size = jnp.abs(x)
    t = 1.0 / (1.0 + 0.5 * size)
    poly = 0.17087277
    for c in (-0.82215223, 1.48851587, -1.13520398, 0.27886807, -0.18628806, 0.09678418, 0.37409196, 1.00002368, -1.26551223):
        poly = poly * t + c
    tail = 0.5 * t * jnp.exp(poly - size * size)
    return jnp.where(x >= 0.0, tail, 1.0 - tail)


def filter_sums(expected):
    lane = lax.broadcasted_iota(jnp.int32, expected.shape, 1)
    none = jnp.zeros((1, LANE), F32)
    after = jnp.concatenate([expected[1:], none], axis=0)
    before = jnp.concatenate([none, expected[:-1]], axis=0)
    donut_weight, lower_weight = {}, {}
    for a in range(-OUTER, OUTER + 1):
        for c in range(-OUTER, OUTER + 1):
            if a and c and not (abs(a) <= INNER and abs(c) <= INNER):
                donut_weight[c - a] = donut_weight.get(c - a, 0) + 1
            if a >= 1 and c <= -1 and not (a <= INNER and c >= -INNER):
                lower_weight[c - a] = lower_weight.get(c - a, 0) + 1
    donut = lower = None
    for k in range(-2 * OUTER, 2 * OUTER + 1):
        moved = expected
        if k:
            turn = (-k) % LANE
            here = (lane + k < LANE) if k > 0 else (lane + k >= 0)
            moved = jnp.where(here, pltpu.roll(expected, turn, 1), pltpu.roll(after if k > 0 else before, turn, 1))
        if k in donut_weight:
            part = moved * float(donut_weight[k])
            donut = part if donut is None else donut + part
        if k in lower_weight:
            part = moved * float(lower_weight[k])
            lower = part if lower is None else lower + part
    return donut, lower


def cube_root(value):
    positive = value > 0.0
    root = jnp.exp(jnp.log(jnp.where(positive, value, 1.0)) * (1.0 / 3.0))
    return jnp.where(positive, root, value)


def tiled(row):
    return jnp.concatenate([row[:, t : t + LANE] for t in range(0, row.shape[1], LANE)], axis=0)


def tail_kernel(sums_ref, edge_ref, donut_ref, lower_ref, base_hbm, pvalue_donut_ref, pvalue_lower_ref, bias_ref,
                ratio_ref, base_ref, sems):
    step = pl.program_id(0)
    count = donut_ref.shape[0]

    def copy_of(n):
        part = pl.ds(n * count, count)
        return pltpu.make_async_copy(base_hbm.at[part, :], base_ref.at[part, :], sems.at[n])

    @pl.when(step == 0)
    def _():
        for n in range(ROWS // count):
            copy_of(n).start()
        total = sums_ref[0]
        for n in range(1, sums_ref.shape[0]):
            total = total + sums_ref[n]
        pairs = tiled(total[:, BAND : 2 * BAND])
        expected = tiled(total[:, :BAND]) / pairs
        donut_exp, lower_exp = filter_sums(expected)
        ratio_ref[0:1, :] = lanes(cube_root(expected / donut_exp))
        ratio_ref[1:2, :] = lanes(cube_root(expected / lower_exp))
        mapped_count = pairs[0:1, 0:1]
        half = LANE // 2
        first = total[:, 2 * BAND : 2 * BAND + 1] / mapped_count
        second = total[:, 2 * BAND + half : 2 * BAND + half + 1] / mapped_count
        own = edge_ref[24:25, :]
        bias = jnp.where(own[:, ROWS : 2 * ROWS] > 0, own[:, :ROWS] / first / second, 1.0)
        put_lanes(bias_ref, 0, bias)

    for n in range(ROWS // count):

        @pl.when(step == n)
        def _():
            copy_of(n).wait()

    for start in range(0, count, STEP):
        base = base_ref[pl.ds(pl.multiple_of(step * count + start, STEP), STEP), :]
        for at, root_ref, out_ref in ((0, donut_ref, pvalue_donut_ref), (1, lower_ref, pvalue_lower_ref)):
            root = root_ref[start : start + STEP, :]
            if start == 0 and at == 0:
                top = jnp.where(step == 0, edge_ref[0:8, :], root[0:8])
                root = jnp.concatenate([top, root[8:]], axis=0)
            if start == count - STEP:
                edge = edge_ref[8:16, :] if at == 0 else edge_ref[16:24, :]
                bottom = jnp.where(step == ROWS // count - 1, edge, root[STEP - 8 :])
                root = jnp.concatenate([root[: STEP - 8], bottom], axis=0)
            value = half_erfc(base - root * ratio_ref[at : at + 1, :])
            out_ref[start : start + STEP, :] = jnp.where(root < 0.0, 1.0, value)


def params(mib=8):
    return pltpu.CompilerParams(vmem_limit_bytes=mib * 2**20)


def cost(flops, moved):
    return pl.CostEstimate(flops=flops, bytes_accessed=moved, transcendentals=0)


def call(kernel, ins, outs, specs=None, **more):
    return pl.pallas_call(
        kernel,
        out_shape=[jax.ShapeDtypeStruct(s, F32) for s in outs],
        in_specs=specs or [VMEM] * len(ins),
        out_specs=[VMEM] * len(outs),
        compiler_params=params(),
        **more,
    )(*ins)


def begin(contacts, mapped):
    return call(begin_kernel, (contacts, mapped), [(ROWS, SPAN), (MESSAGE, LANE)])


def middle(core, skewed, pair, near, far):
    return call(middle_kernel, (core, skewed, pair, near, far), [(MESSAGE, LANE)], [SMEM] + [VMEM] * 4)[0]


def last(core, skewed, pair, near, far):
    return call(last_kernel, (core, skewed, pair, near, far), [(8, LANE)], [SMEM] + [VMEM] * 4)[0]


def pair_counts(core, pair, near, far):
    return call(
        pairs_kernel, (core, pair, near, far), [(1, BAND)], [SMEM] + [VMEM] * 3, cost_estimate=cost(10**6, 2**16)
    )[0]


def final_band(core, skewed, pair, ahead, own, pairs, copies):
    return call(
        band_kernel,
        (core, skewed, pair, ahead, own, pairs),
        [(EDGE, SPAN), (EDGE, SPAN), (copies, 1, 2 * BAND + LANE), (8, SPAN)],
        [SMEM] + [VMEM] * 5,
        scratch_shapes=[pltpu.VMEM((ROWS, SPAN), F32)],
    )


def whole(shape):
    return pl.BlockSpec(shape, lambda i: (0,) * len(shape))


def windows(contacts, vectors):
    return pl.pallas_call(
        window_kernel,
        out_shape=[jax.ShapeDtypeStruct((ROWS, BAND), F32)] * 3
        + [jax.ShapeDtypeStruct((24, SPAN), F32), jax.ShapeDtypeStruct((16, BAND), jnp.int32)],
        in_specs=[VMEM] * 2,
        out_specs=[VMEM, VMEM, pl.BlockSpec(memory_space=pltpu.HBM), VMEM, VMEM],
        scratch_shapes=[pltpu.VMEM((WIDE // LANE, ROWS + 2 * EDGE, LANE), F32)] * 4
        + [pltpu.VMEM((ROWS, BAND), F32), pltpu.SemaphoreType.DMA((4,))],
        compiler_params=params(16),
        cost_estimate=cost(2 * 10**7, 6 * 2**20),
    )(contacts, vectors)


def edges(core, swap, cross, partial, counts, vectors):
    return call(
        edge_kernel,
        (core, swap, cross, partial, counts, vectors),
        [(32, BAND)],
        [SMEM] + [VMEM] * 5,
        scratch_shapes=[pltpu.VMEM((WIDE // LANE, 3 * EDGE, LANE), F32)] * 4,
        cost_estimate=cost(10**6, 2**20),
    )[0]


def tails(sums, edge, donut, lower, base, count=64):
    block = pl.BlockSpec((count, BAND), lambda i: (i, 0))
    return pl.pallas_call(
        tail_kernel,
        grid=(ROWS // count,),
        out_shape=[jax.ShapeDtypeStruct((ROWS, BAND), F32)] * 2 + [jax.ShapeDtypeStruct((SLAB, LANE), F32)],
        in_specs=[whole(sums.shape), whole(edge.shape)] + [block] * 2 + [pl.BlockSpec(memory_space=pltpu.HBM)],
        out_specs=[block] * 2 + [whole((SLAB, LANE))],
        scratch_shapes=[
            pltpu.VMEM((8, BAND), F32),
            pltpu.VMEM((ROWS, BAND), F32),
            pltpu.SemaphoreType.DMA((ROWS // count,)),
        ],
        compiler_params=params(),
    )(sums, edge, donut, lower, base)


def solution(mesh):
    count = mesh.shape["genome"]
    plane = min(32, count)
    chips = [[i, i + 1] for i in range(0, count, 2)]
    planes = [[start + i for i in range(plane)] for start in range(0, count, plane)]
    lines = [[i + start for start in range(0, count, plane)] for i in range(plane)]

    def both_cores(value):
        return lax.all_gather(value, "genome", axis_index_groups=chips)

    def moved(value, target):
        pairs = [(i, target(i)) for i in range(count)]
        return lax.ppermute(value, "genome", [(i, t) for i, t in pairs if 0 <= t < count])

    def around(message):
        pair = both_cores(message)
        near = moved(pair, lambda i: i + 2 if i % 2 == 0 else i - 2)
        far = moved(pair, lambda i: i + 4 if i % 2 == 0 else i - 4)
        return pair, both_cores(near), both_cores(far)

    def shards(contacts, mappable):
        core = lax.rem(lax.axis_index("genome"), 2).astype(jnp.int32).reshape(1)
        mapped = mappable.reshape(SLAB, LANE)
        skewed, message = begin(contacts, mapped)
        exchanged = around(message)
        pairs = pair_counts(core, *exchanged)
        message = middle(core, skewed, *exchanged)
        own = last(core, skewed, *around(message))
        pair = both_cores(own)
        ahead = both_cores(moved(pair, lambda i: i - 2 if i % 2 == 0 else i - 4))
        swap, cross, sums, vectors = final_band(core, skewed, pair, ahead, own, pairs, plane)
        sums = lax.all_to_all(sums, "genome", 0, 0, axis_index_groups=planes)
        donut, lower, base, partial, counts = windows(contacts, vectors)
        sums, swap, cross, partial = lax.optimization_barrier((sums, swap, cross, partial))
        sums = jnp.broadcast_to(jnp.sum(sums, axis=0, keepdims=True), (count // plane,) + sums.shape[1:])
        sums = lax.all_to_all(sums, "genome", 0, 0, axis_index_groups=lines)
        swap = moved(swap, lambda i: i ^ 1)
        cross = moved(cross, lambda i: i - 1 if i % 2 == 0 else i + 1)
        edge = edges(core, swap, cross, partial, counts, vectors)
        pvalue_donut, pvalue_lower, bias = tails(sums, edge, donut, lower, base)
        return pvalue_donut, pvalue_lower, bias.reshape(ROWS)

    placed = (P("genome", None), P("genome"))
    return jax.shard_map(
        shards,
        mesh=mesh,
        in_specs=placed,
        out_specs=(P("genome", None), P("genome", None), P("genome")),
        check_vma=False,
    )
```

```python
import jax
import jax.numpy as jnp
from jax import lax
from jax.experimental import pallas as pl
from jax.experimental.pallas import tpu as pltpu
from jax.sharding import PartitionSpec as P

OUTER = 5
INNER = 2
ROWS = 256
BAND = 1024
LANE = 128
SLAB = ROWS // LANE
HOPS = BAND // ROWS
SPAN = ROWS + BAND
WIDE = SPAN + LANE
STEP = 32
EDGE = 8
MASKED = -1.0
TABLE_STEP = 32
VMEM = pl.BlockSpec(memory_space=pltpu.VMEM)
SMEM = pl.BlockSpec(memory_space=pltpu.SMEM)
F32 = jnp.float32
X_AT, SPREAD_AT, SUMS_AT, MAPPED_AT, MESSAGE = 0, SLAB, SLAB * (HOPS + 2), SLAB * (HOPS + 3), 16


def lanes(tiles):
    return jnp.concatenate([tiles[r : r + 1] for r in range(tiles.shape[0])], axis=1)


def put_lanes(ref, first, row):
    for t in range(row.shape[1] // LANE):
        ref[first + t : first + t + 1, :] = row[:, t * LANE : (t + 1) * LANE]


def on_diagonal(start, count, width):
    rows = lax.broadcasted_iota(jnp.int32, (count, width), 0) + start
    return rows == lax.broadcasted_iota(jnp.int32, (count, width), 1)


def column_of(row, start, count):
    part = jnp.where(on_diagonal(start, count, ROWS), row, 0.0)
    return jnp.sum(part, axis=1, keepdims=True)


def fold(value):
    total = value[0:8]
    for r in range(8, value.shape[0], 8):
        total = total + value[r : r + 8]
    return total


def spread_part(rows, weight_row, start):
    part = rows * column_of(weight_row, start, STEP)
    return fold(jnp.where(on_diagonal(start, STEP, SPAN), 0.0, part))


def spread_of(skewed_ref, weight_row):
    total = jnp.zeros((8, SPAN), F32)
    for start in range(0, ROWS, STEP):
        total = total + spread_part(skewed_ref[start : start + STEP, :], weight_row, start)
    return jnp.sum(total, axis=0, keepdims=True)


def own_sums(skewed_ref, ahead_row):
    total = jnp.zeros((8, ROWS), F32)
    for start in range(0, ROWS, STEP):
        part = skewed_ref[start : start + STEP, :] * ahead_row
        sums = jnp.sum(part, axis=1, keepdims=True)
        total = total + fold(jnp.where(on_diagonal(start, STEP, ROWS), sums, 0.0))
    return jnp.sum(total, axis=0, keepdims=True)


def put_message(out_ref, x_row, spread_row, sums_row, mapped_row):
    put_lanes(out_ref, X_AT, x_row)
    put_lanes(out_ref, SPREAD_AT, spread_row)
    put_lanes(out_ref, SUMS_AT, sums_row)
    put_lanes(out_ref, MAPPED_AT, mapped_row)


def begin_kernel(contacts_ref, mapped_ref, skewed_ref, out_ref, counts_ref):
    for start in range(0, ROWS, STEP):
        counts = contacts_ref[start : start + STEP, :]
        counts_ref[start : start + STEP, :] = counts.astype(jnp.int16)
        counts = counts.astype(F32)
        padded = jnp.concatenate([counts, jnp.zeros((STEP, SPAN - BAND), F32)], axis=1)
        skewed_ref[start : start + STEP, :] = pltpu.roll(padded, start, 1, stride=1, stride_axis=0)
    mapped = lanes(mapped_ref[...]).astype(F32)
    put_message(out_ref, mapped, spread_of(skewed_ref, mapped), jnp.zeros((1, ROWS), F32), mapped)


def ahead_of(core, slabs):
    tiles = [jnp.where(core == 0, slabs[k], slabs[k + 1]) for k in range(HOPS + 1)]
    return jnp.concatenate([lanes(t) for t in tiles], axis=1)


def sum_rows(core_ref, skewed_ref, pair_ref, near_ref, far_ref):
    core = core_ref[0]

    def message(k):
        at = k % 2
        chip = k // 2
        if chip == 0:
            return pair_ref.at[at]
        ref = near_ref if abs(chip) == 1 else far_ref
        return ref.at[1 if chip > 0 else 0, at]

    x_tiles = [message(k)[X_AT : X_AT + SLAB, :] for k in range(HOPS + 2)]
    arrived = jnp.zeros((SLAB, LANE), F32)
    for k in range(HOPS + 1):
        at = SPREAD_AT + SLAB * k
        arrived = arrived + jnp.where(
            core == 0, message(-k)[at : at + SLAB, :], message(1 - k)[at : at + SLAB, :]
        )
    sums = own_sums(skewed_ref, ahead_of(core, x_tiles)) + lanes(arrived)
    x_row = lanes(jnp.where(core == 0, x_tiles[0], x_tiles[1]))
    mapped = jnp.where(core == 0, pair_ref[0, MAPPED_AT : MAPPED_AT + SLAB, :], pair_ref[1, MAPPED_AT : MAPPED_AT + SLAB, :])
    return lanes(mapped), x_row * sums


def middle_kernel(core_ref, skewed_ref, pair_ref, near_ref, far_ref, out_ref):
    mapped, sums = sum_rows(core_ref, skewed_ref, pair_ref, near_ref, far_ref)
    x_row = jnp.where(mapped > 0, 1.0 / jnp.where(mapped > 0, sums, 1.0), 0.0)
    put_message(out_ref, x_row, spread_of(skewed_ref, x_row), sums, mapped)


def last_kernel(core_ref, skewed_ref, pair_ref, near_ref, far_ref, out_ref):
    mapped, sums = sum_rows(core_ref, skewed_ref, pair_ref, near_ref, far_ref)
    before = jnp.where(core_ref[0] == 0, pair_ref[0], pair_ref[1])
    before = lanes(before[SUMS_AT : SUMS_AT + SLAB])
    bias = jnp.where(mapped > 0, before * sums, 1.0)
    out_ref[...] = jnp.zeros((8, LANE), F32)
    put_lanes(out_ref, 0, jnp.where(mapped > 0, 1.0 / bias, 0.0))
    put_lanes(out_ref, SLAB, bias)
    for at, value in ((4, before), (5, sums)):
        total = jnp.sum(jnp.where(mapped > 0, value, 0.0), axis=1, keepdims=True)
        out_ref[at : at + 1, :] = jnp.broadcast_to(total, (1, LANE))


def flipped(rows):
    order = 7 - lax.broadcasted_iota(jnp.int32, (8, LANE), 0)
    tiles = [jnp.take_along_axis(rows[:, t : t + LANE], order, axis=0, mode="promise_in_bounds") for t in range(0, rows.shape[1], LANE)]
    return jnp.concatenate(tiles, axis=1)


def along_diagonals(rows_of, width):
    total = None
    for g in range(LANE // 8):
        part = None
        for h in range(SLAB):
            rows = rows_of(h * LANE + 8 * g)
            rows = rows[:, h * LANE : h * LANE + SPAN - LANE]
            part = rows if part is None else part + rows
        if g:
            part = pltpu.roll(part, SPAN - LANE - 8 * g, 1)
        total = part if total is None else total + part
    total = pltpu.roll(flipped(total), SPAN - LANE - 7, 1, stride=1, stride_axis=0)
    return jnp.sum(total[:, :width], axis=0, keepdims=True)


def pairs_kernel(core_ref, pair_ref, near_ref, far_ref, out_ref):
    refs = [pair_ref.at[0], pair_ref.at[1], near_ref.at[1, 0], near_ref.at[1, 1], far_ref.at[1, 0], far_ref.at[1, 1]]
    ahead = ahead_of(core_ref[0], [r[MAPPED_AT : MAPPED_AT + SLAB, :] for r in refs])
    row = ahead[:, :ROWS]
    out_ref[...] = along_diagonals(lambda r: column_of(row, r, 8) * ahead, BAND)


def band_kernel(core_ref, skewed_ref, pair_ref, ahead_ref, own_ref, pairs_ref,
                final_ref, swap_ref, cross_ref, sums_ref, vectors_ref):
    core = core_ref[0]
    slabs = [pair_ref[0], pair_ref[1], ahead_ref[0, 0], ahead_ref[0, 1], ahead_ref[1, 0], ahead_ref[1, 1]]
    ahead = ahead_of(core, [s[X_AT : X_AT + SLAB] for s in slabs])
    x_row = ahead[:, :ROWS]
    for start in range(0, ROWS, STEP):
        final_ref[start : start + STEP, :] = (
            skewed_ref[start : start + STEP, :] * column_of(x_row, start, STEP) * ahead
        )
    first, last = final_ref[0:EDGE, :], final_ref[ROWS - EDGE : ROWS, :]
    swap_ref[...] = jnp.where(core == 0, last, first)
    cross_ref[...] = jnp.where(core == 0, first, last)
    diagonals = along_diagonals(lambda r: final_ref[r : r + 8, :], BAND)
    own = own_ref[...]
    row = jnp.concatenate([diagonals, pairs_ref[...], own[4:5, : LANE // 2], own[5:6, : LANE // 2]], axis=1)
    for n in range(sums_ref.shape[0]):
        sums_ref[n] = row
    vectors_ref[0:1, :] = ahead
    vectors_ref[1:2, :] = jnp.where(ahead > 0, 1.0 / jnp.where(ahead > 0, ahead, 1.0), 0.0)
    vectors_ref[2:3, :] = jnp.concatenate([lanes(own[SLAB : 2 * SLAB]), jnp.zeros((1, SPAN - ROWS), F32)], axis=1)


def straight(rows, start, tile):
    rows = pltpu.roll(flipped(rows), SPAN - 7 - start, 1, stride=1, stride_axis=0)
    return flipped(rows[:, tile * LANE : tile * LANE + BAND])


def put_tiles(ref, start, value):
    for t in range(value.shape[1] // LANE):
        ref[t, pl.ds(start, value.shape[0]), :] = value[:, t * LANE : (t + 1) * LANE]


def put_tables(refs, start, cells):
    left_out_ref, left_ref, sides_out_ref, sides_ref = refs
    two = cells + pltpu.roll(cells, WIDE - 1, 1)
    three = two + pltpu.roll(cells, WIDE - 2, 1)
    left_out = pltpu.roll(three, 5, 1)
    left_in = pltpu.roll(two, 2, 1)
    sides_out = left_out + pltpu.roll(three, WIDE - 3, 1)
    put_tiles(left_out_ref, start, left_out)
    put_tiles(left_ref, start, left_out + left_in)
    put_tiles(sides_out_ref, start, sides_out)
    put_tiles(sides_ref, start, sides_out + left_in + pltpu.roll(two, WIDE - 1, 1))


NEAR, BEYOND = range(1, INNER + 1), range(INNER + 1, OUTER + 1)


def box_sums(out_ref, in_ref, at, signs):
    def rows(ref, shift):
        return jnp.concatenate([ref[t, at + shift : at + shift + 8, :] for t in range(SPAN // LANE)], axis=1)

    return sum([rows(out_ref, s * a) for a in NEAR for s in signs] + [rows(in_ref, s * a) for a in BEYOND for s in signs])


def inverse_root(count):
    k = jnp.maximum(count, 1.0)
    q = lax.rsqrt(k)
    return k, q * (1.5 - 0.5 * k * q * q)


def root_of(sums, weight, start, tile, counts, k, q):
    value = jnp.where(weight > 0, jnp.maximum(sums, 0.0) * weight, MASKED)
    value = straight(value, start, tile)
    positive = value > 0.0
    root = jnp.exp(jnp.log(jnp.where(positive, value, 1.0) * (q * q)) * (1.0 / 3.0))
    root = jnp.where(positive, root * (k * q * (3.0 / 2.0**0.5)), 0.0)
    distance = lax.broadcasted_iota(jnp.int32, (8, BAND), 1)
    return jnp.where((counts > 0) & (distance >= 2 * OUTER) & (value >= 0.0), root, MASKED)


def window_kernel(core_ref, final_ref, counts_ref, swap_ref, cross_ref, vectors_ref,
                  donut_ref, lower_ref, own_ref, left_out_ref, left_ref, sides_out_ref, sides_ref, float_ref):
    core = core_ref[0]
    ahead, bias_ahead = vectors_ref[0:1, :], vectors_ref[1:2, :]
    bias_row = bias_ahead[:, :ROWS]
    own_ref[0:1, :] = jnp.concatenate([vectors_ref[2:3, :ROWS], ahead[:, : BAND - ROWS]], axis=1)
    tables = (left_out_ref, left_ref, sides_out_ref, sides_ref)
    swap, cross = swap_ref[...], cross_ref[...]
    before = jnp.where(core == 0, cross, swap)
    after = jnp.where(core == 0, swap, cross)
    gap = jnp.zeros((EDGE, LANE), F32)
    put_tables(tables, 0, jnp.concatenate([before[:, ROWS:], gap, before[:, :ROWS]], axis=1))
    put_tables(tables, ROWS + EDGE, jnp.concatenate([gap] * SLAB + [after[:, : WIDE - ROWS]], axis=1))

    for start in range(0, ROWS, 8):
        put_tables(tables, start + EDGE, jnp.concatenate([final_ref[start : start + 8, :], gap], axis=1))

    for start in range(0, ROWS, STEP):
        here = slice(start, start + STEP)
        float_ref[here, :] = counts_ref[here, :].astype(jnp.int32).astype(F32)

    for i in range(SLAB):
        begin = i * LANE
        views = [ref.at[:, pl.ds(begin, LANE + 2 * EDGE), :] for ref in tables]
        for start in range(0, LANE, 8):
            here = pl.ds(begin + start, 8)
            weight = column_of(bias_row, begin + start, 8) * bias_ahead
            counts = float_ref[here, :]
            k, q = inverse_root(counts)
            donut = box_sums(views[2], views[3], start + EDGE, (1, -1))
            donut_ref[here, :BAND] = root_of(donut, weight, start, i, counts, k, q)
            lower = box_sums(views[0], views[1], start + EDGE, (1,))
            lower_ref[here, :] = root_of(lower, weight, start, i, counts, k, q)


def half_erfc(x):
    size = jnp.abs(x)
    t = 1.0 / (1.0 + 0.5 * size)
    poly = 0.17087277
    for c in (-0.82215223, 1.48851587, -1.13520398, 0.27886807, -0.18628806, 0.09678418, 0.37409196, 1.00002368, -1.26551223):
        poly = poly * t + c
    tail = 0.5 * t * jnp.exp(poly - size * size)
    return jnp.where(x >= 0.0, tail, 1.0 - tail)


def filter_sums(expected):
    lane = lax.broadcasted_iota(jnp.int32, expected.shape, 1)
    none = jnp.zeros((1, LANE), F32)
    after = jnp.concatenate([expected[1:], none], axis=0)
    before = jnp.concatenate([none, expected[:-1]], axis=0)
    donut_weight, lower_weight = {}, {}
    for a in range(-OUTER, OUTER + 1):
        for c in range(-OUTER, OUTER + 1):
            if a and c and not (abs(a) <= INNER and abs(c) <= INNER):
                donut_weight[c - a] = donut_weight.get(c - a, 0) + 1
            if a >= 1 and c <= -1 and not (a <= INNER and c >= -INNER):
                lower_weight[c - a] = lower_weight.get(c - a, 0) + 1
    donut = lower = None
    for k in range(-2 * OUTER, 2 * OUTER + 1):
        moved = expected
        if k:
            turn = (-k) % LANE
            here = (lane + k < LANE) if k > 0 else (lane + k >= 0)
            moved = jnp.where(here, pltpu.roll(expected, turn, 1), pltpu.roll(after if k > 0 else before, turn, 1))
        if k in donut_weight:
            part = moved * float(donut_weight[k])
            donut = part if donut is None else donut + part
        if k in lower_weight:
            part = moved * float(lower_weight[k])
            lower = part if lower is None else lower + part
    return donut, lower


def cube_root(value):
    positive = value > 0.0
    root = jnp.exp(jnp.log(jnp.where(positive, value, 1.0)) * (1.0 / 3.0))
    return jnp.where(positive, root, value)


def tiled(row):
    return jnp.concatenate([row[:, t : t + LANE] for t in range(0, row.shape[1], LANE)], axis=0)


def tail_kernel(sums_ref, own_ref, donut_ref, lower_ref, counts_ref, pvalue_donut_ref, pvalue_lower_ref, bias_ref,
                ratio_ref):
    @pl.when(pl.program_id(0) == 0)
    def _():
        total = sums_ref[0]
        for n in range(1, sums_ref.shape[0]):
            total = total + sums_ref[n]
        pairs = tiled(total[:, BAND : 2 * BAND])
        expected = tiled(total[:, :BAND]) / pairs
        donut_exp, lower_exp = filter_sums(expected)
        ratio_ref[0:1, :] = lanes(cube_root(expected / donut_exp))
        ratio_ref[1:2, :] = lanes(cube_root(expected / lower_exp))
        mapped_count = pairs[0:1, 0:1]
        half = LANE // 2
        first = total[:, 2 * BAND : 2 * BAND + 1] / mapped_count
        second = total[:, 2 * BAND + half : 2 * BAND + half + 1] / mapped_count
        own = own_ref[0:1, :]
        put_lanes(bias_ref, 0, jnp.where(own[:, ROWS : 2 * ROWS] > 0, own[:, :ROWS] / first / second, 1.0))

    for start in range(0, pvalue_donut_ref.shape[0], STEP):
        here = slice(start, start + STEP)
        k, q = inverse_root(counts_ref[here, :].astype(jnp.int32).astype(F32))
        base = q * (k * (3.0 / 2.0**0.5) - 1.0 / (3.0 * 2.0**0.5))
        for at, root_ref, out_ref in ((0, donut_ref, pvalue_donut_ref), (1, lower_ref, pvalue_lower_ref)):
            root = root_ref[here, :]
            value = half_erfc(base - root * ratio_ref[at : at + 1, :])
            out_ref[here, :] = jnp.where(root < 0.0, 1.0, value)


def params(mib=8):
    return pltpu.CompilerParams(vmem_limit_bytes=mib * 2**20)


def cost(flops, moved):
    return pl.CostEstimate(flops=flops, bytes_accessed=moved, transcendentals=0)


def call(kernel, ins, outs, specs=None, **more):
    return pl.pallas_call(
        kernel,
        out_shape=[jax.ShapeDtypeStruct(s, F32) for s in outs],
        in_specs=specs or [VMEM] * len(ins),
        out_specs=[VMEM] * len(outs),
        compiler_params=params(),
        **more,
    )(*ins)


def begin(contacts, mapped):
    shapes = [((ROWS, SPAN), F32), ((MESSAGE, LANE), F32), ((ROWS, BAND), jnp.int16)]
    return pl.pallas_call(
        begin_kernel,
        out_shape=[jax.ShapeDtypeStruct(*s) for s in shapes],
        in_specs=[VMEM] * 2,
        out_specs=[VMEM] * 3,
        compiler_params=params(),
    )(contacts, mapped)


def middle(core, skewed, pair, near, far):
    return call(middle_kernel, (core, skewed, pair, near, far), [(MESSAGE, LANE)], [SMEM] + [VMEM] * 4)[0]


def last(core, skewed, pair, near, far):
    return call(last_kernel, (core, skewed, pair, near, far), [(8, LANE)], [SMEM] + [VMEM] * 4)[0]


def pair_counts(core, pair, near, far):
    return call(
        pairs_kernel, (core, pair, near, far), [(1, BAND)], [SMEM] + [VMEM] * 3, cost_estimate=cost(10**6, 2**16)
    )[0]


def final_band(core, skewed, pair, ahead, own, pairs, copies):
    return call(
        band_kernel,
        (core, skewed, pair, ahead, own, pairs),
        [(ROWS, SPAN), (EDGE, SPAN), (EDGE, SPAN), (copies, 1, 2 * BAND + LANE), (8, SPAN)],
        [SMEM] + [VMEM] * 5,
    )


def windows(core, final, counts, swap, cross, vectors):
    return pl.pallas_call(
        window_kernel,
        out_shape=[jax.ShapeDtypeStruct(s, F32) for s in ((ROWS, SPAN), (ROWS, BAND), (8, BAND))],
        in_specs=[SMEM] + [VMEM] * 5,
        out_specs=[VMEM] * 3,
        scratch_shapes=[pltpu.VMEM((WIDE // LANE, ROWS + 2 * EDGE, LANE), F32)] * 4 + [pltpu.VMEM((ROWS, BAND), F32)],
        input_output_aliases={1: 0},
        compiler_params=params(16),
        cost_estimate=cost(2 * 10**7, 6 * 2**20),
    )(core, final, counts, swap, cross, vectors)


def whole(shape):
    return pl.BlockSpec(shape, lambda i: (0,) * len(shape))


def tails(sums, own, donut, lower, counts, rows=64):
    block = pl.BlockSpec((rows, BAND), lambda i: (i, 0))
    return pl.pallas_call(
        tail_kernel,
        grid=(ROWS // rows,),
        out_shape=[jax.ShapeDtypeStruct((ROWS, BAND), F32)] * 2 + [jax.ShapeDtypeStruct((SLAB, LANE), F32)],
        in_specs=[whole(sums.shape), whole(own.shape)] + [block] * 3,
        out_specs=[block] * 2 + [whole((SLAB, LANE))],
        scratch_shapes=[pltpu.VMEM((8, BAND), F32)],
        compiler_params=params(),
    )(sums, own, donut, lower, counts)


def solution(mesh):
    size = mesh.shape["genome"]
    plane = min(32, size)
    chips = [[i, i + 1] for i in range(0, size, 2)]
    planes = [[start + i for i in range(plane)] for start in range(0, size, plane)]
    lines = [[i + start for start in range(0, size, plane)] for i in range(plane)]

    def both_cores(value):
        return lax.all_gather(value, "genome", axis_index_groups=chips)

    def moved(value, target):
        pairs = [(i, target(i)) for i in range(size)]
        return lax.ppermute(value, "genome", [(i, t) for i, t in pairs if 0 <= t < size])

    def around(message):
        pair = both_cores(message)
        near = moved(pair, lambda i: i + 2 if i % 2 == 0 else i - 2)
        far = moved(pair, lambda i: i + 4 if i % 2 == 0 else i - 4)
        return pair, both_cores(near), both_cores(far)

    def shards(contacts, mappable):
        core = lax.rem(lax.axis_index("genome"), 2).astype(jnp.int32).reshape(1)
        mapped = mappable.reshape(SLAB, LANE)
        skewed, message, counts = begin(contacts, mapped)
        exchanged = around(message)
        pairs = pair_counts(core, *exchanged)
        message = middle(core, skewed, *exchanged)
        own = last(core, skewed, *around(message))
        pair = both_cores(own)
        ahead = both_cores(moved(pair, lambda i: i - 2 if i % 2 == 0 else i - 4))
        final, swap, cross, sums, vectors = final_band(core, skewed, pair, ahead, own, pairs, plane)
        cross = moved(cross, lambda i: i - 1 if i % 2 == 0 else i + 1)
        swap = moved(swap, lambda i: i ^ 1)
        sums = lax.all_to_all(sums, "genome", 0, 0, axis_index_groups=planes)
        sums, swap, cross = lax.optimization_barrier((sums, swap, cross))
        sums = jnp.broadcast_to(jnp.sum(sums, axis=0, keepdims=True), (size // plane,) + sums.shape[1:])
        sums = lax.all_to_all(sums, "genome", 0, 0, axis_index_groups=lines)
        donut, lower, own = windows(core, final, counts, swap, cross, vectors)
        pvalue_donut, pvalue_lower, bias = tails(sums, own, donut, lower, counts)
        return pvalue_donut, pvalue_lower, bias.reshape(ROWS)

    placed = (P("genome", None), P("genome"))
    return jax.shard_map(
        shards,
        mesh=mesh,
        in_specs=placed,
        out_specs=(P("genome", None), P("genome", None), P("genome")),
        check_vma=False,
    )
```

```python
import jax
import jax.numpy as jnp
from jax import lax
from jax.experimental import pallas as pl
from jax.experimental.pallas import tpu as pltpu
from jax.sharding import PartitionSpec as P

OUTER = 5
INNER = 2
ROWS = 256
BAND = 1024
LANE = 128
SLAB = ROWS // LANE
HOPS = BAND // ROWS
SPAN = ROWS + BAND
HALF = BAND + LANE
WIDE = SPAN + LANE
STEP = 32
EDGE = 8
MASKED = -1.0
TABLE_STEP = 32
VMEM = pl.BlockSpec(memory_space=pltpu.VMEM)
SMEM = pl.BlockSpec(memory_space=pltpu.SMEM)
F32 = jnp.float32
X_AT, SPREAD_AT, SUMS_AT, MAPPED_AT, MESSAGE = 0, SLAB, SLAB * (HOPS + 2), SLAB * (HOPS + 3), 16


def lanes(tiles):
    return jnp.concatenate([tiles[r : r + 1] for r in range(tiles.shape[0])], axis=1)


def put_lanes(ref, first, row):
    for t in range(row.shape[1] // LANE):
        ref[first + t : first + t + 1, :] = row[:, t * LANE : (t + 1) * LANE]


def on_diagonal(start, count, width):
    rows = lax.broadcasted_iota(jnp.int32, (count, width), 0) + start
    return rows == lax.broadcasted_iota(jnp.int32, (count, width), 1)


def column_of(row, start, count):
    part = jnp.where(on_diagonal(start, count, ROWS), row, 0.0)
    return jnp.sum(part, axis=1, keepdims=True)


def fold(value):
    total = value[0:8]
    for r in range(8, value.shape[0], 8):
        total = total + value[r : r + 8]
    return total


def spread_part(rows, weight_row, start):
    part = rows * column_of(weight_row, start, STEP)
    return fold(jnp.where(on_diagonal(start, STEP, SPAN), 0.0, part))


def spread_of(skewed_ref, weight_row):
    total = jnp.zeros((8, SPAN), F32)
    for start in range(0, ROWS, STEP):
        total = total + spread_part(skewed_ref[start : start + STEP, :], weight_row, start)
    return jnp.sum(total, axis=0, keepdims=True)


def own_sums(skewed_ref, ahead_row):
    total = jnp.zeros((8, ROWS), F32)
    for start in range(0, ROWS, STEP):
        part = skewed_ref[start : start + STEP, :] * ahead_row
        sums = jnp.sum(part, axis=1, keepdims=True)
        total = total + fold(jnp.where(on_diagonal(start, STEP, ROWS), sums, 0.0))
    return jnp.sum(total, axis=0, keepdims=True)


def put_message(out_ref, x_row, spread_row, sums_row, mapped_row):
    put_lanes(out_ref, X_AT, x_row)
    put_lanes(out_ref, SPREAD_AT, spread_row)
    put_lanes(out_ref, SUMS_AT, sums_row)
    put_lanes(out_ref, MAPPED_AT, mapped_row)


def begin_kernel(contacts_ref, mapped_ref, skewed_ref, out_ref, counts_ref):
    for start in range(0, ROWS, STEP):
        counts = contacts_ref[start : start + STEP, :]
        counts_ref[start : start + STEP, :] = counts.astype(jnp.int16)
        counts = counts.astype(F32)
        padded = jnp.concatenate([counts, jnp.zeros((STEP, SPAN - BAND), F32)], axis=1)
        skewed_ref[start : start + STEP, :] = pltpu.roll(padded, start, 1, stride=1, stride_axis=0)
    mapped = lanes(mapped_ref[...]).astype(F32)
    put_message(out_ref, mapped, spread_of(skewed_ref, mapped), jnp.zeros((1, ROWS), F32), mapped)


def ahead_of(core, slabs):
    tiles = [jnp.where(core == 0, slabs[k], slabs[k + 1]) for k in range(HOPS + 1)]
    return jnp.concatenate([lanes(t) for t in tiles], axis=1)


def sum_rows(core_ref, skewed_ref, pair_ref, near_ref, far_ref):
    core = core_ref[0]

    def message(k):
        at = k % 2
        chip = k // 2
        if chip == 0:
            return pair_ref.at[at]
        ref = near_ref if abs(chip) == 1 else far_ref
        return ref.at[1 if chip > 0 else 0, at]

    x_tiles = [message(k)[X_AT : X_AT + SLAB, :] for k in range(HOPS + 2)]
    arrived = jnp.zeros((SLAB, LANE), F32)
    for k in range(HOPS + 1):
        at = SPREAD_AT + SLAB * k
        arrived = arrived + jnp.where(
            core == 0, message(-k)[at : at + SLAB, :], message(1 - k)[at : at + SLAB, :]
        )
    sums = own_sums(skewed_ref, ahead_of(core, x_tiles)) + lanes(arrived)
    x_row = lanes(jnp.where(core == 0, x_tiles[0], x_tiles[1]))
    mapped = jnp.where(core == 0, pair_ref[0, MAPPED_AT : MAPPED_AT + SLAB, :], pair_ref[1, MAPPED_AT : MAPPED_AT + SLAB, :])
    return lanes(mapped), x_row * sums


def middle_kernel(core_ref, skewed_ref, pair_ref, near_ref, far_ref, out_ref):
    mapped, sums = sum_rows(core_ref, skewed_ref, pair_ref, near_ref, far_ref)
    x_row = jnp.where(mapped > 0, 1.0 / jnp.where(mapped > 0, sums, 1.0), 0.0)
    put_message(out_ref, x_row, spread_of(skewed_ref, x_row), sums, mapped)


def last_kernel(core_ref, skewed_ref, pair_ref, near_ref, far_ref, out_ref):
    mapped, sums = sum_rows(core_ref, skewed_ref, pair_ref, near_ref, far_ref)
    before = jnp.where(core_ref[0] == 0, pair_ref[0], pair_ref[1])
    before = lanes(before[SUMS_AT : SUMS_AT + SLAB])
    bias = jnp.where(mapped > 0, before * sums, 1.0)
    out_ref[...] = jnp.zeros((8, LANE), F32)
    put_lanes(out_ref, 0, jnp.where(mapped > 0, 1.0 / bias, 0.0))
    put_lanes(out_ref, SLAB, bias)
    for at, value in ((4, before), (5, sums)):
        total = jnp.sum(jnp.where(mapped > 0, value, 0.0), axis=1, keepdims=True)
        out_ref[at : at + 1, :] = jnp.broadcast_to(total, (1, LANE))


def flipped(rows):
    order = 7 - lax.broadcasted_iota(jnp.int32, (8, LANE), 0)
    tiles = [jnp.take_along_axis(rows[:, t : t + LANE], order, axis=0, mode="promise_in_bounds") for t in range(0, rows.shape[1], LANE)]
    return jnp.concatenate(tiles, axis=1)


def along_diagonals(rows_of, width):
    total = None
    for g in range(LANE // 8):
        part = None
        for h in range(SLAB):
            rows = rows_of(h * LANE + 8 * g)
            rows = rows[:, h * LANE : h * LANE + SPAN - LANE]
            part = rows if part is None else part + rows
        if g:
            part = pltpu.roll(part, SPAN - LANE - 8 * g, 1)
        total = part if total is None else total + part
    total = pltpu.roll(flipped(total), SPAN - LANE - 7, 1, stride=1, stride_axis=0)
    return jnp.sum(total[:, :width], axis=0, keepdims=True)


def pairs_kernel(core_ref, pair_ref, near_ref, far_ref, out_ref):
    refs = [pair_ref.at[0], pair_ref.at[1], near_ref.at[1, 0], near_ref.at[1, 1], far_ref.at[1, 0], far_ref.at[1, 1]]
    ahead = ahead_of(core_ref[0], [r[MAPPED_AT : MAPPED_AT + SLAB, :] for r in refs])
    row = ahead[:, :ROWS]
    out_ref[...] = along_diagonals(lambda r: column_of(row, r, 8) * ahead, BAND)


def band_kernel(core_ref, skewed_ref, pair_ref, ahead_ref, own_ref, pairs_ref,
                final_ref, swap_ref, cross_ref, sums_ref, vectors_ref):
    core = core_ref[0]
    slabs = [pair_ref[0], pair_ref[1], ahead_ref[0, 0], ahead_ref[0, 1], ahead_ref[1, 0], ahead_ref[1, 1]]
    ahead = ahead_of(core, [s[X_AT : X_AT + SLAB] for s in slabs])
    x_row = ahead[:, :ROWS]
    for start in range(0, ROWS, STEP):
        final_ref[start : start + STEP, :] = (
            skewed_ref[start : start + STEP, :] * column_of(x_row, start, STEP) * ahead
        )
    first, last = final_ref[0:EDGE, :], final_ref[ROWS - EDGE : ROWS, :]
    swap_ref[...] = jnp.where(core == 0, last, first)
    cross_ref[...] = jnp.where(core == 0, first, last)
    diagonals = along_diagonals(lambda r: final_ref[r : r + 8, :], BAND)
    own = own_ref[...]
    row = jnp.concatenate([diagonals, pairs_ref[...], own[4:5], own[5:6]], axis=1)
    for n in range(sums_ref.shape[0]):
        sums_ref[n] = row[:, :HALF] if n % 2 == 0 else row[:, HALF:]
    vectors_ref[0:1, :] = ahead
    vectors_ref[1:2, :] = jnp.where(ahead > 0, 1.0 / jnp.where(ahead > 0, ahead, 1.0), 0.0)
    vectors_ref[2:3, :] = jnp.concatenate([lanes(own[SLAB : 2 * SLAB]), jnp.zeros((1, SPAN - ROWS), F32)], axis=1)


def straight(rows, start, tile):
    rows = pltpu.roll(flipped(rows), SPAN - 7 - start, 1, stride=1, stride_axis=0)
    return flipped(rows[:, tile * LANE : tile * LANE + BAND])


def put_tiles(ref, start, value):
    for t in range(value.shape[1] // LANE):
        ref[t, pl.ds(start, value.shape[0]), :] = value[:, t * LANE : (t + 1) * LANE]


def put_tables(refs, start, cells):
    left_out_ref, left_ref, sides_out_ref, sides_ref = refs
    two = cells + pltpu.roll(cells, WIDE - 1, 1)
    three = two + pltpu.roll(cells, WIDE - 2, 1)
    left_out = pltpu.roll(three, 5, 1)
    left_in = pltpu.roll(two, 2, 1)
    sides_out = left_out + pltpu.roll(three, WIDE - 3, 1)
    put_tiles(left_out_ref, start, left_out)
    put_tiles(left_ref, start, left_out + left_in)
    put_tiles(sides_out_ref, start, sides_out)
    put_tiles(sides_ref, start, sides_out + left_in + pltpu.roll(two, WIDE - 1, 1))


NEAR, BEYOND = range(1, INNER + 1), range(INNER + 1, OUTER + 1)


def box_sums(out_ref, in_ref, at, signs):
    def rows(ref, shift):
        return jnp.concatenate([ref[t, at + shift : at + shift + 8, :] for t in range(SPAN // LANE)], axis=1)

    return sum([rows(out_ref, s * a) for a in NEAR for s in signs] + [rows(in_ref, s * a) for a in BEYOND for s in signs])


def inverse_root(count):
    k = jnp.maximum(count, 1.0)
    q = lax.rsqrt(k)
    return k, q * (1.5 - 0.5 * k * q * q)


def root_of(sums, weight, start, tile, counts, k, q):
    value = jnp.where(weight > 0, jnp.maximum(sums, 0.0) * weight, MASKED)
    value = straight(value, start, tile)
    positive = value > 0.0
    root = jnp.exp(jnp.log(jnp.where(positive, value, 1.0) * (q * q)) * (1.0 / 3.0))
    root = jnp.where(positive, root * (k * q * (3.0 / 2.0**0.5)), 0.0)
    distance = lax.broadcasted_iota(jnp.int32, (8, BAND), 1)
    return jnp.where((counts > 0) & (distance >= 2 * OUTER) & (value >= 0.0), root, MASKED)


def window_kernel(core_ref, final_ref, counts_ref, swap_ref, cross_ref, vectors_ref,
                  donut_ref, lower_ref, own_ref, left_out_ref, left_ref, sides_out_ref, sides_ref, float_ref):
    core = core_ref[0]
    ahead, bias_ahead = vectors_ref[0:1, :], vectors_ref[1:2, :]
    bias_row = bias_ahead[:, :ROWS]
    own_ref[0:1, :] = jnp.concatenate([vectors_ref[2:3, :ROWS], ahead[:, : BAND - ROWS]], axis=1)
    tables = (left_out_ref, left_ref, sides_out_ref, sides_ref)
    swap, cross = swap_ref[...], cross_ref[...]
    before = jnp.where(core == 0, cross, swap)
    after = jnp.where(core == 0, swap, cross)
    gap = jnp.zeros((EDGE, LANE), F32)
    put_tables(tables, 0, jnp.concatenate([before[:, ROWS:], gap, before[:, :ROWS]], axis=1))
    put_tables(tables, ROWS + EDGE, jnp.concatenate([gap] * SLAB + [after[:, : WIDE - ROWS]], axis=1))

    for start in range(0, ROWS, 8):
        put_tables(tables, start + EDGE, jnp.concatenate([final_ref[start : start + 8, :], gap], axis=1))

    for start in range(0, ROWS, STEP):
        here = slice(start, start + STEP)
        float_ref[here, :] = counts_ref[here, :].astype(jnp.int32).astype(F32)

    for i in range(SLAB):
        begin = i * LANE
        views = [ref.at[:, pl.ds(begin, LANE + 2 * EDGE), :] for ref in tables]
        for start in range(0, LANE, 8):
            here = pl.ds(begin + start, 8)
            weight = column_of(bias_row, begin + start, 8) * bias_ahead
            counts = float_ref[here, :]
            k, q = inverse_root(counts)
            donut = box_sums(views[2], views[3], start + EDGE, (1, -1))
            donut_ref[here, :BAND] = root_of(donut, weight, start, i, counts, k, q)
            lower = box_sums(views[0], views[1], start + EDGE, (1,))
            lower_ref[here, :] = root_of(lower, weight, start, i, counts, k, q)


def half_erfc(x):
    size = jnp.abs(x)
    t = 1.0 / (1.0 + 0.5 * size)
    poly = 0.17087277
    for c in (-0.82215223, 1.48851587, -1.13520398, 0.27886807, -0.18628806, 0.09678418, 0.37409196, 1.00002368, -1.26551223):
        poly = poly * t + c
    tail = 0.5 * t * jnp.exp(poly - size * size)
    return jnp.where(x >= 0.0, tail, 1.0 - tail)


def filter_sums(expected):
    lane = lax.broadcasted_iota(jnp.int32, expected.shape, 1)
    none = jnp.zeros((1, LANE), F32)
    after = jnp.concatenate([expected[1:], none], axis=0)
    before = jnp.concatenate([none, expected[:-1]], axis=0)
    donut_weight, lower_weight = {}, {}
    for a in range(-OUTER, OUTER + 1):
        for c in range(-OUTER, OUTER + 1):
            if a and c and not (abs(a) <= INNER and abs(c) <= INNER):
                donut_weight[c - a] = donut_weight.get(c - a, 0) + 1
            if a >= 1 and c <= -1 and not (a <= INNER and c >= -INNER):
                lower_weight[c - a] = lower_weight.get(c - a, 0) + 1
    donut = lower = None
    for k in range(-2 * OUTER, 2 * OUTER + 1):
        moved = expected
        if k:
            turn = (-k) % LANE
            here = (lane + k < LANE) if k > 0 else (lane + k >= 0)
            moved = jnp.where(here, pltpu.roll(expected, turn, 1), pltpu.roll(after if k > 0 else before, turn, 1))
        if k in donut_weight:
            part = moved * float(donut_weight[k])
            donut = part if donut is None else donut + part
        if k in lower_weight:
            part = moved * float(lower_weight[k])
            lower = part if lower is None else lower + part
    return donut, lower


def cube_root(value):
    positive = value > 0.0
    root = jnp.exp(jnp.log(jnp.where(positive, value, 1.0)) * (1.0 / 3.0))
    return jnp.where(positive, root, value)


def tiled(row):
    return jnp.concatenate([row[:, t : t + LANE] for t in range(0, row.shape[1], LANE)], axis=0)


def tail_kernel(sums_ref, own_ref, donut_ref, lower_ref, counts_ref, pvalue_donut_ref, pvalue_lower_ref, bias_ref,
                ratio_ref):
    @pl.when(pl.program_id(0) == 0)
    def _():
        total = jnp.concatenate([sum(sums_ref[core, n] for n in range(sums_ref.shape[1])) for core in range(2)], axis=1)
        pairs = tiled(total[:, BAND : 2 * BAND])
        expected = tiled(total[:, :BAND]) / pairs
        donut_exp, lower_exp = filter_sums(expected)
        ratio_ref[0:1, :] = lanes(cube_root(expected / donut_exp))
        ratio_ref[1:2, :] = lanes(cube_root(expected / lower_exp))
        mapped_count = pairs[0:1, 0:1]
        first = total[:, 2 * BAND : 2 * BAND + 1] / mapped_count
        second = total[:, 2 * BAND + LANE : 2 * BAND + LANE + 1] / mapped_count
        own = own_ref[0:1, :]
        put_lanes(bias_ref, 0, jnp.where(own[:, ROWS : 2 * ROWS] > 0, own[:, :ROWS] / first / second, 1.0))

    for start in range(0, pvalue_donut_ref.shape[0], STEP):
        here = slice(start, start + STEP)
        k, q = inverse_root(counts_ref[here, :].astype(jnp.int32).astype(F32))
        base = q * (k * (3.0 / 2.0**0.5) - 1.0 / (3.0 * 2.0**0.5))
        for at, root_ref, out_ref in ((0, donut_ref, pvalue_donut_ref), (1, lower_ref, pvalue_lower_ref)):
            root = root_ref[here, :]
            value = half_erfc(base - root * ratio_ref[at : at + 1, :])
            out_ref[here, :] = jnp.where(root < 0.0, 1.0, value)


def params(mib=8):
    return pltpu.CompilerParams(vmem_limit_bytes=mib * 2**20)


def cost(flops, moved):
    return pl.CostEstimate(flops=flops, bytes_accessed=moved, transcendentals=0)


def call(kernel, ins, outs, specs=None, **more):
    return pl.pallas_call(
        kernel,
        out_shape=[jax.ShapeDtypeStruct(s, F32) for s in outs],
        in_specs=specs or [VMEM] * len(ins),
        out_specs=[VMEM] * len(outs),
        compiler_params=params(),
        **more,
    )(*ins)


def begin(contacts, mapped):
    shapes = [((ROWS, SPAN), F32), ((MESSAGE, LANE), F32), ((ROWS, BAND), jnp.int16)]
    return pl.pallas_call(
        begin_kernel,
        out_shape=[jax.ShapeDtypeStruct(*s) for s in shapes],
        in_specs=[VMEM] * 2,
        out_specs=[VMEM] * 3,
        compiler_params=params(),
    )(contacts, mapped)


def middle(core, skewed, pair, near, far):
    return call(middle_kernel, (core, skewed, pair, near, far), [(MESSAGE, LANE)], [SMEM] + [VMEM] * 4)[0]


def last(core, skewed, pair, near, far):
    return call(last_kernel, (core, skewed, pair, near, far), [(8, LANE)], [SMEM] + [VMEM] * 4)[0]


def pair_counts(core, pair, near, far):
    return call(
        pairs_kernel, (core, pair, near, far), [(1, BAND)], [SMEM] + [VMEM] * 3, cost_estimate=cost(10**6, 2**16)
    )[0]


def final_band(core, skewed, pair, ahead, own, pairs, copies):
    return call(
        band_kernel,
        (core, skewed, pair, ahead, own, pairs),
        [(ROWS, SPAN), (EDGE, SPAN), (EDGE, SPAN), (copies, 1, HALF), (8, SPAN)],
        [SMEM] + [VMEM] * 5,
    )


def windows(core, final, counts, swap, cross, vectors):
    return pl.pallas_call(
        window_kernel,
        out_shape=[jax.ShapeDtypeStruct(s, F32) for s in ((ROWS, SPAN), (ROWS, BAND), (8, BAND))],
        in_specs=[SMEM] + [VMEM] * 5,
        out_specs=[VMEM] * 3,
        scratch_shapes=[pltpu.VMEM((WIDE // LANE, ROWS + 2 * EDGE, LANE), F32)] * 4 + [pltpu.VMEM((ROWS, BAND), F32)],
        input_output_aliases={1: 0},
        compiler_params=params(16),
        cost_estimate=cost(2 * 10**7, 6 * 2**20),
    )(core, final, counts, swap, cross, vectors)


def whole(shape):
    return pl.BlockSpec(shape, lambda i: (0,) * len(shape))


def tails(sums, own, donut, lower, counts, rows=64):
    block = pl.BlockSpec((rows, BAND), lambda i: (i, 0))
    return pl.pallas_call(
        tail_kernel,
        grid=(ROWS // rows,),
        out_shape=[jax.ShapeDtypeStruct((ROWS, BAND), F32)] * 2 + [jax.ShapeDtypeStruct((SLAB, LANE), F32)],
        in_specs=[whole(sums.shape), whole(own.shape)] + [block] * 3,
        out_specs=[block] * 2 + [whole((SLAB, LANE))],
        scratch_shapes=[pltpu.VMEM((8, BAND), F32)],
        compiler_params=params(),
    )(sums, own, donut, lower, counts)


def solution(mesh):
    size = mesh.shape["genome"]
    plane = min(32, size)
    chips = [[i, i + 1] for i in range(0, size, 2)]
    planes = [[start + i for i in range(plane)] for start in range(0, size, plane)]
    lines = [[i + start for start in range(0, size, plane)] for i in range(plane)]

    def both_cores(value):
        return lax.all_gather(value, "genome", axis_index_groups=chips)

    def moved(value, target):
        pairs = [(i, target(i)) for i in range(size)]
        return lax.ppermute(value, "genome", [(i, t) for i, t in pairs if 0 <= t < size])

    def around(message):
        pair = both_cores(message)
        near = moved(pair, lambda i: i + 2 if i % 2 == 0 else i - 2)
        far = moved(pair, lambda i: i + 4 if i % 2 == 0 else i - 4)
        return pair, both_cores(near), both_cores(far)

    def shards(contacts, mappable):
        core = lax.rem(lax.axis_index("genome"), 2).astype(jnp.int32).reshape(1)
        mapped = mappable.reshape(SLAB, LANE)
        skewed, message, counts = begin(contacts, mapped)
        exchanged = around(message)
        pairs = pair_counts(core, *exchanged)
        message = middle(core, skewed, *exchanged)
        own = last(core, skewed, *around(message))
        pair = both_cores(own)
        ahead = both_cores(moved(pair, lambda i: i - 2 if i % 2 == 0 else i - 4))
        final, swap, cross, sums, vectors = final_band(core, skewed, pair, ahead, own, pairs, plane)
        cross = moved(cross, lambda i: i - 1 if i % 2 == 0 else i + 1)
        swap = moved(swap, lambda i: i ^ 1)
        sums = lax.all_to_all(sums, "genome", 0, 0, axis_index_groups=planes)
        sums, swap, cross = lax.optimization_barrier((sums, swap, cross))
        sums = jnp.broadcast_to(jnp.sum(sums, axis=0, keepdims=True), (size // plane,) + sums.shape[1:])
        sums = lax.all_to_all(sums, "genome", 0, 0, axis_index_groups=lines)
        donut, lower, own = windows(core, final, counts, swap, cross, vectors)
        pvalue_donut, pvalue_lower, bias = tails(both_cores(sums), own, donut, lower, counts)
        return pvalue_donut, pvalue_lower, bias.reshape(ROWS)

    placed = (P("genome", None), P("genome"))
    return jax.shard_map(
        shards,
        mesh=mesh,
        in_specs=placed,
        out_specs=(P("genome", None), P("genome", None), P("genome")),
        check_vma=False,
    )
```

```python
import jax
import jax.numpy as jnp
from jax import lax
from jax.experimental import pallas as pl
from jax.experimental.pallas import tpu as pltpu
from jax.sharding import PartitionSpec as P

OUTER = 5
INNER = 2
ROWS = 256
BAND = 1024
LANE = 128
SLAB = ROWS // LANE
HOPS = BAND // ROWS
SPAN = ROWS + BAND
WIDE = SPAN + LANE
STEP = 32
EDGE = 8
MASKED = -1.0
TABLE_STEP = 32
VMEM = pl.BlockSpec(memory_space=pltpu.VMEM)
SMEM = pl.BlockSpec(memory_space=pltpu.SMEM)
F32 = jnp.float32
X_AT, SPREAD_AT, SUMS_AT, MAPPED_AT, MESSAGE = 0, SLAB, SLAB * (HOPS + 2), SLAB * (HOPS + 3), 16


def lanes(tiles):
    return jnp.concatenate([tiles[r : r + 1] for r in range(tiles.shape[0])], axis=1)


def put_lanes(ref, first, row):
    for t in range(row.shape[1] // LANE):
        ref[first + t : first + t + 1, :] = row[:, t * LANE : (t + 1) * LANE]


def on_diagonal(start, count, width):
    rows = lax.broadcasted_iota(jnp.int32, (count, width), 0) + start
    return rows == lax.broadcasted_iota(jnp.int32, (count, width), 1)


def column_of(row, start, count):
    part = jnp.where(on_diagonal(start, count, ROWS), row, 0.0)
    return jnp.sum(part, axis=1, keepdims=True)


def fold(value):
    total = value[0:8]
    for r in range(8, value.shape[0], 8):
        total = total + value[r : r + 8]
    return total


def spread_part(rows, weight_row, start):
    part = rows * column_of(weight_row, start, STEP)
    return fold(jnp.where(on_diagonal(start, STEP, SPAN), 0.0, part))


def spread_of(skewed_ref, weight_row):
    total = jnp.zeros((8, SPAN), F32)
    for start in range(0, ROWS, STEP):
        total = total + spread_part(skewed_ref[start : start + STEP, :], weight_row, start)
    return jnp.sum(total, axis=0, keepdims=True)


def own_sums(skewed_ref, ahead_row):
    total = jnp.zeros((8, ROWS), F32)
    for start in range(0, ROWS, STEP):
        part = skewed_ref[start : start + STEP, :] * ahead_row
        sums = jnp.sum(part, axis=1, keepdims=True)
        total = total + fold(jnp.where(on_diagonal(start, STEP, ROWS), sums, 0.0))
    return jnp.sum(total, axis=0, keepdims=True)


def put_message(out_ref, x_row, spread_row, sums_row, mapped_row):
    put_lanes(out_ref, X_AT, x_row)
    put_lanes(out_ref, SPREAD_AT, spread_row)
    put_lanes(out_ref, SUMS_AT, sums_row)
    put_lanes(out_ref, MAPPED_AT, mapped_row)


def begin_kernel(contacts_ref, mapped_ref, skewed_ref, out_ref, counts_ref):
    for start in range(0, ROWS, STEP):
        counts = contacts_ref[start : start + STEP, :]
        counts_ref[start : start + STEP, :] = counts.astype(jnp.int16)
        counts = counts.astype(F32)
        padded = jnp.concatenate([counts, jnp.zeros((STEP, SPAN - BAND), F32)], axis=1)
        skewed_ref[start : start + STEP, :] = pltpu.roll(padded, start, 1, stride=1, stride_axis=0)
    mapped = lanes(mapped_ref[...]).astype(F32)
    put_message(out_ref, mapped, spread_of(skewed_ref, mapped), jnp.zeros((1, ROWS), F32), mapped)


def ahead_of(core, slabs):
    tiles = [jnp.where(core == 0, slabs[k], slabs[k + 1]) for k in range(HOPS + 1)]
    return jnp.concatenate([lanes(t) for t in tiles], axis=1)


def sum_rows(core_ref, skewed_ref, pair_ref, near_ref, far_ref):
    core = core_ref[0]

    def message(k):
        at = k % 2
        chip = k // 2
        if chip == 0:
            return pair_ref.at[at]
        ref = near_ref if abs(chip) == 1 else far_ref
        return ref.at[1 if chip > 0 else 0, at]

    x_tiles = [message(k)[X_AT : X_AT + SLAB, :] for k in range(HOPS + 2)]
    arrived = jnp.zeros((SLAB, LANE), F32)
    for k in range(HOPS + 1):
        at = SPREAD_AT + SLAB * k
        arrived = arrived + jnp.where(
            core == 0, message(-k)[at : at + SLAB, :], message(1 - k)[at : at + SLAB, :]
        )
    sums = own_sums(skewed_ref, ahead_of(core, x_tiles)) + lanes(arrived)
    x_row = lanes(jnp.where(core == 0, x_tiles[0], x_tiles[1]))
    mapped = jnp.where(core == 0, pair_ref[0, MAPPED_AT : MAPPED_AT + SLAB, :], pair_ref[1, MAPPED_AT : MAPPED_AT + SLAB, :])
    return lanes(mapped), x_row * sums


def middle_kernel(core_ref, skewed_ref, pair_ref, near_ref, far_ref, out_ref):
    mapped, sums = sum_rows(core_ref, skewed_ref, pair_ref, near_ref, far_ref)
    x_row = jnp.where(mapped > 0, 1.0 / jnp.where(mapped > 0, sums, 1.0), 0.0)
    put_message(out_ref, x_row, spread_of(skewed_ref, x_row), sums, mapped)


def last_kernel(core_ref, skewed_ref, pair_ref, near_ref, far_ref, out_ref):
    mapped, sums = sum_rows(core_ref, skewed_ref, pair_ref, near_ref, far_ref)
    before = jnp.where(core_ref[0] == 0, pair_ref[0], pair_ref[1])
    before = lanes(before[SUMS_AT : SUMS_AT + SLAB])
    bias = jnp.where(mapped > 0, before * sums, 1.0)
    out_ref[...] = jnp.zeros((8, LANE), F32)
    put_lanes(out_ref, 0, jnp.where(mapped > 0, 1.0 / bias, 0.0))
    put_lanes(out_ref, SLAB, bias)
    for at, value in ((4, before), (5, sums)):
        total = jnp.sum(jnp.where(mapped > 0, value, 0.0), axis=1, keepdims=True)
        out_ref[at : at + 1, :] = jnp.broadcast_to(total, (1, LANE))


def flipped(rows):
    order = 7 - lax.broadcasted_iota(jnp.int32, (8, LANE), 0)
    tiles = [jnp.take_along_axis(rows[:, t : t + LANE], order, axis=0, mode="promise_in_bounds") for t in range(0, rows.shape[1], LANE)]
    return jnp.concatenate(tiles, axis=1)


def along_diagonals(rows_of, width):
    total = None
    for g in range(LANE // 8):
        part = None
        for h in range(SLAB):
            rows = rows_of(h * LANE + 8 * g)
            rows = rows[:, h * LANE : h * LANE + SPAN - LANE]
            part = rows if part is None else part + rows
        if g:
            part = pltpu.roll(part, SPAN - LANE - 8 * g, 1)
        total = part if total is None else total + part
    total = pltpu.roll(flipped(total), SPAN - LANE - 7, 1, stride=1, stride_axis=0)
    return jnp.sum(total[:, :width], axis=0, keepdims=True)


def pairs_kernel(core_ref, pair_ref, near_ref, far_ref, out_ref):
    refs = [pair_ref.at[0], pair_ref.at[1], near_ref.at[1, 0], near_ref.at[1, 1], far_ref.at[1, 0], far_ref.at[1, 1]]
    ahead = ahead_of(core_ref[0], [r[MAPPED_AT : MAPPED_AT + SLAB, :] for r in refs])
    row = ahead[:, :ROWS]
    out_ref[...] = along_diagonals(lambda r: column_of(row, r, 8) * ahead, BAND)


def band_kernel(core_ref, skewed_ref, pair_ref, ahead_ref, own_ref, pairs_ref,
                final_ref, swap_ref, cross_ref, sums_ref, vectors_ref):
    core = core_ref[0]
    slabs = [pair_ref[0], pair_ref[1], ahead_ref[0, 0], ahead_ref[0, 1], ahead_ref[1, 0], ahead_ref[1, 1]]
    ahead = ahead_of(core, [s[X_AT : X_AT + SLAB] for s in slabs])
    x_row = ahead[:, :ROWS]
    for start in range(0, ROWS, STEP):
        final_ref[start : start + STEP, :] = (
            skewed_ref[start : start + STEP, :] * column_of(x_row, start, STEP) * ahead
        )
    first, last = final_ref[0:EDGE, :], final_ref[ROWS - EDGE : ROWS, :]
    swap_ref[...] = jnp.where(core == 0, last, first)
    cross_ref[...] = jnp.where(core == 0, first, last)
    diagonals = along_diagonals(lambda r: final_ref[r : r + 8, :], BAND)
    own = own_ref[...]
    row = jnp.concatenate([diagonals, pairs_ref[...], own[4:5, : LANE // 2], own[5:6, : LANE // 2]], axis=1)
    for n in range(sums_ref.shape[0]):
        sums_ref[n] = row
    vectors_ref[0:1, :] = ahead
    vectors_ref[1:2, :] = jnp.where(ahead > 0, 1.0 / jnp.where(ahead > 0, ahead, 1.0), 0.0)
    vectors_ref[2:3, :] = jnp.concatenate([lanes(own[SLAB : 2 * SLAB]), jnp.zeros((1, SPAN - ROWS), F32)], axis=1)


def straight(rows, start, tile):
    rows = pltpu.roll(flipped(rows), SPAN - 7 - start, 1, stride=1, stride_axis=0)
    return flipped(rows[:, tile * LANE : tile * LANE + BAND])


def put_tiles(ref, start, value):
    for t in range(value.shape[1] // LANE):
        ref[t, pl.ds(start, value.shape[0]), :] = value[:, t * LANE : (t + 1) * LANE]


def put_tables(refs, start, cells):
    left_out_ref, left_ref, sides_out_ref, sides_ref = refs
    two = cells + pltpu.roll(cells, WIDE - 1, 1)
    three = two + pltpu.roll(cells, WIDE - 2, 1)
    left_out = pltpu.roll(three, 5, 1)
    left_in = pltpu.roll(two, 2, 1)
    sides_out = left_out + pltpu.roll(three, WIDE - 3, 1)
    put_tiles(left_out_ref, start, left_out)
    put_tiles(left_ref, start, left_out + left_in)
    put_tiles(sides_out_ref, start, sides_out)
    put_tiles(sides_ref, start, sides_out + left_in + pltpu.roll(two, WIDE - 1, 1))


NEAR, BEYOND = range(1, INNER + 1), range(INNER + 1, OUTER + 1)


def box_sums(out_ref, in_ref, at, signs):
    def rows(ref, shift):
        return jnp.concatenate([ref[t, at + shift : at + shift + 8, :] for t in range(SPAN // LANE)], axis=1)

    return sum([rows(out_ref, s * a) for a in NEAR for s in signs] + [rows(in_ref, s * a) for a in BEYOND for s in signs])


def inverse_root(count):
    k = jnp.maximum(count, 1.0)
    q = lax.rsqrt(k)
    return k, q * (1.5 - 0.5 * k * q * q)


def root_of(sums, weight, start, tile, counts, k, q):
    value = jnp.where(weight > 0, jnp.maximum(sums, 0.0) * weight, MASKED)
    value = straight(value, start, tile)
    positive = value > 0.0
    root = jnp.exp(jnp.log(jnp.where(positive, value, 1.0) * (q * q)) * (1.0 / 3.0))
    root = jnp.where(positive, root * (k * q * (3.0 / 2.0**0.5)), 0.0)
    distance = lax.broadcasted_iota(jnp.int32, (8, BAND), 1)
    return jnp.where((counts > 0) & (distance >= 2 * OUTER) & (value >= 0.0), root, MASKED)


def window_kernel(final_ref, counts_ref, vectors_ref, donut_ref, lower_ref, partial_ref, left_out_ref, left_ref, sides_out_ref, sides_ref, float_ref):
    bias_ahead = vectors_ref[1:2, :]
    bias_row = bias_ahead[:, :ROWS]
    tables = (left_out_ref, left_ref, sides_out_ref, sides_ref)
    gap = jnp.zeros((EDGE, LANE), F32)
    for ref in tables:
        put_tiles(ref, 0, jnp.zeros((EDGE, WIDE), F32))
        put_tiles(ref, ROWS + EDGE, jnp.zeros((EDGE, WIDE), F32))
    for start in range(0, ROWS, 8):
        put_tables(tables, start + EDGE, jnp.concatenate([final_ref[start : start + 8, :], gap], axis=1))

    for start in range(0, ROWS, STEP):
        here = slice(start, start + STEP)
        float_ref[here, :] = counts_ref[here, :].astype(jnp.int32).astype(F32)

    for i in range(SLAB):
        begin = i * LANE
        views = [ref.at[:, pl.ds(begin, LANE + 2 * EDGE), :] for ref in tables]
        for start in range(0, LANE, 8):
            here = pl.ds(begin + start, 8)
            weight = column_of(bias_row, begin + start, 8) * bias_ahead
            counts = float_ref[here, :]
            k, q = inverse_root(counts)
            donut = box_sums(views[2], views[3], start + EDGE, (1, -1))
            donut_ref[here, :BAND] = root_of(donut, weight, start, i, counts, k, q)
            lower = box_sums(views[0], views[1], start + EDGE, (1,))
            lower_ref[here, :] = root_of(lower, weight, start, i, counts, k, q)
            if begin + start == 0:
                partial_ref[0:8, :] = donut
            if begin + start == ROWS - 8:
                partial_ref[8:16, :] = donut
                partial_ref[16:24, :] = lower


def edge_kernel(core_ref, swap_ref, cross_ref, partial_ref, counts_ref, vectors_ref, out_ref,
                left_out_ref, left_ref, sides_out_ref, sides_ref):
    core = core_ref[0]
    swap, cross = swap_ref[...], cross_ref[...]
    before = jnp.where(core == 0, cross, swap)
    after = jnp.where(core == 0, swap, cross)
    gap = jnp.zeros((EDGE, LANE), F32)
    tables = (left_out_ref, left_ref, sides_out_ref, sides_ref)
    for ref in tables:
        put_tiles(ref, EDGE, jnp.zeros((EDGE, WIDE), F32))
    put_tables(tables, 0, jnp.concatenate([before[:, ROWS:], gap, before[:, :ROWS]], axis=1))
    put_tables(tables, 2 * EDGE, jnp.concatenate([gap] * SLAB + [after[:, : WIDE - ROWS]], axis=1))
    bias_ahead = vectors_ref[1:2, :]
    bias_row = bias_ahead[:, :ROWS]
    last = ROWS - 8
    donut_first = partial_ref[0:8, :] + box_sums(sides_out_ref, sides_ref, EDGE, (-1,))
    donut_last = partial_ref[8:16, :] + box_sums(sides_out_ref, sides_ref, EDGE, (1,))
    lower_last = partial_ref[16:24, :] + box_sums(left_out_ref, left_ref, EDGE, (1,))
    floats = [counts_ref[r : r + 16, :].astype(jnp.int32).astype(F32) for r in (0, ROWS - 16)]
    first_counts, last_counts = floats[0][0:8], floats[1][8:16]
    for at, sums, start, counts in ((0, donut_first, 0, first_counts), (8, donut_last, last, last_counts), (16, lower_last, last, last_counts)):
        weight = column_of(bias_row, start, 8) * bias_ahead
        out_ref[at : at + 8, :] = root_of(sums, weight, start % LANE, start // LANE, counts, *inverse_root(counts))
    out_ref[24:25, :] = jnp.concatenate([vectors_ref[2:3, :ROWS], vectors_ref[0:1, : BAND - ROWS]], axis=1)


def half_erfc(x):
    size = jnp.abs(x)
    t = 1.0 / (1.0 + 0.5 * size)
    poly = 0.17087277
    for c in (-0.82215223, 1.48851587, -1.13520398, 0.27886807, -0.18628806, 0.09678418, 0.37409196, 1.00002368, -1.26551223):
        poly = poly * t + c
    tail = 0.5 * t * jnp.exp(poly - size * size)
    return jnp.where(x >= 0.0, tail, 1.0 - tail)


def filter_sums(expected):
    lane = lax.broadcasted_iota(jnp.int32, expected.shape, 1)
    none = jnp.zeros((1, LANE), F32)
    after = jnp.concatenate([expected[1:], none], axis=0)
    before = jnp.concatenate([none, expected[:-1]], axis=0)
    donut_weight, lower_weight = {}, {}
    for a in range(-OUTER, OUTER + 1):
        for c in range(-OUTER, OUTER + 1):
            if a and c and not (abs(a) <= INNER and abs(c) <= INNER):
                donut_weight[c - a] = donut_weight.get(c - a, 0) + 1
            if a >= 1 and c <= -1 and not (a <= INNER and c >= -INNER):
                lower_weight[c - a] = lower_weight.get(c - a, 0) + 1
    donut = lower = None
    for k in range(-2 * OUTER, 2 * OUTER + 1):
        moved = expected
        if k:
            turn = (-k) % LANE
            here = (lane + k < LANE) if k > 0 else (lane + k >= 0)
            moved = jnp.where(here, pltpu.roll(expected, turn, 1), pltpu.roll(after if k > 0 else before, turn, 1))
        if k in donut_weight:
            part = moved * float(donut_weight[k])
            donut = part if donut is None else donut + part
        if k in lower_weight:
            part = moved * float(lower_weight[k])
            lower = part if lower is None else lower + part
    return donut, lower


def cube_root(value):
    positive = value > 0.0
    root = jnp.exp(jnp.log(jnp.where(positive, value, 1.0)) * (1.0 / 3.0))
    return jnp.where(positive, root, value)


def tiled(row):
    return jnp.concatenate([row[:, t : t + LANE] for t in range(0, row.shape[1], LANE)], axis=0)


def tail_kernel(sums_ref, edge_ref, donut_ref, lower_ref, counts_ref, pvalue_donut_ref, pvalue_lower_ref, bias_ref,
                ratio_ref):
    @pl.when(pl.program_id(0) == 0)
    def _():
        total = sums_ref[0]
        for n in range(1, sums_ref.shape[0]):
            total = total + sums_ref[n]
        pairs = tiled(total[:, BAND : 2 * BAND])
        expected = tiled(total[:, :BAND]) / pairs
        donut_exp, lower_exp = filter_sums(expected)
        ratio_ref[0:1, :] = lanes(cube_root(expected / donut_exp))
        ratio_ref[1:2, :] = lanes(cube_root(expected / lower_exp))
        mapped_count = pairs[0:1, 0:1]
        half = LANE // 2
        first = total[:, 2 * BAND : 2 * BAND + 1] / mapped_count
        second = total[:, 2 * BAND + half : 2 * BAND + half + 1] / mapped_count
        own = edge_ref[24:25, :]
        put_lanes(bias_ref, 0, jnp.where(own[:, ROWS : 2 * ROWS] > 0, own[:, :ROWS] / first / second, 1.0))

    step, rows = pl.program_id(0), pvalue_donut_ref.shape[0]
    for start in range(0, rows, STEP):
        here = slice(start, start + STEP)
        k, q = inverse_root(counts_ref[here, :].astype(jnp.int32).astype(F32))
        base = q * (k * (3.0 / 2.0**0.5) - 1.0 / (3.0 * 2.0**0.5))
        for at, root_ref, out_ref in ((0, donut_ref, pvalue_donut_ref), (1, lower_ref, pvalue_lower_ref)):
            root = root_ref[here, :]
            if start == 0 and at == 0:
                top = jnp.where(step == 0, edge_ref[0:8, :], root[0:8])
                root = jnp.concatenate([top, root[8:]], axis=0)
            if start == rows - STEP:
                edge = edge_ref[8:16, :] if at == 0 else edge_ref[16:24, :]
                bottom = jnp.where(step == ROWS // rows - 1, edge, root[STEP - 8 :])
                root = jnp.concatenate([root[: STEP - 8], bottom], axis=0)
            value = half_erfc(base - root * ratio_ref[at : at + 1, :])
            out_ref[here, :] = jnp.where(root < 0.0, 1.0, value)


def params(mib=8):
    return pltpu.CompilerParams(vmem_limit_bytes=mib * 2**20)


def cost(flops, moved):
    return pl.CostEstimate(flops=flops, bytes_accessed=moved, transcendentals=0)


def call(kernel, ins, outs, specs=None, **more):
    return pl.pallas_call(
        kernel,
        out_shape=[jax.ShapeDtypeStruct(s, F32) for s in outs],
        in_specs=specs or [VMEM] * len(ins),
        out_specs=[VMEM] * len(outs),
        compiler_params=params(),
        **more,
    )(*ins)


def begin(contacts, mapped):
    shapes = [((ROWS, SPAN), F32), ((MESSAGE, LANE), F32), ((ROWS, BAND), jnp.int16)]
    return pl.pallas_call(
        begin_kernel,
        out_shape=[jax.ShapeDtypeStruct(*s) for s in shapes],
        in_specs=[VMEM] * 2,
        out_specs=[VMEM] * 3,
        compiler_params=params(),
    )(contacts, mapped)


def middle(core, skewed, pair, near, far):
    return call(middle_kernel, (core, skewed, pair, near, far), [(MESSAGE, LANE)], [SMEM] + [VMEM] * 4)[0]


def last(core, skewed, pair, near, far):
    return call(last_kernel, (core, skewed, pair, near, far), [(8, LANE)], [SMEM] + [VMEM] * 4)[0]


def pair_counts(core, pair, near, far):
    return call(
        pairs_kernel, (core, pair, near, far), [(1, BAND)], [SMEM] + [VMEM] * 3, cost_estimate=cost(10**6, 2**16)
    )[0]


def final_band(core, skewed, pair, ahead, own, pairs, copies):
    return call(
        band_kernel,
        (core, skewed, pair, ahead, own, pairs),
        [(ROWS, SPAN), (EDGE, SPAN), (EDGE, SPAN), (copies, 1, 2 * BAND + LANE), (8, SPAN)],
        [SMEM] + [VMEM] * 5,
    )


def windows(final, counts, vectors):
    return pl.pallas_call(
        window_kernel,
        out_shape=[jax.ShapeDtypeStruct(s, F32) for s in ((ROWS, SPAN), (ROWS, BAND), (24, SPAN))],
        in_specs=[VMEM] * 3,
        out_specs=[VMEM] * 3,
        scratch_shapes=[pltpu.VMEM((WIDE // LANE, ROWS + 2 * EDGE, LANE), F32)] * 4 + [pltpu.VMEM((ROWS, BAND), F32)],
        input_output_aliases={0: 0},
        compiler_params=params(16),
        cost_estimate=cost(2 * 10**7, 6 * 2**20),
    )(final, counts, vectors)


def edges(core, swap, cross, partial, counts, vectors):
    return call(
        edge_kernel,
        (core, swap, cross, partial, counts, vectors),
        [(32, BAND)],
        [SMEM] + [VMEM] * 5,
        scratch_shapes=[pltpu.VMEM((WIDE // LANE, 3 * EDGE, LANE), F32)] * 4,
        cost_estimate=cost(10**6, 2**20),
    )[0]


def whole(shape):
    return pl.BlockSpec(shape, lambda i: (0,) * len(shape))


def tails(sums, own, donut, lower, counts, rows=64):
    block = pl.BlockSpec((rows, BAND), lambda i: (i, 0))
    return pl.pallas_call(
        tail_kernel,
        grid=(ROWS // rows,),
        out_shape=[jax.ShapeDtypeStruct((ROWS, BAND), F32)] * 2 + [jax.ShapeDtypeStruct((SLAB, LANE), F32)],
        in_specs=[whole(sums.shape), whole(own.shape)] + [block] * 3,
        out_specs=[block] * 2 + [whole((SLAB, LANE))],
        scratch_shapes=[pltpu.VMEM((8, BAND), F32)],
        compiler_params=params(),
    )(sums, own, donut, lower, counts)


def solution(mesh):
    size = mesh.shape["genome"]
    plane = min(32, size)
    chips = [[i, i + 1] for i in range(0, size, 2)]
    planes = [[start + i for i in range(plane)] for start in range(0, size, plane)]
    lines = [[i + start for start in range(0, size, plane)] for i in range(plane)]

    def both_cores(value):
        return lax.all_gather(value, "genome", axis_index_groups=chips)

    def moved(value, target):
        pairs = [(i, target(i)) for i in range(size)]
        return lax.ppermute(value, "genome", [(i, t) for i, t in pairs if 0 <= t < size])

    def around(message):
        pair = both_cores(message)
        near = moved(pair, lambda i: i + 2 if i % 2 == 0 else i - 2)
        far = moved(pair, lambda i: i + 4 if i % 2 == 0 else i - 4)
        return pair, both_cores(near), both_cores(far)

    def shards(contacts, mappable):
        core = lax.rem(lax.axis_index("genome"), 2).astype(jnp.int32).reshape(1)
        mapped = mappable.reshape(SLAB, LANE)
        skewed, message, counts = begin(contacts, mapped)
        exchanged = around(message)
        pairs = pair_counts(core, *exchanged)
        message = middle(core, skewed, *exchanged)
        own = last(core, skewed, *around(message))
        pair = both_cores(own)
        ahead = both_cores(moved(pair, lambda i: i - 2 if i % 2 == 0 else i - 4))
        final, swap, cross, sums, vectors = final_band(core, skewed, pair, ahead, own, pairs, plane)
        swap = moved(swap, lambda i: i ^ 1)
        sums = lax.all_to_all(sums, "genome", 0, 0, axis_index_groups=planes)
        sums = jnp.broadcast_to(jnp.sum(sums, axis=0, keepdims=True), (size // plane,) + sums.shape[1:])
        sums, swap, cross, final = lax.optimization_barrier((sums, swap, cross, final))
        sums = lax.all_to_all(sums, "genome", 0, 0, axis_index_groups=lines)
        cross = moved(cross, lambda i: i - 1 if i % 2 == 0 else i + 1)
        donut, lower, partial = windows(final, counts, vectors)
        edge = edges(core, swap, cross, partial, counts, vectors)
        pvalue_donut, pvalue_lower, bias = tails(sums, edge, donut, lower, counts)
        return pvalue_donut, pvalue_lower, bias.reshape(ROWS)

    placed = (P("genome", None), P("genome"))
    return jax.shard_map(
        shards,
        mesh=mesh,
        in_specs=placed,
        out_specs=(P("genome", None), P("genome", None), P("genome")),
        check_vma=False,
    )
```

```python
import jax
import jax.numpy as jnp
from jax import lax
from jax.experimental import pallas as pl
from jax.experimental.pallas import tpu as pltpu
from jax.sharding import PartitionSpec as P

OUTER = 5
INNER = 2
ROWS = 256
BAND = 1024
LANE = 128
SLAB = ROWS // LANE
HOPS = BAND // ROWS
SPAN = ROWS + BAND
WIDE = SPAN + LANE
STEP = 32
EDGE = 8
MASKED = -1.0
TABLE_STEP = 32
VMEM = pl.BlockSpec(memory_space=pltpu.VMEM)
SMEM = pl.BlockSpec(memory_space=pltpu.SMEM)
F32 = jnp.float32
X_AT, SPREAD_AT, SUMS_AT, MAPPED_AT, MESSAGE = 0, SLAB, SLAB * (HOPS + 2), SLAB * (HOPS + 3), 16


def lanes(tiles):
    return jnp.concatenate([tiles[r : r + 1] for r in range(tiles.shape[0])], axis=1)


def put_lanes(ref, first, row):
    for t in range(row.shape[1] // LANE):
        ref[first + t : first + t + 1, :] = row[:, t * LANE : (t + 1) * LANE]


def on_diagonal(start, count, width):
    rows = lax.broadcasted_iota(jnp.int32, (count, width), 0) + start
    return rows == lax.broadcasted_iota(jnp.int32, (count, width), 1)


def column_of(row, start, count):
    part = jnp.where(on_diagonal(start, count, ROWS), row, 0.0)
    return jnp.sum(part, axis=1, keepdims=True)


def fold(value):
    total = value[0:8]
    for r in range(8, value.shape[0], 8):
        total = total + value[r : r + 8]
    return total


def spread_part(rows, weight_row, start):
    part = rows * column_of(weight_row, start, STEP)
    return fold(jnp.where(on_diagonal(start, STEP, SPAN), 0.0, part))


def spread_of(skewed_ref, weight_row):
    total = jnp.zeros((8, SPAN), F32)
    for start in range(0, ROWS, STEP):
        total = total + spread_part(skewed_ref[start : start + STEP, :], weight_row, start)
    return jnp.sum(total, axis=0, keepdims=True)


def own_sums(skewed_ref, ahead_row):
    total = jnp.zeros((8, ROWS), F32)
    for start in range(0, ROWS, STEP):
        part = skewed_ref[start : start + STEP, :] * ahead_row
        sums = jnp.sum(part, axis=1, keepdims=True)
        total = total + fold(jnp.where(on_diagonal(start, STEP, ROWS), sums, 0.0))
    return jnp.sum(total, axis=0, keepdims=True)


def put_message(out_ref, x_row, spread_row, sums_row, mapped_row):
    put_lanes(out_ref, X_AT, x_row)
    put_lanes(out_ref, SPREAD_AT, spread_row)
    put_lanes(out_ref, SUMS_AT, sums_row)
    put_lanes(out_ref, MAPPED_AT, mapped_row)


def begin_kernel(contacts_ref, mapped_ref, skewed_ref, out_ref, counts_ref):
    for start in range(0, ROWS, STEP):
        counts = contacts_ref[start : start + STEP, :]
        counts_ref[start : start + STEP, :] = counts.astype(jnp.int16)
        counts = counts.astype(F32)
        padded = jnp.concatenate([counts, jnp.zeros((STEP, SPAN - BAND), F32)], axis=1)
        skewed_ref[start : start + STEP, :] = pltpu.roll(padded, start, 1, stride=1, stride_axis=0)
    mapped = lanes(mapped_ref[...]).astype(F32)
    put_message(out_ref, mapped, spread_of(skewed_ref, mapped), jnp.zeros((1, ROWS), F32), mapped)


def ahead_of(core, slabs):
    tiles = [jnp.where(core == 0, slabs[k], slabs[k + 1]) for k in range(HOPS + 1)]
    return jnp.concatenate([lanes(t) for t in tiles], axis=1)


def sum_rows(core_ref, skewed_ref, pair_ref, near_ref, far_ref):
    core = core_ref[0]

    def message(k):
        at = k % 2
        chip = k // 2
        if chip == 0:
            return pair_ref.at[at]
        ref = near_ref if abs(chip) == 1 else far_ref
        return ref.at[1 if chip > 0 else 0, at]

    x_tiles = [message(k)[X_AT : X_AT + SLAB, :] for k in range(HOPS + 2)]
    arrived = jnp.zeros((SLAB, LANE), F32)
    for k in range(HOPS + 1):
        at = SPREAD_AT + SLAB * k
        arrived = arrived + jnp.where(
            core == 0, message(-k)[at : at + SLAB, :], message(1 - k)[at : at + SLAB, :]
        )
    sums = own_sums(skewed_ref, ahead_of(core, x_tiles)) + lanes(arrived)
    x_row = lanes(jnp.where(core == 0, x_tiles[0], x_tiles[1]))
    mapped = jnp.where(core == 0, pair_ref[0, MAPPED_AT : MAPPED_AT + SLAB, :], pair_ref[1, MAPPED_AT : MAPPED_AT + SLAB, :])
    return lanes(mapped), x_row * sums


def middle_kernel(core_ref, skewed_ref, pair_ref, near_ref, far_ref, out_ref):
    mapped, sums = sum_rows(core_ref, skewed_ref, pair_ref, near_ref, far_ref)
    x_row = jnp.where(mapped > 0, 1.0 / jnp.where(mapped > 0, sums, 1.0), 0.0)
    put_message(out_ref, x_row, spread_of(skewed_ref, x_row), sums, mapped)


def last_kernel(core_ref, skewed_ref, pair_ref, near_ref, far_ref, out_ref):
    mapped, sums = sum_rows(core_ref, skewed_ref, pair_ref, near_ref, far_ref)
    before = jnp.where(core_ref[0] == 0, pair_ref[0], pair_ref[1])
    before = lanes(before[SUMS_AT : SUMS_AT + SLAB])
    bias = jnp.where(mapped > 0, before * sums, 1.0)
    out_ref[...] = jnp.zeros((8, LANE), F32)
    put_lanes(out_ref, 0, jnp.where(mapped > 0, 1.0 / bias, 0.0))
    put_lanes(out_ref, SLAB, bias)
    for at, value in ((4, before), (5, sums)):
        total = jnp.sum(jnp.where(mapped > 0, value, 0.0), axis=1, keepdims=True)
        out_ref[at : at + 1, :] = jnp.broadcast_to(total, (1, LANE))


def line_kernel(sums_ref, out_ref):
    total = sums_ref[0]
    for n in range(1, sums_ref.shape[0]):
        total = total + sums_ref[n]
    for n in range(out_ref.shape[0]):
        out_ref[n] = total


def flipped(rows):
    order = 7 - lax.broadcasted_iota(jnp.int32, (8, LANE), 0)
    tiles = [jnp.take_along_axis(rows[:, t : t + LANE], order, axis=0, mode="promise_in_bounds") for t in range(0, rows.shape[1], LANE)]
    return jnp.concatenate(tiles, axis=1)


def diagonal_sums(groups, width):
    total = None
    for g, part in enumerate(groups):
        if g:
            part = pltpu.roll(part, SPAN - LANE - 8 * g, 1)
        total = part if total is None else total + part
    total = pltpu.roll(flipped(total), SPAN - LANE - 7, 1, stride=1, stride_axis=0)
    return jnp.sum(total[:, :width], axis=0, keepdims=True)


def along_diagonals(ref, width):
    groups = []
    for g in range(0, LANE, 8):
        rows = [ref[h * LANE + g : h * LANE + g + 8, h * LANE : h * LANE + SPAN - LANE] for h in range(SLAB)]
        groups.append(sum(rows[1:], rows[0]))
    return diagonal_sums(groups, width)


def pairs_kernel(core_ref, pair_ref, near_ref, far_ref, out_ref):
    refs = [pair_ref.at[0], pair_ref.at[1], near_ref.at[1, 0], near_ref.at[1, 1], far_ref.at[1, 0], far_ref.at[1, 1]]
    ahead = ahead_of(core_ref[0], [r[MAPPED_AT : MAPPED_AT + SLAB, :] for r in refs])
    width = SPAN - LANE
    none = jnp.zeros((8 - SLAB, width), F32)
    rows = jnp.concatenate([ahead[:, h * LANE : h * LANE + width] for h in range(SLAB)] + [none], axis=0)
    products = lax.dot_general(rows[:, :LANE], rows, (((0,), (0,)), ((), ())), preferred_element_type=F32)
    out_ref[...] = diagonal_sums([products[r : r + 8] for r in range(0, LANE, 8)], BAND)


def band_kernel(core_ref, skewed_ref, pair_ref, ahead_ref, own_ref, pairs_ref,
                final_ref, swap_ref, cross_ref, sums_ref, vectors_ref):
    core = core_ref[0]
    slabs = [pair_ref[0], pair_ref[1], ahead_ref[0, 0], ahead_ref[0, 1], ahead_ref[1, 0], ahead_ref[1, 1]]
    ahead = ahead_of(core, [s[X_AT : X_AT + SLAB] for s in slabs])
    x_row = ahead[:, :ROWS]
    for start in range(0, ROWS, STEP):
        final_ref[start : start + STEP, :] = (
            skewed_ref[start : start + STEP, :] * column_of(x_row, start, STEP) * ahead
        )
    first, last = final_ref[0:EDGE, :], final_ref[ROWS - EDGE : ROWS, :]
    swap_ref[...] = jnp.where(core == 0, last, first)
    cross_ref[...] = jnp.where(core == 0, first, last)
    diagonals = along_diagonals(final_ref, BAND)
    own = own_ref[...]
    row = jnp.concatenate([diagonals, pairs_ref[...], own[4:5, : LANE // 2], own[5:6, : LANE // 2]], axis=1)
    for n in range(sums_ref.shape[0]):
        sums_ref[n] = row
    vectors_ref[0:1, :] = ahead
    vectors_ref[1:2, :] = jnp.where(ahead > 0, 1.0 / jnp.where(ahead > 0, ahead, 1.0), 0.0)
    vectors_ref[2:3, :] = jnp.concatenate([lanes(own[SLAB : 2 * SLAB]), jnp.zeros((1, SPAN - ROWS), F32)], axis=1)


def straight(rows, start, tile):
    rows = pltpu.roll(flipped(rows), SPAN - 7 - start, 1, stride=1, stride_axis=0)
    return flipped(rows[:, tile * LANE : tile * LANE + BAND])


def put_tiles(ref, start, value):
    for t in range(value.shape[1] // LANE):
        ref[t, pl.ds(start, value.shape[0]), :] = value[:, t * LANE : (t + 1) * LANE]


def put_tables(refs, start, cells):
    left_out_ref, left_ref, sides_out_ref, sides_ref = refs
    two = cells + pltpu.roll(cells, WIDE - 1, 1)
    three = two + pltpu.roll(cells, WIDE - 2, 1)
    left_out = pltpu.roll(three, 5, 1)
    left_in = pltpu.roll(two, 2, 1)
    sides_out = left_out + pltpu.roll(three, WIDE - 3, 1)
    put_tiles(left_out_ref, start, left_out)
    put_tiles(left_ref, start, left_out + left_in)
    put_tiles(sides_out_ref, start, sides_out)
    put_tiles(sides_ref, start, sides_out + left_in + pltpu.roll(two, WIDE - 1, 1))


NEAR, BEYOND = range(1, INNER + 1), range(INNER + 1, OUTER + 1)


def box_sums(out_ref, in_ref, at, signs):
    def rows(ref, shift):
        return jnp.concatenate([ref[t, at + shift : at + shift + 8, :] for t in range(SPAN // LANE)], axis=1)

    return sum([rows(out_ref, s * a) for a in NEAR for s in signs] + [rows(in_ref, s * a) for a in BEYOND for s in signs])


def inverse_root(count):
    k = jnp.maximum(count, 1.0)
    return k, lax.rsqrt(k)


def root_of(sums, weight, start, tile, counts, k, q):
    value = jnp.where(weight > 0, jnp.maximum(sums, 0.0) * weight, MASKED)
    value = straight(value, start, tile)
    positive = value > 0.0
    root = jnp.exp(jnp.log(jnp.where(positive, value, 1.0) * (q * q)) * (1.0 / 3.0))
    root = jnp.where(positive, root * (k * q * (3.0 / 2.0**0.5)), 0.0)
    distance = lax.broadcasted_iota(jnp.int32, (8, BAND), 1)
    return jnp.where((counts > 0) & (distance >= 2 * OUTER) & (value >= 0.0), root, MASKED)


def window_kernel(final_ref, counts_ref, vectors_ref, donut_ref, lower_ref, partial_ref, left_out_ref, left_ref, sides_out_ref, sides_ref, float_ref):
    bias_ahead = vectors_ref[1:2, :]
    bias_row = bias_ahead[:, :ROWS]
    tables = (left_out_ref, left_ref, sides_out_ref, sides_ref)
    gap = jnp.zeros((EDGE, LANE), F32)
    for ref in tables:
        put_tiles(ref, 0, jnp.zeros((EDGE, WIDE), F32))
        put_tiles(ref, ROWS + EDGE, jnp.zeros((EDGE, WIDE), F32))
    for start in range(0, ROWS, 8):
        put_tables(tables, start + EDGE, jnp.concatenate([final_ref[start : start + 8, :], gap], axis=1))

    for start in range(0, ROWS, STEP):
        here = slice(start, start + STEP)
        float_ref[here, :] = counts_ref[here, :].astype(jnp.int32).astype(F32)

    for i in range(SLAB):
        begin = i * LANE
        views = [ref.at[:, pl.ds(begin, LANE + 2 * EDGE), :] for ref in tables]
        for start in range(0, LANE, 8):
            here = pl.ds(begin + start, 8)
            weight = column_of(bias_row, begin + start, 8) * bias_ahead
            counts = float_ref[here, :]
            k, q = inverse_root(counts)
            donut = box_sums(views[2], views[3], start + EDGE, (1, -1))
            donut_ref[here, :BAND] = root_of(donut, weight, start, i, counts, k, q)
            lower = box_sums(views[0], views[1], start + EDGE, (1,))
            lower_ref[here, :] = root_of(lower, weight, start, i, counts, k, q)
            if begin + start == 0:
                partial_ref[0:8, :] = donut
            if begin + start == ROWS - 8:
                partial_ref[8:16, :] = donut
                partial_ref[16:24, :] = lower


def edge_kernel(core_ref, swap_ref, cross_ref, partial_ref, counts_ref, vectors_ref, out_ref,
                left_out_ref, left_ref, sides_out_ref, sides_ref):
    core = core_ref[0]
    swap, cross = swap_ref[...], cross_ref[...]
    before = jnp.where(core == 0, cross, swap)
    after = jnp.where(core == 0, swap, cross)
    gap = jnp.zeros((EDGE, LANE), F32)
    tables = (left_out_ref, left_ref, sides_out_ref, sides_ref)
    for ref in tables:
        put_tiles(ref, EDGE, jnp.zeros((EDGE, WIDE), F32))
    put_tables(tables, 0, jnp.concatenate([before[:, ROWS:], gap, before[:, :ROWS]], axis=1))
    put_tables(tables, 2 * EDGE, jnp.concatenate([gap] * SLAB + [after[:, : WIDE - ROWS]], axis=1))
    bias_ahead = vectors_ref[1:2, :]
    bias_row = bias_ahead[:, :ROWS]
    last = ROWS - 8
    donut_first = partial_ref[0:8, :] + box_sums(sides_out_ref, sides_ref, EDGE, (-1,))
    donut_last = partial_ref[8:16, :] + box_sums(sides_out_ref, sides_ref, EDGE, (1,))
    lower_last = partial_ref[16:24, :] + box_sums(left_out_ref, left_ref, EDGE, (1,))
    floats = [counts_ref[r : r + 16, :].astype(jnp.int32).astype(F32) for r in (0, ROWS - 16)]
    first_counts, last_counts = floats[0][0:8], floats[1][8:16]
    for at, sums, start, counts in ((0, donut_first, 0, first_counts), (8, donut_last, last, last_counts), (16, lower_last, last, last_counts)):
        weight = column_of(bias_row, start, 8) * bias_ahead
        out_ref[at : at + 8, :] = root_of(sums, weight, start % LANE, start // LANE, counts, *inverse_root(counts))
    out_ref[24:25, :] = jnp.concatenate([vectors_ref[2:3, :ROWS], vectors_ref[0:1, : BAND - ROWS]], axis=1)


def half_erfc(x):
    size = jnp.abs(x)
    t = 1.0 / (1.0 + 0.5 * size)
    poly = 0.17087277
    for c in (-0.82215223, 1.48851587, -1.13520398, 0.27886807, -0.18628806, 0.09678418, 0.37409196, 1.00002368, -1.26551223):
        poly = poly * t + c
    tail = 0.5 * t * jnp.exp(poly - size * size)
    return jnp.where(x >= 0.0, tail, 1.0 - tail)


def filter_sums(expected):
    lane = lax.broadcasted_iota(jnp.int32, expected.shape, 1)
    none = jnp.zeros((1, LANE), F32)
    after = jnp.concatenate([expected[1:], none], axis=0)
    before = jnp.concatenate([none, expected[:-1]], axis=0)
    donut_weight, lower_weight = {}, {}
    for a in range(-OUTER, OUTER + 1):
        for c in range(-OUTER, OUTER + 1):
            if a and c and not (abs(a) <= INNER and abs(c) <= INNER):
                donut_weight[c - a] = donut_weight.get(c - a, 0) + 1
            if a >= 1 and c <= -1 and not (a <= INNER and c >= -INNER):
                lower_weight[c - a] = lower_weight.get(c - a, 0) + 1
    donut = lower = None
    for k in range(-2 * OUTER, 2 * OUTER + 1):
        moved = expected
        if k:
            turn = (-k) % LANE
            here = (lane + k < LANE) if k > 0 else (lane + k >= 0)
            moved = jnp.where(here, pltpu.roll(expected, turn, 1), pltpu.roll(after if k > 0 else before, turn, 1))
        if k in donut_weight:
            part = moved * float(donut_weight[k])
            donut = part if donut is None else donut + part
        if k in lower_weight:
            part = moved * float(lower_weight[k])
            lower = part if lower is None else lower + part
    return donut, lower


def cube_root(value):
    positive = value > 0.0
    root = jnp.exp(jnp.log(jnp.where(positive, value, 1.0)) * (1.0 / 3.0))
    return jnp.where(positive, root, value)


def tiled(row):
    return jnp.concatenate([row[:, t : t + LANE] for t in range(0, row.shape[1], LANE)], axis=0)


def tail_kernel(sums_ref, edge_ref, donut_ref, lower_ref, counts_ref, pvalue_donut_ref, pvalue_lower_ref, bias_ref,
                ratio_ref):
    @pl.when(pl.program_id(0) == 0)
    def _():
        total = sums_ref[0]
        for n in range(1, sums_ref.shape[0]):
            total = total + sums_ref[n]
        pairs = tiled(total[:, BAND : 2 * BAND])
        expected = tiled(total[:, :BAND]) / pairs
        donut_exp, lower_exp = filter_sums(expected)
        ratio_ref[0:1, :] = lanes(cube_root(expected / donut_exp))
        ratio_ref[1:2, :] = lanes(cube_root(expected / lower_exp))
        mapped_count = pairs[0:1, 0:1]
        half = LANE // 2
        first = total[:, 2 * BAND : 2 * BAND + 1] / mapped_count
        second = total[:, 2 * BAND + half : 2 * BAND + half + 1] / mapped_count
        own = edge_ref[24:25, :]
        put_lanes(bias_ref, 0, jnp.where(own[:, ROWS : 2 * ROWS] > 0, own[:, :ROWS] / first / second, 1.0))

    step, rows = pl.program_id(0), pvalue_donut_ref.shape[0]
    for start in range(0, rows, STEP):
        here = slice(start, start + STEP)
        k, q = inverse_root(counts_ref[here, :].astype(jnp.int32).astype(F32))
        base = q * (k * (3.0 / 2.0**0.5) - 1.0 / (3.0 * 2.0**0.5))
        for at, root_ref, out_ref in ((0, donut_ref, pvalue_donut_ref), (1, lower_ref, pvalue_lower_ref)):
            root = root_ref[here, :]
            if start == 0 and at == 0:
                top = jnp.where(step == 0, edge_ref[0:8, :], root[0:8])
                root = jnp.concatenate([top, root[8:]], axis=0)
            if start == rows - STEP:
                edge = edge_ref[8:16, :] if at == 0 else edge_ref[16:24, :]
                bottom = jnp.where(step == ROWS // rows - 1, edge, root[STEP - 8 :])
                root = jnp.concatenate([root[: STEP - 8], bottom], axis=0)
            value = half_erfc(base - root * ratio_ref[at : at + 1, :])
            out_ref[here, :] = jnp.where(root < 0.0, 1.0, value)


def params(mib=8):
    return pltpu.CompilerParams(vmem_limit_bytes=mib * 2**20)


def cost(flops, moved):
    return pl.CostEstimate(flops=flops, bytes_accessed=moved, transcendentals=0)


def call(kernel, ins, outs, specs=None, **more):
    return pl.pallas_call(
        kernel,
        out_shape=[jax.ShapeDtypeStruct(s, F32) for s in outs],
        in_specs=specs or [VMEM] * len(ins),
        out_specs=[VMEM] * len(outs),
        compiler_params=params(),
        **more,
    )(*ins)


def begin(contacts, mapped):
    shapes = [((ROWS, SPAN), F32), ((MESSAGE, LANE), F32), ((ROWS, BAND), jnp.int16)]
    return pl.pallas_call(
        begin_kernel,
        out_shape=[jax.ShapeDtypeStruct(*s) for s in shapes],
        in_specs=[VMEM] * 2,
        out_specs=[VMEM] * 3,
        compiler_params=params(),
    )(contacts, mapped)


def middle(core, skewed, pair, near, far):
    return call(middle_kernel, (core, skewed, pair, near, far), [(MESSAGE, LANE)], [SMEM] + [VMEM] * 4)[0]


def last(core, skewed, pair, near, far):
    return call(last_kernel, (core, skewed, pair, near, far), [(8, LANE)], [SMEM] + [VMEM] * 4)[0]


def pair_counts(core, pair, near, far):
    return call(
        pairs_kernel, (core, pair, near, far), [(1, BAND)], [SMEM] + [VMEM] * 3, cost_estimate=cost(10**6, 2**16)
    )[0]


def final_band(core, skewed, pair, ahead, own, pairs, copies):
    return call(
        band_kernel,
        (core, skewed, pair, ahead, own, pairs),
        [(ROWS, SPAN), (EDGE, SPAN), (EDGE, SPAN), (copies, 1, 2 * BAND + LANE), (8, SPAN)],
        [SMEM] + [VMEM] * 5,
    )


def windows(final, counts, vectors):
    return pl.pallas_call(
        window_kernel,
        out_shape=[jax.ShapeDtypeStruct(s, F32) for s in ((ROWS, SPAN), (ROWS, BAND), (24, SPAN))],
        in_specs=[VMEM] * 3,
        out_specs=[VMEM] * 3,
        scratch_shapes=[pltpu.VMEM((WIDE // LANE, ROWS + 2 * EDGE, LANE), F32)] * 4 + [pltpu.VMEM((ROWS, BAND), F32)],
        input_output_aliases={0: 0},
        compiler_params=params(16),
        cost_estimate=cost(2 * 10**7, 6 * 2**20),
    )(final, counts, vectors)


def edges(core, swap, cross, partial, counts, vectors):
    return call(
        edge_kernel,
        (core, swap, cross, partial, counts, vectors),
        [(32, BAND)],
        [SMEM] + [VMEM] * 5,
        scratch_shapes=[pltpu.VMEM((WIDE // LANE, 3 * EDGE, LANE), F32)] * 4,
        cost_estimate=cost(10**6, 2**20),
    )[0]


def whole(shape):
    return pl.BlockSpec(shape, lambda i: (0,) * len(shape))


def tails(sums, own, donut, lower, counts, rows=64):
    block = pl.BlockSpec((rows, BAND), lambda i: (i, 0))
    return pl.pallas_call(
        tail_kernel,
        grid=(ROWS // rows,),
        out_shape=[jax.ShapeDtypeStruct((ROWS, BAND), F32)] * 2 + [jax.ShapeDtypeStruct((SLAB, LANE), F32)],
        in_specs=[whole(sums.shape), whole(own.shape)] + [block] * 3,
        out_specs=[block] * 2 + [whole((SLAB, LANE))],
        scratch_shapes=[pltpu.VMEM((8, BAND), F32)],
        compiler_params=params(),
    )(sums, own, donut, lower, counts)


def solution(mesh):
    size = mesh.shape["genome"]
    plane = min(32, size)
    chips = [[i, i + 1] for i in range(0, size, 2)]
    planes = [[start + i for i in range(plane)] for start in range(0, size, plane)]
    lines = [[i + start for start in range(0, size, plane)] for i in range(plane)]

    def both_cores(value):
        return lax.all_gather(value, "genome", axis_index_groups=chips)

    def moved(value, target):
        pairs = [(i, target(i)) for i in range(size)]
        return lax.ppermute(value, "genome", [(i, t) for i, t in pairs if 0 <= t < size])

    def around(message):
        pair = both_cores(message)
        near = moved(pair, lambda i: i + 2 if i % 2 == 0 else i - 2)
        far = moved(pair, lambda i: i + 4 if i % 2 == 0 else i - 4)
        return pair, both_cores(near), both_cores(far)

    def shards(contacts, mappable):
        core = lax.rem(lax.axis_index("genome"), 2).astype(jnp.int32).reshape(1)
        mapped = mappable.reshape(SLAB, LANE)
        skewed, message, counts = begin(contacts, mapped)
        exchanged = around(message)
        pairs = pair_counts(core, *exchanged)
        message = middle(core, skewed, *exchanged)
        own = last(core, skewed, *around(message))
        pair = both_cores(own)
        ahead = both_cores(moved(pair, lambda i: i - 2 if i % 2 == 0 else i - 4))
        final, swap, cross, sums, vectors = final_band(core, skewed, pair, ahead, own, pairs, plane)
        swap = moved(swap, lambda i: i ^ 1)
        sums = lax.all_to_all(sums, "genome", 0, 0, axis_index_groups=planes)
        sums = call(line_kernel, (sums,), [(size // plane,) + sums.shape[1:]])[0]
        sums, swap, cross, final = lax.optimization_barrier((sums, swap, cross, final))
        sums = lax.all_to_all(sums, "genome", 0, 0, axis_index_groups=lines)
        cross = moved(cross, lambda i: i - 1 if i % 2 == 0 else i + 1)
        donut, lower, partial = windows(final, counts, vectors)
        edge = edges(core, swap, cross, partial, counts, vectors)
        pvalue_donut, pvalue_lower, bias = tails(sums, edge, donut, lower, counts)
        return pvalue_donut, pvalue_lower, bias.reshape(ROWS)

    placed = (P("genome", None), P("genome"))
    return jax.shard_map(
        shards,
        mesh=mesh,
        in_specs=placed,
        out_specs=(P("genome", None), P("genome", None), P("genome")),
        check_vma=False,
    )
```

```python
import math

import jax
import jax.numpy as jnp
from jax import lax
from jax.experimental import pallas as pl
from jax.experimental.pallas import tpu as pltpu
from jax.sharding import PartitionSpec as P

UNIT = math.log2(math.e) ** 0.5
SPREAD = 3.0 / 2.0**0.5 * UNIT
OUTER = 5
INNER = 2
ROWS = 256
BAND = 1024
LANE = 128
SLAB = ROWS // LANE
HOPS = BAND // ROWS
SPAN = ROWS + BAND
WIDE = SPAN + LANE
STEP = 32
EDGE = 8
MASKED = -1.0
TABLE_STEP = 32
VMEM = pl.BlockSpec(memory_space=pltpu.VMEM)
SMEM = pl.BlockSpec(memory_space=pltpu.SMEM)
F32 = jnp.float32
X_AT, SPREAD_AT, SUMS_AT, MAPPED_AT, MESSAGE = 0, SLAB, SLAB * (HOPS + 2), SLAB * (HOPS + 3), 16


def lanes(tiles):
    return jnp.concatenate([tiles[r : r + 1] for r in range(tiles.shape[0])], axis=1)


def put_lanes(ref, first, row):
    for t in range(row.shape[1] // LANE):
        ref[first + t : first + t + 1, :] = row[:, t * LANE : (t + 1) * LANE]


def on_diagonal(start, count, width):
    rows = lax.broadcasted_iota(jnp.int32, (count, width), 0) + start
    return rows == lax.broadcasted_iota(jnp.int32, (count, width), 1)


def column_of(row, start, count):
    part = jnp.where(on_diagonal(start, count, ROWS), row, 0.0)
    return jnp.sum(part, axis=1, keepdims=True)


def fold(value):
    total = value[0:8]
    for r in range(8, value.shape[0], 8):
        total = total + value[r : r + 8]
    return total


def spread_part(rows, weight_row, start):
    part = rows * column_of(weight_row, start, STEP)
    return fold(jnp.where(on_diagonal(start, STEP, SPAN), 0.0, part))


def spread_of(skewed_ref, weight_row):
    total = jnp.zeros((8, SPAN), F32)
    for start in range(0, ROWS, STEP):
        total = total + spread_part(skewed_ref[start : start + STEP, :], weight_row, start)
    return jnp.sum(total, axis=0, keepdims=True)


def own_sums(skewed_ref, ahead_row):
    total = jnp.zeros((8, ROWS), F32)
    for start in range(0, ROWS, STEP):
        part = skewed_ref[start : start + STEP, :] * ahead_row
        sums = jnp.sum(part, axis=1, keepdims=True)
        total = total + fold(jnp.where(on_diagonal(start, STEP, ROWS), sums, 0.0))
    return jnp.sum(total, axis=0, keepdims=True)


def put_message(out_ref, x_row, spread_row, sums_row, mapped_row):
    put_lanes(out_ref, X_AT, x_row)
    put_lanes(out_ref, SPREAD_AT, spread_row)
    put_lanes(out_ref, SUMS_AT, sums_row)
    put_lanes(out_ref, MAPPED_AT, mapped_row)


def begin_kernel(contacts_ref, mapped_ref, skewed_ref, out_ref, counts_ref):
    for start in range(0, ROWS, STEP):
        counts = contacts_ref[start : start + STEP, :]
        counts_ref[start : start + STEP, :] = counts.astype(jnp.int16)
        counts = counts.astype(F32)
        padded = jnp.concatenate([counts, jnp.zeros((STEP, SPAN - BAND), F32)], axis=1)
        skewed_ref[start : start + STEP, :] = pltpu.roll(padded, start, 1, stride=1, stride_axis=0)
    mapped = lanes(mapped_ref[...]).astype(F32)
    put_message(out_ref, mapped, spread_of(skewed_ref, mapped), jnp.zeros((1, ROWS), F32), mapped)


def ahead_of(core, slabs):
    tiles = [jnp.where(core == 0, slabs[k], slabs[k + 1]) for k in range(HOPS + 1)]
    return jnp.concatenate([lanes(t) for t in tiles], axis=1)


def sum_rows(core_ref, skewed_ref, pair_ref, near_ref, far_ref):
    core = core_ref[0]

    def message(k):
        at = k % 2
        chip = k // 2
        if chip == 0:
            return pair_ref.at[at]
        ref = near_ref if abs(chip) == 1 else far_ref
        return ref.at[1 if chip > 0 else 0, at]

    x_tiles = [message(k)[X_AT : X_AT + SLAB, :] for k in range(HOPS + 2)]
    arrived = jnp.zeros((SLAB, LANE), F32)
    for k in range(HOPS + 1):
        at = SPREAD_AT + SLAB * k
        arrived = arrived + jnp.where(
            core == 0, message(-k)[at : at + SLAB, :], message(1 - k)[at : at + SLAB, :]
        )
    sums = own_sums(skewed_ref, ahead_of(core, x_tiles)) + lanes(arrived)
    x_row = lanes(jnp.where(core == 0, x_tiles[0], x_tiles[1]))
    mapped = jnp.where(core == 0, pair_ref[0, MAPPED_AT : MAPPED_AT + SLAB, :], pair_ref[1, MAPPED_AT : MAPPED_AT + SLAB, :])
    return lanes(mapped), x_row * sums


def middle_kernel(core_ref, skewed_ref, pair_ref, near_ref, far_ref, out_ref):
    mapped, sums = sum_rows(core_ref, skewed_ref, pair_ref, near_ref, far_ref)
    x_row = jnp.where(mapped > 0, 1.0 / jnp.where(mapped > 0, sums, 1.0), 0.0)
    put_message(out_ref, x_row, spread_of(skewed_ref, x_row), sums, mapped)


def last_kernel(core_ref, skewed_ref, pair_ref, near_ref, far_ref, out_ref):
    mapped, sums = sum_rows(core_ref, skewed_ref, pair_ref, near_ref, far_ref)
    before = jnp.where(core_ref[0] == 0, pair_ref[0], pair_ref[1])
    before = lanes(before[SUMS_AT : SUMS_AT + SLAB])
    bias = jnp.where(mapped > 0, before * sums, 1.0)
    out_ref[...] = jnp.zeros((8, LANE), F32)
    put_lanes(out_ref, 0, jnp.where(mapped > 0, 1.0 / bias, 0.0))
    put_lanes(out_ref, SLAB, bias)
    for at, value in ((4, before), (5, sums)):
        total = jnp.sum(jnp.where(mapped > 0, value, 0.0), axis=1, keepdims=True)
        out_ref[at : at + 1, :] = jnp.broadcast_to(total, (1, LANE))


def line_kernel(sums_ref, out_ref):
    total = sums_ref[0]
    for n in range(1, sums_ref.shape[0]):
        total = total + sums_ref[n]
    for n in range(out_ref.shape[0]):
        out_ref[n] = total


def flipped(rows):
    order = 7 - lax.broadcasted_iota(jnp.int32, (8, LANE), 0)
    tiles = [jnp.take_along_axis(rows[:, t : t + LANE], order, axis=0, mode="promise_in_bounds") for t in range(0, rows.shape[1], LANE)]
    return jnp.concatenate(tiles, axis=1)


def diagonal_sums(groups, width):
    total = None
    for g, part in enumerate(groups):
        if g:
            part = pltpu.roll(part, SPAN - LANE - 8 * g, 1)
        total = part if total is None else total + part
    total = pltpu.roll(flipped(total), SPAN - LANE - 7, 1, stride=1, stride_axis=0)
    return jnp.sum(total[:, :width], axis=0, keepdims=True)


def along_diagonals(ref, width):
    groups = []
    for g in range(0, LANE, 8):
        rows = [ref[h * LANE + g : h * LANE + g + 8, h * LANE : h * LANE + SPAN - LANE] for h in range(SLAB)]
        groups.append(sum(rows[1:], rows[0]))
    return diagonal_sums(groups, width)


def pairs_kernel(core_ref, pair_ref, near_ref, far_ref, out_ref):
    refs = [pair_ref.at[0], pair_ref.at[1], near_ref.at[1, 0], near_ref.at[1, 1], far_ref.at[1, 0], far_ref.at[1, 1]]
    ahead = ahead_of(core_ref[0], [r[MAPPED_AT : MAPPED_AT + SLAB, :] for r in refs])
    width = SPAN - LANE
    none = jnp.zeros((8 - SLAB, width), F32)
    rows = jnp.concatenate([ahead[:, h * LANE : h * LANE + width] for h in range(SLAB)] + [none], axis=0)
    products = lax.dot_general(rows[:, :LANE], rows, (((0,), (0,)), ((), ())), preferred_element_type=F32)
    out_ref[...] = diagonal_sums([products[r : r + 8] for r in range(0, LANE, 8)], BAND)


def band_kernel(core_ref, skewed_ref, pair_ref, ahead_ref, own_ref, pairs_ref,
                final_ref, swap_ref, cross_ref, sums_ref, vectors_ref):
    core = core_ref[0]
    slabs = [pair_ref[0], pair_ref[1], ahead_ref[0, 0], ahead_ref[0, 1], ahead_ref[1, 0], ahead_ref[1, 1]]
    ahead = ahead_of(core, [s[X_AT : X_AT + SLAB] for s in slabs])
    x_row = ahead[:, :ROWS]
    for start in range(0, ROWS, STEP):
        final_ref[start : start + STEP, :] = (
            skewed_ref[start : start + STEP, :] * column_of(x_row, start, STEP) * ahead
        )
    first, last = final_ref[0:EDGE, :], final_ref[ROWS - EDGE : ROWS, :]
    swap_ref[...] = jnp.where(core == 0, last, first)
    cross_ref[...] = jnp.where(core == 0, first, last)
    diagonals = along_diagonals(final_ref, BAND)
    own = own_ref[...]
    row = jnp.concatenate([diagonals, pairs_ref[...], own[4:5, : LANE // 2], own[5:6, : LANE // 2]], axis=1)
    for n in range(sums_ref.shape[0]):
        sums_ref[n] = row
    vectors_ref[0:1, :] = ahead
    vectors_ref[1:2, :] = jnp.where(ahead > 0, 1.0 / jnp.where(ahead > 0, ahead, 1.0), 0.0)
    vectors_ref[2:3, :] = jnp.concatenate([lanes(own[SLAB : 2 * SLAB]), jnp.zeros((1, SPAN - ROWS), F32)], axis=1)


def straight(rows, start, tile):
    rows = pltpu.roll(flipped(rows), SPAN - 7 - start, 1, stride=1, stride_axis=0)
    return flipped(rows[:, tile * LANE : tile * LANE + BAND])


def put_tiles(ref, start, value):
    for t in range(value.shape[1] // LANE):
        ref[t, pl.ds(start, value.shape[0]), :] = value[:, t * LANE : (t + 1) * LANE]


def put_tables(refs, start, cells):
    left_out_ref, left_ref, sides_out_ref, sides_ref = refs
    two = cells + pltpu.roll(cells, WIDE - 1, 1)
    three = two + pltpu.roll(cells, WIDE - 2, 1)
    left_out = pltpu.roll(three, 5, 1)
    left_in = pltpu.roll(two, 2, 1)
    sides_out = left_out + pltpu.roll(three, WIDE - 3, 1)
    put_tiles(left_out_ref, start, left_out)
    put_tiles(left_ref, start, left_out + left_in)
    put_tiles(sides_out_ref, start, sides_out)
    put_tiles(sides_ref, start, sides_out + left_in + pltpu.roll(two, WIDE - 1, 1))


NEAR, BEYOND = range(1, INNER + 1), range(INNER + 1, OUTER + 1)


def box_sums(out_ref, in_ref, at, signs):
    def rows(ref, shift):
        return jnp.concatenate([ref[t, at + shift : at + shift + 8, :] for t in range(SPAN // LANE)], axis=1)

    return sum([rows(out_ref, s * a) for a in NEAR for s in signs] + [rows(in_ref, s * a) for a in BEYOND for s in signs])


def inverse_root(count):
    k = jnp.maximum(count, 1.0)
    return k, lax.rsqrt(k)


def root_of(sums, weight, start, tile, counts, k, q):
    value = jnp.where(weight > 0, jnp.maximum(sums, 0.0) * weight, MASKED)
    value = straight(value, start, tile)
    positive = value > 0.0
    root = jnp.exp(jnp.log(jnp.where(positive, value, 1.0) * (q * q)) * (1.0 / 3.0))
    root = jnp.where(positive, root * (k * q * SPREAD), 0.0)
    distance = lax.broadcasted_iota(jnp.int32, (8, BAND), 1)
    return jnp.where((counts > 0) & (distance >= 2 * OUTER) & (value >= 0.0), root, MASKED)


def window_kernel(final_ref, counts_ref, vectors_ref, donut_ref, lower_ref, partial_ref, left_out_ref, left_ref, sides_out_ref, sides_ref, float_ref):
    bias_ahead = vectors_ref[1:2, :]
    bias_row = bias_ahead[:, :ROWS]
    tables = (left_out_ref, left_ref, sides_out_ref, sides_ref)
    gap = jnp.zeros((EDGE, LANE), F32)
    for ref in tables:
        put_tiles(ref, 0, jnp.zeros((EDGE, WIDE), F32))
        put_tiles(ref, ROWS + EDGE, jnp.zeros((EDGE, WIDE), F32))
    for start in range(0, ROWS, 8):
        put_tables(tables, start + EDGE, jnp.concatenate([final_ref[start : start + 8, :], gap], axis=1))

    for start in range(0, ROWS, STEP):
        here = slice(start, start + STEP)
        float_ref[here, :] = counts_ref[here, :].astype(jnp.int32).astype(F32)

    for i in range(SLAB):
        begin = i * LANE
        views = [ref.at[:, pl.ds(begin, LANE + 2 * EDGE), :] for ref in tables]
        for start in range(0, LANE, 8):
            here = pl.ds(begin + start, 8)
            weight = column_of(bias_row, begin + start, 8) * bias_ahead
            counts = float_ref[here, :]
            k, q = inverse_root(counts)
            donut = box_sums(views[2], views[3], start + EDGE, (1, -1))
            donut_ref[here, :BAND] = root_of(donut, weight, start, i, counts, k, q)
            lower = box_sums(views[0], views[1], start + EDGE, (1,))
            lower_ref[here, :] = root_of(lower, weight, start, i, counts, k, q)
            if begin + start == 0:
                partial_ref[0:8, :] = donut
            if begin + start == ROWS - 8:
                partial_ref[8:16, :] = donut
                partial_ref[16:24, :] = lower


def edge_kernel(core_ref, swap_ref, cross_ref, partial_ref, counts_ref, vectors_ref, out_ref,
                left_out_ref, left_ref, sides_out_ref, sides_ref):
    core = core_ref[0]
    swap, cross = swap_ref[...], cross_ref[...]
    before = jnp.where(core == 0, cross, swap)
    after = jnp.where(core == 0, swap, cross)
    gap = jnp.zeros((EDGE, LANE), F32)
    tables = (left_out_ref, left_ref, sides_out_ref, sides_ref)
    for ref in tables:
        put_tiles(ref, EDGE, jnp.zeros((EDGE, WIDE), F32))
    put_tables(tables, 0, jnp.concatenate([before[:, ROWS:], gap, before[:, :ROWS]], axis=1))
    put_tables(tables, 2 * EDGE, jnp.concatenate([gap] * SLAB + [after[:, : WIDE - ROWS]], axis=1))
    bias_ahead = vectors_ref[1:2, :]
    bias_row = bias_ahead[:, :ROWS]
    last = ROWS - 8
    donut_first = partial_ref[0:8, :] + box_sums(sides_out_ref, sides_ref, EDGE, (-1,))
    donut_last = partial_ref[8:16, :] + box_sums(sides_out_ref, sides_ref, EDGE, (1,))
    lower_last = partial_ref[16:24, :] + box_sums(left_out_ref, left_ref, EDGE, (1,))
    floats = [counts_ref[r : r + 16, :].astype(jnp.int32).astype(F32) for r in (0, ROWS - 16)]
    first_counts, last_counts = floats[0][0:8], floats[1][8:16]
    for at, sums, start, counts in ((0, donut_first, 0, first_counts), (8, donut_last, last, last_counts), (16, lower_last, last, last_counts)):
        weight = column_of(bias_row, start, 8) * bias_ahead
        out_ref[at : at + 8, :] = root_of(sums, weight, start % LANE, start // LANE, counts, *inverse_root(counts))
    out_ref[24:25, :] = jnp.concatenate([vectors_ref[2:3, :ROWS], vectors_ref[0:1, : BAND - ROWS]], axis=1)


ERFC_FIT = (
    -1.26551223, 1.00002368, 0.37409196, 0.09678418, -0.18628806,
    0.27886807, -1.13520398, 1.48851587, -0.82215223, 0.17087277,
)
ERFC_AT = 2.0 * UNIT
ERFC_TERMS = [c * UNIT**2 * ERFC_AT**n for n, c in enumerate(ERFC_FIT)]
ERFC_TERMS[0] += math.log2(0.5 * ERFC_AT)


def half_erfc(y):
    size = jnp.abs(y)
    t = 1.0 / (ERFC_AT + size)
    poly = ERFC_TERMS[-1]
    for c in ERFC_TERMS[-2::-1]:
        poly = poly * t + c
    tail = t * jnp.exp2(poly - y * y)
    return jnp.where(y >= 0.0, tail, 1.0 - tail)


def filter_sums(expected):
    lane = lax.broadcasted_iota(jnp.int32, expected.shape, 1)
    none = jnp.zeros((1, LANE), F32)
    after = jnp.concatenate([expected[1:], none], axis=0)
    before = jnp.concatenate([none, expected[:-1]], axis=0)
    donut_weight, lower_weight = {}, {}
    for a in range(-OUTER, OUTER + 1):
        for c in range(-OUTER, OUTER + 1):
            if a and c and not (abs(a) <= INNER and abs(c) <= INNER):
                donut_weight[c - a] = donut_weight.get(c - a, 0) + 1
            if a >= 1 and c <= -1 and not (a <= INNER and c >= -INNER):
                lower_weight[c - a] = lower_weight.get(c - a, 0) + 1
    donut = lower = None
    for k in range(-2 * OUTER, 2 * OUTER + 1):
        moved = expected
        if k:
            turn = (-k) % LANE
            here = (lane + k < LANE) if k > 0 else (lane + k >= 0)
            moved = jnp.where(here, pltpu.roll(expected, turn, 1), pltpu.roll(after if k > 0 else before, turn, 1))
        if k in donut_weight:
            part = moved * float(donut_weight[k])
            donut = part if donut is None else donut + part
        if k in lower_weight:
            part = moved * float(lower_weight[k])
            lower = part if lower is None else lower + part
    return donut, lower


def cube_root(value):
    positive = value > 0.0
    root = jnp.exp(jnp.log(jnp.where(positive, value, 1.0)) * (1.0 / 3.0))
    return jnp.where(positive, root, value)


def tiled(row):
    return jnp.concatenate([row[:, t : t + LANE] for t in range(0, row.shape[1], LANE)], axis=0)


def tail_kernel(sums_ref, edge_ref, donut_ref, lower_ref, counts_ref, pvalue_donut_ref, pvalue_lower_ref, bias_ref,
                ratio_ref):
    @pl.when(pl.program_id(0) == 0)
    def _():
        total = sums_ref[0]
        for n in range(1, sums_ref.shape[0]):
            total = total + sums_ref[n]
        pairs = tiled(total[:, BAND : 2 * BAND])
        expected = tiled(total[:, :BAND]) / pairs
        donut_exp, lower_exp = filter_sums(expected)
        ratio_ref[0:1, :] = lanes(cube_root(expected / donut_exp))
        ratio_ref[1:2, :] = lanes(cube_root(expected / lower_exp))
        mapped_count = pairs[0:1, 0:1]
        half = LANE // 2
        first = total[:, 2 * BAND : 2 * BAND + 1] / mapped_count
        second = total[:, 2 * BAND + half : 2 * BAND + half + 1] / mapped_count
        own = edge_ref[24:25, :]
        put_lanes(bias_ref, 0, jnp.where(own[:, ROWS : 2 * ROWS] > 0, own[:, :ROWS] / first / second, 1.0))

    step, rows = pl.program_id(0), pvalue_donut_ref.shape[0]
    for start in range(0, rows, STEP):
        here = slice(start, start + STEP)
        k = counts_ref[here, :].astype(jnp.int32).astype(F32)
        base = lax.rsqrt(k) * (k * SPREAD - SPREAD / 9.0)
        for at, root_ref, out_ref in ((0, donut_ref, pvalue_donut_ref), (1, lower_ref, pvalue_lower_ref)):
            root = root_ref[here, :]
            if start == 0 and at == 0:
                top = jnp.where(step == 0, edge_ref[0:8, :], root[0:8])
                root = jnp.concatenate([top, root[8:]], axis=0)
            if start == rows - STEP:
                edge = edge_ref[8:16, :] if at == 0 else edge_ref[16:24, :]
                bottom = jnp.where(step == ROWS // rows - 1, edge, root[STEP - 8 :])
                root = jnp.concatenate([root[: STEP - 8], bottom], axis=0)
            value = half_erfc(base - root * ratio_ref[at : at + 1, :])
            out_ref[here, :] = jnp.where(root < 0.0, 1.0, value)


def params(mib=8):
    return pltpu.CompilerParams(vmem_limit_bytes=mib * 2**20)


def cost(flops, moved):
    return pl.CostEstimate(flops=flops, bytes_accessed=moved, transcendentals=0)


def call(kernel, ins, outs, specs=None, **more):
    return pl.pallas_call(
        kernel,
        out_shape=[jax.ShapeDtypeStruct(s, F32) for s in outs],
        in_specs=specs or [VMEM] * len(ins),
        out_specs=[VMEM] * len(outs),
        compiler_params=params(),
        **more,
    )(*ins)


def begin(contacts, mapped):
    shapes = [((ROWS, SPAN), F32), ((MESSAGE, LANE), F32), ((ROWS, BAND), jnp.int16)]
    return pl.pallas_call(
        begin_kernel,
        out_shape=[jax.ShapeDtypeStruct(*s) for s in shapes],
        in_specs=[VMEM] * 2,
        out_specs=[VMEM] * 3,
        compiler_params=params(),
    )(contacts, mapped)


def middle(core, skewed, pair, near, far):
    return call(middle_kernel, (core, skewed, pair, near, far), [(MESSAGE, LANE)], [SMEM] + [VMEM] * 4)[0]


def last(core, skewed, pair, near, far):
    return call(last_kernel, (core, skewed, pair, near, far), [(8, LANE)], [SMEM] + [VMEM] * 4)[0]


def pair_counts(core, pair, near, far):
    return call(
        pairs_kernel, (core, pair, near, far), [(1, BAND)], [SMEM] + [VMEM] * 3, cost_estimate=cost(10**6, 2**16)
    )[0]


def final_band(core, skewed, pair, ahead, own, pairs, copies):
    return call(
        band_kernel,
        (core, skewed, pair, ahead, own, pairs),
        [(ROWS, SPAN), (EDGE, SPAN), (EDGE, SPAN), (copies, 1, 2 * BAND + LANE), (8, SPAN)],
        [SMEM] + [VMEM] * 5,
    )


def windows(final, counts, vectors):
    return pl.pallas_call(
        window_kernel,
        out_shape=[jax.ShapeDtypeStruct(s, F32) for s in ((ROWS, SPAN), (ROWS, BAND), (24, SPAN))],
        in_specs=[VMEM] * 3,
        out_specs=[VMEM] * 3,
        scratch_shapes=[pltpu.VMEM((WIDE // LANE, ROWS + 2 * EDGE, LANE), F32)] * 4 + [pltpu.VMEM((ROWS, BAND), F32)],
        input_output_aliases={0: 0},
        compiler_params=params(16),
        cost_estimate=cost(2 * 10**7, 6 * 2**20),
    )(final, counts, vectors)


def edges(core, swap, cross, partial, counts, vectors):
    return call(
        edge_kernel,
        (core, swap, cross, partial, counts, vectors),
        [(32, BAND)],
        [SMEM] + [VMEM] * 5,
        scratch_shapes=[pltpu.VMEM((WIDE // LANE, 3 * EDGE, LANE), F32)] * 4,
        cost_estimate=cost(10**6, 2**20),
    )[0]


def whole(shape):
    return pl.BlockSpec(shape, lambda i: (0,) * len(shape))


def tails(sums, own, donut, lower, counts, rows=64):
    block = pl.BlockSpec((rows, BAND), lambda i: (i, 0))
    return pl.pallas_call(
        tail_kernel,
        grid=(ROWS // rows,),
        out_shape=[jax.ShapeDtypeStruct((ROWS, BAND), F32)] * 2 + [jax.ShapeDtypeStruct((SLAB, LANE), F32)],
        in_specs=[whole(sums.shape), whole(own.shape)] + [block] * 3,
        out_specs=[block] * 2 + [whole((SLAB, LANE))],
        scratch_shapes=[pltpu.VMEM((8, BAND), F32)],
        compiler_params=params(),
    )(sums, own, donut, lower, counts)


def solution(mesh):
    size = mesh.shape["genome"]
    plane = min(32, size)
    chips = [[i, i + 1] for i in range(0, size, 2)]
    planes = [[start + i for i in range(plane)] for start in range(0, size, plane)]
    lines = [[i + start for start in range(0, size, plane)] for i in range(plane)]

    def both_cores(value):
        return lax.all_gather(value, "genome", axis_index_groups=chips)

    def moved(value, target):
        pairs = [(i, target(i)) for i in range(size)]
        return lax.ppermute(value, "genome", [(i, t) for i, t in pairs if 0 <= t < size])

    def around(message):
        pair = both_cores(message)
        near = moved(pair, lambda i: i + 2 if i % 2 == 0 else i - 2)
        far = moved(pair, lambda i: i + 4 if i % 2 == 0 else i - 4)
        return pair, both_cores(near), both_cores(far)

    def shards(contacts, mappable):
        core = lax.rem(lax.axis_index("genome"), 2).astype(jnp.int32).reshape(1)
        mapped = mappable.reshape(SLAB, LANE)
        skewed, message, counts = begin(contacts, mapped)
        exchanged = around(message)
        pairs = pair_counts(core, *exchanged)
        message = middle(core, skewed, *exchanged)
        own = last(core, skewed, *around(message))
        pair = both_cores(own)
        ahead = both_cores(moved(pair, lambda i: i - 2 if i % 2 == 0 else i - 4))
        final, swap, cross, sums, vectors = final_band(core, skewed, pair, ahead, own, pairs, plane)
        swap = moved(swap, lambda i: i ^ 1)
        sums = lax.all_to_all(sums, "genome", 0, 0, axis_index_groups=planes)
        sums = call(line_kernel, (sums,), [(size // plane,) + sums.shape[1:]])[0]
        sums, swap, cross, final = lax.optimization_barrier((sums, swap, cross, final))
        sums = lax.all_to_all(sums, "genome", 0, 0, axis_index_groups=lines)
        cross = moved(cross, lambda i: i - 1 if i % 2 == 0 else i + 1)
        donut, lower, partial = windows(final, counts, vectors)
        edge = edges(core, swap, cross, partial, counts, vectors)
        pvalue_donut, pvalue_lower, bias = tails(sums, edge, donut, lower, counts)
        return pvalue_donut, pvalue_lower, bias.reshape(ROWS)

    placed = (P("genome", None), P("genome"))
    return jax.shard_map(
        shards,
        mesh=mesh,
        in_specs=placed,
        out_specs=(P("genome", None), P("genome", None), P("genome")),
        check_vma=False,
    )
```

```python
import math

import jax
import jax.numpy as jnp
from jax import lax
from jax.experimental import pallas as pl
from jax.experimental.pallas import tpu as pltpu
from jax.sharding import PartitionSpec as P

UNIT = math.log2(math.e) ** 0.5
SPREAD = 3.0 / 2.0**0.5 * UNIT
OUTER = 5
INNER = 2
ROWS = 256
BAND = 1024
LANE = 128
SLAB = ROWS // LANE
HOPS = BAND // ROWS
SPAN = ROWS + BAND
HALF = BAND + LANE
WIDE = SPAN + LANE
STEP = 32
EDGE = 8
MASKED = -1.0
TABLE_STEP = 32
VMEM = pl.BlockSpec(memory_space=pltpu.VMEM)
SMEM = pl.BlockSpec(memory_space=pltpu.SMEM)
F32 = jnp.float32
X_AT, SPREAD_AT, SUMS_AT, MAPPED_AT, MESSAGE = 0, SLAB, SLAB * (HOPS + 2), SLAB * (HOPS + 3), 16


def lanes(tiles):
    return jnp.concatenate([tiles[r : r + 1] for r in range(tiles.shape[0])], axis=1)


def put_lanes(ref, first, row):
    for t in range(row.shape[1] // LANE):
        ref[first + t : first + t + 1, :] = row[:, t * LANE : (t + 1) * LANE]


def on_diagonal(start, count, width):
    rows = lax.broadcasted_iota(jnp.int32, (count, width), 0) + start
    return rows == lax.broadcasted_iota(jnp.int32, (count, width), 1)


def column_of(row, start, count):
    part = jnp.where(on_diagonal(start, count, ROWS), row, 0.0)
    return jnp.sum(part, axis=1, keepdims=True)


def fold(value):
    total = value[0:8]
    for r in range(8, value.shape[0], 8):
        total = total + value[r : r + 8]
    return total


def spread_part(rows, weight_row, start):
    part = rows * column_of(weight_row, start, STEP)
    return fold(jnp.where(on_diagonal(start, STEP, SPAN), 0.0, part))


def spread_of(skewed_ref, weight_row):
    total = jnp.zeros((8, SPAN), F32)
    for start in range(0, ROWS, STEP):
        total = total + spread_part(skewed_ref[start : start + STEP, :], weight_row, start)
    return jnp.sum(total, axis=0, keepdims=True)


def own_sums(skewed_ref, ahead_row):
    total = jnp.zeros((8, ROWS), F32)
    for start in range(0, ROWS, STEP):
        part = skewed_ref[start : start + STEP, :] * ahead_row
        sums = jnp.sum(part, axis=1, keepdims=True)
        total = total + fold(jnp.where(on_diagonal(start, STEP, ROWS), sums, 0.0))
    return jnp.sum(total, axis=0, keepdims=True)


def put_message(out_ref, x_row, spread_row, sums_row, mapped_row):
    put_lanes(out_ref, X_AT, x_row)
    put_lanes(out_ref, SPREAD_AT, spread_row)
    put_lanes(out_ref, SUMS_AT, sums_row)
    put_lanes(out_ref, MAPPED_AT, mapped_row)


def begin_kernel(contacts_ref, mapped_ref, skewed_ref, out_ref, counts_ref):
    for start in range(0, ROWS, STEP):
        counts = contacts_ref[start : start + STEP, :]
        counts_ref[start : start + STEP, :] = counts.astype(jnp.int16)
        counts = counts.astype(F32)
        padded = jnp.concatenate([counts, jnp.zeros((STEP, SPAN - BAND), F32)], axis=1)
        skewed_ref[start : start + STEP, :] = pltpu.roll(padded, start, 1, stride=1, stride_axis=0)
    mapped = lanes(mapped_ref[...]).astype(F32)
    put_message(out_ref, mapped, spread_of(skewed_ref, mapped), jnp.zeros((1, ROWS), F32), mapped)


def ahead_of(core, slabs):
    tiles = [jnp.where(core == 0, slabs[k], slabs[k + 1]) for k in range(HOPS + 1)]
    return jnp.concatenate([lanes(t) for t in tiles], axis=1)


def sum_rows(core_ref, skewed_ref, pair_ref, near_ref, far_ref):
    core = core_ref[0]

    def message(k):
        at = k % 2
        chip = k // 2
        if chip == 0:
            return pair_ref.at[at]
        ref = near_ref if abs(chip) == 1 else far_ref
        return ref.at[1 if chip > 0 else 0, at]

    x_tiles = [message(k)[X_AT : X_AT + SLAB, :] for k in range(HOPS + 2)]
    arrived = jnp.zeros((SLAB, LANE), F32)
    for k in range(HOPS + 1):
        at = SPREAD_AT + SLAB * k
        arrived = arrived + jnp.where(
            core == 0, message(-k)[at : at + SLAB, :], message(1 - k)[at : at + SLAB, :]
        )
    sums = own_sums(skewed_ref, ahead_of(core, x_tiles)) + lanes(arrived)
    x_row = lanes(jnp.where(core == 0, x_tiles[0], x_tiles[1]))
    mapped = jnp.where(core == 0, pair_ref[0, MAPPED_AT : MAPPED_AT + SLAB, :], pair_ref[1, MAPPED_AT : MAPPED_AT + SLAB, :])
    return lanes(mapped), x_row * sums


def middle_kernel(core_ref, skewed_ref, pair_ref, near_ref, far_ref, out_ref):
    mapped, sums = sum_rows(core_ref, skewed_ref, pair_ref, near_ref, far_ref)
    x_row = jnp.where(mapped > 0, 1.0 / jnp.where(mapped > 0, sums, 1.0), 0.0)
    put_message(out_ref, x_row, spread_of(skewed_ref, x_row), sums, mapped)


def last_kernel(core_ref, skewed_ref, pair_ref, near_ref, far_ref, out_ref):
    mapped, sums = sum_rows(core_ref, skewed_ref, pair_ref, near_ref, far_ref)
    before = jnp.where(core_ref[0] == 0, pair_ref[0], pair_ref[1])
    before = lanes(before[SUMS_AT : SUMS_AT + SLAB])
    bias = jnp.where(mapped > 0, before * sums, 1.0)
    out_ref[...] = jnp.zeros((8, LANE), F32)
    put_lanes(out_ref, 0, jnp.where(mapped > 0, 1.0 / bias, 0.0))
    put_lanes(out_ref, SLAB, bias)
    for at, value in ((4, before), (5, sums)):
        total = jnp.sum(jnp.where(mapped > 0, value, 0.0), axis=1, keepdims=True)
        out_ref[at : at + 1, :] = jnp.broadcast_to(total, (1, LANE))


def line_kernel(sums_ref, out_ref):
    total = sums_ref[0]
    for n in range(1, sums_ref.shape[0]):
        total = total + sums_ref[n]
    for n in range(out_ref.shape[0]):
        out_ref[n] = total


def flipped(rows):
    order = 7 - lax.broadcasted_iota(jnp.int32, (8, LANE), 0)
    tiles = [jnp.take_along_axis(rows[:, t : t + LANE], order, axis=0, mode="promise_in_bounds") for t in range(0, rows.shape[1], LANE)]
    return jnp.concatenate(tiles, axis=1)


def diagonal_sums(groups, width):
    total = None
    for g, part in enumerate(groups):
        if g:
            part = pltpu.roll(part, SPAN - LANE - 8 * g, 1)
        total = part if total is None else total + part
    total = pltpu.roll(flipped(total), SPAN - LANE - 7, 1, stride=1, stride_axis=0)
    return jnp.sum(total[:, :width], axis=0, keepdims=True)


def along_diagonals(ref, width):
    groups = []
    for g in range(0, LANE, 8):
        rows = [ref[h * LANE + g : h * LANE + g + 8, h * LANE : h * LANE + SPAN - LANE] for h in range(SLAB)]
        groups.append(sum(rows[1:], rows[0]))
    return diagonal_sums(groups, width)


def pairs_kernel(core_ref, pair_ref, near_ref, far_ref, out_ref):
    refs = [pair_ref.at[0], pair_ref.at[1], near_ref.at[1, 0], near_ref.at[1, 1], far_ref.at[1, 0], far_ref.at[1, 1]]
    ahead = ahead_of(core_ref[0], [r[MAPPED_AT : MAPPED_AT + SLAB, :] for r in refs])
    width = SPAN - LANE
    none = jnp.zeros((8 - SLAB, width), F32)
    rows = jnp.concatenate([ahead[:, h * LANE : h * LANE + width] for h in range(SLAB)] + [none], axis=0)
    products = lax.dot_general(rows[:, :LANE], rows, (((0,), (0,)), ((), ())), preferred_element_type=F32)
    out_ref[...] = diagonal_sums([products[r : r + 8] for r in range(0, LANE, 8)], BAND)


def band_kernel(core_ref, skewed_ref, pair_ref, ahead_ref, own_ref, pairs_ref,
                final_ref, swap_ref, cross_ref, sums_ref, vectors_ref):
    core = core_ref[0]
    slabs = [pair_ref[0], pair_ref[1], ahead_ref[0, 0], ahead_ref[0, 1], ahead_ref[1, 0], ahead_ref[1, 1]]
    ahead = ahead_of(core, [s[X_AT : X_AT + SLAB] for s in slabs])
    x_row = ahead[:, :ROWS]
    for start in range(0, ROWS, STEP):
        final_ref[start : start + STEP, :] = (
            skewed_ref[start : start + STEP, :] * column_of(x_row, start, STEP) * ahead
        )
    first, last = final_ref[0:EDGE, :], final_ref[ROWS - EDGE : ROWS, :]
    swap_ref[...] = jnp.where(core == 0, last, first)
    cross_ref[...] = jnp.where(core == 0, first, last)
    diagonals = along_diagonals(final_ref, BAND)
    own = own_ref[...]
    row = jnp.concatenate([diagonals, pairs_ref[...], own[4:5], own[5:6]], axis=1)
    for n in range(sums_ref.shape[0]):
        sums_ref[n] = row[:, :HALF] if n % 2 == 0 else row[:, HALF:]
    vectors_ref[0:1, :] = ahead
    vectors_ref[1:2, :] = jnp.where(ahead > 0, 1.0 / jnp.where(ahead > 0, ahead, 1.0), 0.0)
    vectors_ref[2:3, :] = jnp.concatenate([lanes(own[SLAB : 2 * SLAB]), jnp.zeros((1, SPAN - ROWS), F32)], axis=1)


def straight(rows, start, tile):
    rows = pltpu.roll(flipped(rows), SPAN - 7 - start, 1, stride=1, stride_axis=0)
    return flipped(rows[:, tile * LANE : tile * LANE + BAND])


def put_tiles(ref, start, value):
    for t in range(value.shape[1] // LANE):
        ref[t, pl.ds(start, value.shape[0]), :] = value[:, t * LANE : (t + 1) * LANE]


def put_tables(refs, start, cells):
    left_out_ref, left_ref, sides_out_ref, sides_ref = refs
    two = cells + pltpu.roll(cells, WIDE - 1, 1)
    three = two + pltpu.roll(cells, WIDE - 2, 1)
    left_out = pltpu.roll(three, 5, 1)
    left_in = pltpu.roll(two, 2, 1)
    sides_out = left_out + pltpu.roll(three, WIDE - 3, 1)
    put_tiles(left_out_ref, start, left_out)
    put_tiles(left_ref, start, left_out + left_in)
    put_tiles(sides_out_ref, start, sides_out)
    put_tiles(sides_ref, start, sides_out + left_in + pltpu.roll(two, WIDE - 1, 1))


NEAR, BEYOND = range(1, INNER + 1), range(INNER + 1, OUTER + 1)


def box_sums(out_ref, in_ref, at, signs):
    def rows(ref, shift):
        return jnp.concatenate([ref[t, at + shift : at + shift + 8, :] for t in range(SPAN // LANE)], axis=1)

    return sum([rows(out_ref, s * a) for a in NEAR for s in signs] + [rows(in_ref, s * a) for a in BEYOND for s in signs])


def inverse_root(count):
    k = jnp.maximum(count, 1.0)
    return k, lax.rsqrt(k)


def root_of(sums, weight, start, tile, counts, k, q):
    value = jnp.where(weight > 0, jnp.maximum(sums, 0.0) * weight, MASKED)
    value = straight(value, start, tile)
    positive = value > 0.0
    root = jnp.exp(jnp.log(jnp.where(positive, value, 1.0) * (q * q)) * (1.0 / 3.0))
    root = jnp.where(positive, root * (k * q * SPREAD), 0.0)
    distance = lax.broadcasted_iota(jnp.int32, (8, BAND), 1)
    return jnp.where((counts > 0) & (distance >= 2 * OUTER) & (value >= 0.0), root, MASKED)


def window_kernel(final_ref, counts_ref, vectors_ref, donut_ref, lower_ref, partial_ref, left_out_ref, left_ref, sides_out_ref, sides_ref, float_ref):
    bias_ahead = vectors_ref[1:2, :]
    bias_row = bias_ahead[:, :ROWS]
    tables = (left_out_ref, left_ref, sides_out_ref, sides_ref)
    gap = jnp.zeros((EDGE, LANE), F32)
    for ref in tables:
        put_tiles(ref, 0, jnp.zeros((EDGE, WIDE), F32))
        put_tiles(ref, ROWS + EDGE, jnp.zeros((EDGE, WIDE), F32))
    for start in range(0, ROWS, 8):
        put_tables(tables, start + EDGE, jnp.concatenate([final_ref[start : start + 8, :], gap], axis=1))

    for start in range(0, ROWS, STEP):
        here = slice(start, start + STEP)
        float_ref[here, :] = counts_ref[here, :].astype(jnp.int32).astype(F32)

    for i in range(SLAB):
        begin = i * LANE
        views = [ref.at[:, pl.ds(begin, LANE + 2 * EDGE), :] for ref in tables]
        for start in range(0, LANE, 8):
            here = pl.ds(begin + start, 8)
            weight = column_of(bias_row, begin + start, 8) * bias_ahead
            counts = float_ref[here, :]
            k, q = inverse_root(counts)
            donut = box_sums(views[2], views[3], start + EDGE, (1, -1))
            donut_ref[here, :BAND] = root_of(donut, weight, start, i, counts, k, q)
            lower = box_sums(views[0], views[1], start + EDGE, (1,))
            lower_ref[here, :] = root_of(lower, weight, start, i, counts, k, q)
            if begin + start == 0:
                partial_ref[0:8, :] = donut
            if begin + start == ROWS - 8:
                partial_ref[8:16, :] = donut
                partial_ref[16:24, :] = lower


def edge_kernel(core_ref, swap_ref, cross_ref, partial_ref, counts_ref, vectors_ref, out_ref,
                left_out_ref, left_ref, sides_out_ref, sides_ref):
    core = core_ref[0]
    swap, cross = swap_ref[...], cross_ref[...]
    before = jnp.where(core == 0, cross, swap)
    after = jnp.where(core == 0, swap, cross)
    gap = jnp.zeros((EDGE, LANE), F32)
    tables = (left_out_ref, left_ref, sides_out_ref, sides_ref)
    for ref in tables:
        put_tiles(ref, EDGE, jnp.zeros((EDGE, WIDE), F32))
    put_tables(tables, 0, jnp.concatenate([before[:, ROWS:], gap, before[:, :ROWS]], axis=1))
    put_tables(tables, 2 * EDGE, jnp.concatenate([gap] * SLAB + [after[:, : WIDE - ROWS]], axis=1))
    bias_ahead = vectors_ref[1:2, :]
    bias_row = bias_ahead[:, :ROWS]
    last = ROWS - 8
    donut_first = partial_ref[0:8, :] + box_sums(sides_out_ref, sides_ref, EDGE, (-1,))
    donut_last = partial_ref[8:16, :] + box_sums(sides_out_ref, sides_ref, EDGE, (1,))
    lower_last = partial_ref[16:24, :] + box_sums(left_out_ref, left_ref, EDGE, (1,))
    floats = [counts_ref[r : r + 16, :].astype(jnp.int32).astype(F32) for r in (0, ROWS - 16)]
    first_counts, last_counts = floats[0][0:8], floats[1][8:16]
    for at, sums, start, counts in ((0, donut_first, 0, first_counts), (8, donut_last, last, last_counts), (16, lower_last, last, last_counts)):
        weight = column_of(bias_row, start, 8) * bias_ahead
        out_ref[at : at + 8, :] = root_of(sums, weight, start % LANE, start // LANE, counts, *inverse_root(counts))
    out_ref[24:25, :] = jnp.concatenate([vectors_ref[2:3, :ROWS], vectors_ref[0:1, : BAND - ROWS]], axis=1)


ERFC_FIT = (
    -1.26551223, 1.00002368, 0.37409196, 0.09678418, -0.18628806,
    0.27886807, -1.13520398, 1.48851587, -0.82215223, 0.17087277,
)
ERFC_AT = 2.0 * UNIT
ERFC_TERMS = [c * UNIT**2 * ERFC_AT**n for n, c in enumerate(ERFC_FIT)]
ERFC_TERMS[0] += math.log2(0.5 * ERFC_AT)


def half_erfc(y):
    size = jnp.abs(y)
    t = 1.0 / (ERFC_AT + size)
    poly = ERFC_TERMS[-1]
    for c in ERFC_TERMS[-2::-1]:
        poly = poly * t + c
    tail = t * jnp.exp2(poly - y * y)
    return jnp.where(y >= 0.0, tail, 1.0 - tail)


def filter_sums(expected):
    lane = lax.broadcasted_iota(jnp.int32, expected.shape, 1)
    none = jnp.zeros((1, LANE), F32)
    after = jnp.concatenate([expected[1:], none], axis=0)
    before = jnp.concatenate([none, expected[:-1]], axis=0)
    donut_weight, lower_weight = {}, {}
    for a in range(-OUTER, OUTER + 1):
        for c in range(-OUTER, OUTER + 1):
            if a and c and not (abs(a) <= INNER and abs(c) <= INNER):
                donut_weight[c - a] = donut_weight.get(c - a, 0) + 1
            if a >= 1 and c <= -1 and not (a <= INNER and c >= -INNER):
                lower_weight[c - a] = lower_weight.get(c - a, 0) + 1
    donut = lower = None
    for k in range(-2 * OUTER, 2 * OUTER + 1):
        moved = expected
        if k:
            turn = (-k) % LANE
            here = (lane + k < LANE) if k > 0 else (lane + k >= 0)
            moved = jnp.where(here, pltpu.roll(expected, turn, 1), pltpu.roll(after if k > 0 else before, turn, 1))
        if k in donut_weight:
            part = moved * float(donut_weight[k])
            donut = part if donut is None else donut + part
        if k in lower_weight:
            part = moved * float(lower_weight[k])
            lower = part if lower is None else lower + part
    return donut, lower


def cube_root(value):
    positive = value > 0.0
    root = jnp.exp(jnp.log(jnp.where(positive, value, 1.0)) * (1.0 / 3.0))
    return jnp.where(positive, root, value)


def tiled(row):
    return jnp.concatenate([row[:, t : t + LANE] for t in range(0, row.shape[1], LANE)], axis=0)


def tail_kernel(sums_ref, edge_ref, donut_ref, lower_ref, counts_ref, pvalue_donut_ref, pvalue_lower_ref, bias_ref,
                ratio_ref):
    @pl.when(pl.program_id(0) == 0)
    def _():
        total = jnp.concatenate([sum(sums_ref[core, n] for n in range(sums_ref.shape[1])) for core in range(2)], axis=1)
        pairs = tiled(total[:, BAND : 2 * BAND])
        expected = tiled(total[:, :BAND]) / pairs
        donut_exp, lower_exp = filter_sums(expected)
        ratio_ref[0:1, :] = lanes(cube_root(expected / donut_exp))
        ratio_ref[1:2, :] = lanes(cube_root(expected / lower_exp))
        mapped_count = pairs[0:1, 0:1]
        first = total[:, 2 * BAND : 2 * BAND + 1] / mapped_count
        second = total[:, 2 * BAND + LANE : 2 * BAND + LANE + 1] / mapped_count
        own = edge_ref[24:25, :]
        put_lanes(bias_ref, 0, jnp.where(own[:, ROWS : 2 * ROWS] > 0, own[:, :ROWS] / first / second, 1.0))

    step, rows = pl.program_id(0), pvalue_donut_ref.shape[0]
    for start in range(0, rows, STEP):
        here = slice(start, start + STEP)
        k = counts_ref[here, :].astype(jnp.int32).astype(F32)
        base = lax.rsqrt(k) * (k * SPREAD - SPREAD / 9.0)
        for at, root_ref, out_ref in ((0, donut_ref, pvalue_donut_ref), (1, lower_ref, pvalue_lower_ref)):
            root = root_ref[here, :]
            if start == 0 and at == 0:
                top = jnp.where(step == 0, edge_ref[0:8, :], root[0:8])
                root = jnp.concatenate([top, root[8:]], axis=0)
            if start == rows - STEP:
                edge = edge_ref[8:16, :] if at == 0 else edge_ref[16:24, :]
                bottom = jnp.where(step == ROWS // rows - 1, edge, root[STEP - 8 :])
                root = jnp.concatenate([root[: STEP - 8], bottom], axis=0)
            value = half_erfc(base - root * ratio_ref[at : at + 1, :])
            out_ref[here, :] = jnp.where(root < 0.0, 1.0, value)


def params(mib=8):
    return pltpu.CompilerParams(vmem_limit_bytes=mib * 2**20)


def cost(flops, moved):
    return pl.CostEstimate(flops=flops, bytes_accessed=moved, transcendentals=0)


def call(kernel, ins, outs, specs=None, **more):
    return pl.pallas_call(
        kernel,
        out_shape=[jax.ShapeDtypeStruct(s, F32) for s in outs],
        in_specs=specs or [VMEM] * len(ins),
        out_specs=[VMEM] * len(outs),
        compiler_params=params(),
        **more,
    )(*ins)


def begin(contacts, mapped):
    shapes = [((ROWS, SPAN), F32), ((MESSAGE, LANE), F32), ((ROWS, BAND), jnp.int16)]
    return pl.pallas_call(
        begin_kernel,
        out_shape=[jax.ShapeDtypeStruct(*s) for s in shapes],
        in_specs=[VMEM] * 2,
        out_specs=[VMEM] * 3,
        compiler_params=params(),
    )(contacts, mapped)


def middle(core, skewed, pair, near, far):
    return call(middle_kernel, (core, skewed, pair, near, far), [(MESSAGE, LANE)], [SMEM] + [VMEM] * 4)[0]


def last(core, skewed, pair, near, far):
    return call(last_kernel, (core, skewed, pair, near, far), [(8, LANE)], [SMEM] + [VMEM] * 4)[0]


def pair_counts(core, pair, near, far):
    return call(
        pairs_kernel, (core, pair, near, far), [(1, BAND)], [SMEM] + [VMEM] * 3, cost_estimate=cost(10**6, 2**16)
    )[0]


def final_band(core, skewed, pair, ahead, own, pairs, copies):
    return call(
        band_kernel,
        (core, skewed, pair, ahead, own, pairs),
        [(ROWS, SPAN), (EDGE, SPAN), (EDGE, SPAN), (copies, 1, HALF), (8, SPAN)],
        [SMEM] + [VMEM] * 5,
    )


def windows(final, counts, vectors):
    return pl.pallas_call(
        window_kernel,
        out_shape=[jax.ShapeDtypeStruct(s, F32) for s in ((ROWS, SPAN), (ROWS, BAND), (24, SPAN))],
        in_specs=[VMEM] * 3,
        out_specs=[VMEM] * 3,
        scratch_shapes=[pltpu.VMEM((WIDE // LANE, ROWS + 2 * EDGE, LANE), F32)] * 4 + [pltpu.VMEM((ROWS, BAND), F32)],
        input_output_aliases={0: 0},
        compiler_params=params(16),
        cost_estimate=cost(2 * 10**7, 6 * 2**20),
    )(final, counts, vectors)


def edges(core, swap, cross, partial, counts, vectors):
    return call(
        edge_kernel,
        (core, swap, cross, partial, counts, vectors),
        [(32, BAND)],
        [SMEM] + [VMEM] * 5,
        scratch_shapes=[pltpu.VMEM((WIDE // LANE, 3 * EDGE, LANE), F32)] * 4,
        cost_estimate=cost(10**6, 2**20),
    )[0]


def whole(shape):
    return pl.BlockSpec(shape, lambda i: (0,) * len(shape))


def tails(sums, own, donut, lower, counts, rows=64):
    block = pl.BlockSpec((rows, BAND), lambda i: (i, 0))
    return pl.pallas_call(
        tail_kernel,
        grid=(ROWS // rows,),
        out_shape=[jax.ShapeDtypeStruct((ROWS, BAND), F32)] * 2 + [jax.ShapeDtypeStruct((SLAB, LANE), F32)],
        in_specs=[whole(sums.shape), whole(own.shape)] + [block] * 3,
        out_specs=[block] * 2 + [whole((SLAB, LANE))],
        scratch_shapes=[pltpu.VMEM((8, BAND), F32)],
        compiler_params=params(),
    )(sums, own, donut, lower, counts)


def solution(mesh):
    size = mesh.shape["genome"]
    plane = min(32, size)
    chips = [[i, i + 1] for i in range(0, size, 2)]
    planes = [[start + i for i in range(plane)] for start in range(0, size, plane)]
    lines = [[i + start for start in range(0, size, plane)] for i in range(plane)]

    def both_cores(value):
        return lax.all_gather(value, "genome", axis_index_groups=chips)

    def moved(value, target):
        pairs = [(i, target(i)) for i in range(size)]
        return lax.ppermute(value, "genome", [(i, t) for i, t in pairs if 0 <= t < size])

    def around(message):
        pair = both_cores(message)
        near = moved(pair, lambda i: i + 2 if i % 2 == 0 else i - 2)
        far = moved(pair, lambda i: i + 4 if i % 2 == 0 else i - 4)
        return pair, both_cores(near), both_cores(far)

    def shards(contacts, mappable):
        core = lax.rem(lax.axis_index("genome"), 2).astype(jnp.int32).reshape(1)
        mapped = mappable.reshape(SLAB, LANE)
        skewed, message, counts = begin(contacts, mapped)
        exchanged = around(message)
        pairs = pair_counts(core, *exchanged)
        message = middle(core, skewed, *exchanged)
        own = last(core, skewed, *around(message))
        pair = both_cores(own)
        ahead = both_cores(moved(pair, lambda i: i - 2 if i % 2 == 0 else i - 4))
        final, swap, cross, sums, vectors = final_band(core, skewed, pair, ahead, own, pairs, plane)
        swap = moved(swap, lambda i: i ^ 1)
        sums = lax.all_to_all(sums, "genome", 0, 0, axis_index_groups=planes)
        sums = call(line_kernel, (sums,), [(size // plane,) + sums.shape[1:]])[0]
        sums, swap, cross, final = lax.optimization_barrier((sums, swap, cross, final))
        sums = lax.all_to_all(sums, "genome", 0, 0, axis_index_groups=lines)
        cross = moved(cross, lambda i: i - 1 if i % 2 == 0 else i + 1)
        donut, lower, partial = windows(final, counts, vectors)
        edge = edges(core, swap, cross, partial, counts, vectors)
        pvalue_donut, pvalue_lower, bias = tails(both_cores(sums), edge, donut, lower, counts)
        return pvalue_donut, pvalue_lower, bias.reshape(ROWS)

    placed = (P("genome", None), P("genome"))
    return jax.shard_map(
        shards,
        mesh=mesh,
        in_specs=placed,
        out_specs=(P("genome", None), P("genome", None), P("genome")),
        check_vma=False,
    )
```
